32 devices in a mesh: groups: 2 (over x), corpus: 16 (over z, y, core).
Axes of the slice: x: 2, y: 2, z: 4, core: 2. Of those that a mesh axis runs over, the one named last changes fastest.
Arguments:
- queries: bfloat16 [1792, 32, 128], P(('groups', 'corpus')), parts along dimension 0, may hold values from -6 to 6
- passages: bfloat16 [4096, 128, 128], P(('groups', 'corpus')), parts along dimension 0, may hold values from -0.5 to 0.5
- lengths: int32 [4096], P(('groups', 'corpus')), parts along dimension 0, may hold values from 8 to 128
- candidates: int32 [32, 128], P(('groups', 'corpus')), parts along dimension 0, may hold values from 0 to 2047, as said below
Outputs:
- scores: float32 [1792, 128], P(('groups', 'corpus')), parts along dimension 0
- best_scores: float32 [1792, 100], P(('groups', 'corpus')), parts along dimension 0
The draws below stay inside these ranges and needn't reach their ends.
There are 2 independent parts, one for each index of `groups`. The reference program is written for one: setup_inputs(seed, part) draws one part's arguments, and reference() takes and returns one part's arrays. A program takes and returns all parts, laid end to end along the dimension named above; each array names one. Nothing has to cross between parts.
Inputs may be any that keep to these rules, and one draw needn't show every extreme that they name: Row b lists the candidates of queries b * 56 to (b + 1) * 56 - 1. Passage p is held by owner p // 128. In every row at most 12 entries share an owner, and in every row some owner holds exactly 12 of them. Entries may repeat. `lengths`: rows of a tile at or past its length are padding.
All inputs are finite; a program needn't handle non-finite values.
Results may differ from the reference program's by a relative error of at most 0.0003.
Values may be sent and summed in bfloat16 or wider, within the bound.
No kernel may reach another device: no remote copies, remote signals or barrier semaphores. Data moves between devices by JAX's collectives and lax.ppermute only.
A program may use at most 128 MiB of HBM per device.

```python
import jax
import jax.numpy as jnp
from jax import lax

D = 128
QTOK = 32
PTOK = 128
CAND = 128
TOPK = 100
Q_DEV = 56
P_DEV = 128
BLOCKS = 16
CAP = 12
QUERIES = 896
PASSAGES = 2048


def draw_candidates(key, part):
    subkeys = jax.random.split(key, 5)
    all_slots = BLOCKS * CAP
    popular = (jax.random.randint(subkeys[0], (BLOCKS,), 0, 8) == 0).astype(jnp.int32)
    leader = jax.random.randint(subkeys[1], (), 0, BLOCKS)
    levels = jnp.where(jnp.arange(BLOCKS) == leader, 2, popular)
    jitter = jax.random.randint(subkeys[2], (BLOCKS, BLOCKS, CAP), 0, 65536)
    slot_score = (jitter + levels[None, :, None] * 65536).reshape(BLOCKS, all_slots)
    slot_score = slot_score * all_slots + jnp.arange(all_slots, dtype=jnp.int32)[None, :]
    picked = lax.top_k(slot_score, CAND)[1]
    owner_of = picked // CAP
    local_id = jax.random.randint(subkeys[3], (BLOCKS, CAND), 0, P_DEV)
    passage_ids = owner_of * P_DEV + local_id
    shuffle_score = jax.random.randint(subkeys[4], (BLOCKS, CAND), 0, 65536) * CAND + jnp.arange(CAND, dtype=jnp.int32)[None, :]
    position = jnp.argsort(shuffle_score, axis=1, stable=True)
    return jnp.take_along_axis(passage_ids, position, axis=1).astype(jnp.int32)


def set_ends(drawn, key, low, top_value):
    index_at = [jax.random.randint(jax.random.fold_in(key, axis), (), 0, length) for axis, length in enumerate(drawn.shape)]
    main_axis = drawn.shape.index(max(drawn.shape))
    neighbour = index_at[:main_axis] + [(index_at[main_axis] + 1) % drawn.shape[main_axis]] + index_at[main_axis + 1:]
    return drawn.at[tuple(index_at)].set(low).at[tuple(neighbour)].set(top_value)


def block_scale(own_key, shape, pieces, least, high):
    loudness = 1.0
    for axis_at, parts in pieces:
        steps = jax.random.uniform(jax.random.fold_in(jax.random.fold_in(own_key, 6), axis_at), (parts,), jnp.float32, least / len(pieces), high / len(pieces))
        loudness = loudness * jnp.repeat(jnp.exp(steps), shape[axis_at] // parts).reshape((-1,) + (1,) * (len(shape) - 1 - axis_at))
    return loudness


def scatter_about(own_key, shape, scale, limit, cuts=(), held_as=jnp.bfloat16):
    result = jax.random.normal(own_key, shape, jnp.float32) * scale
    if len(cuts) > 0:
        result = block_scale(own_key, shape, cuts, -0.22, 0.18) * result
    return jnp.clip(result, min=-limit, max=limit).astype(held_as)


def setup_inputs(seed: int = 0, part: int = 0) -> dict:
    key_list = jax.random.split(jax.random.key(seed), 5)
    part_splits = jax.random.split(jax.random.fold_in(key_list[4], part), 5)
    return {
        "queries": scatter_about(part_splits[0], (QUERIES, QTOK, D), 1.0, 6.0, ((0, 16),)),
        "passages": scatter_about(part_splits[1], (PASSAGES, PTOK, D), D ** -0.5, 0.5, ((0, 16),)),
        "lengths": set_ends(jax.random.randint(part_splits[2], (PASSAGES,), max(1, PTOK // 16), PTOK + 1), jax.random.fold_in(part_splits[2], 1), max(1, PTOK // 16), PTOK).astype(jnp.int32),
        "candidates": draw_candidates(jax.random.fold_in(jax.random.fold_in(key_list[4], part), 71), part),
    }


def reference(queries, passages, lengths, candidates):
    def one_block(block_idx):
        query_rows = lax.dynamic_slice_in_dim(queries, block_idx * Q_DEV, Q_DEV, 0)
        query_rows = query_rows.reshape(Q_DEV * QTOK, D).astype(jnp.float32)
        passage_ids = candidates[block_idx]
        tile_set = passages[passage_ids]
        tile_len = lengths[passage_ids]
        inside = lax.broadcasted_iota(jnp.int32, (CAND, PTOK), 1) < tile_len[:, None]
        tile_set = jnp.where(inside[:, :, None], tile_set, tile_set[:, :1, :]).astype(jnp.float32)
        similar = jnp.einsum('rd,cpd->rcp', query_rows, tile_set)
        nearest = jnp.max(similar, axis=2)
        return jnp.sum(nearest.reshape(Q_DEV, QTOK, CAND), axis=1) / float(QTOK)

    scores = lax.map(one_block, jnp.arange(BLOCKS, dtype=jnp.int32)).reshape(QUERIES, CAND)
    best_scores = lax.top_k(scores, TOPK)[0]
    return scores, best_scores
```

```python
import functools
import math

import jax
import jax.numpy as jnp
import numpy as np
from jax import lax
from jax.experimental import pallas as pl
from jax.experimental.pallas import tpu as pltpu
from jax.sharding import PartitionSpec as P

TOPK = 100
CORES = 2
LANES = 128
VMEM_LIMIT = 44 * 1024 * 1024


def ring_order(chips):
    return list(range(0, chips, 2)) + list(range(1, chips, 2))[::-1]


def split_exact(x):
    high = x.astype(jnp.bfloat16)
    rest = x - high.astype(jnp.float32)
    middle = rest.astype(jnp.bfloat16)
    low = (rest - middle.astype(jnp.float32)).astype(jnp.bfloat16)
    return high, middle, low


def score_kernel(
    blocks, slots, group, width, per_device, query_tok, offsets,
    plan, lens, rows, *refs,
):
    halves = refs[: 2 * blocks]
    own, other, out, tiles, best, pick, sems = refs[2 * blocks :]
    per_owner, tile_rows, feature = own.shape
    half_rows = halves[0].shape[0]
    query_rows = 2 * half_rows

    def copy(b, i, tile, source):
        return pltpu.make_async_copy(source.at[tile], tiles.at[b, i], sems.at[b, i])

    counts = []
    for b in range(blocks):
        row = rows[offsets[b]]
        count = plan[row, slots]
        counts.append(count)

        def begin(i, carry, b=b, row=row):
            tile = plan[row, i]

            @pl.when(tile < per_owner)
            def _():
                copy(b, i, tile, own).start()

            @pl.when(tile >= per_owner)
            def _():
                copy(b, i, tile - per_owner, other).start()

            return carry

        lax.fori_loop(0, count, begin, 0)

    token_query = lax.broadcasted_iota(jnp.int32, (query_rows, LANES), 0) // query_tok
    query_lane = lax.broadcasted_iota(jnp.int32, (query_rows, LANES), 1)
    pick[...] = (token_query == query_lane).astype(jnp.float32).astype(jnp.bfloat16)
    tile_row = lax.broadcasted_iota(jnp.int32, (tile_rows, feature), 0)

    for b in range(blocks):
        row = rows[offsets[b]]
        count = counts[b]

        def fill(i, carry, b=b, row=row):
            copy(b, i, 0, own).wait()
            tile = tiles[b, i].astype(jnp.float32)
            inside = tile_row < lens[plan[row, i]]
            tiles[b, i] = jnp.where(inside, tile, tile[0:1, :]).astype(jnp.bfloat16)
            return carry

        lax.fori_loop(0, count, fill, 0)

        def chunk(start, size, b=b):
            first, second = halves[2 * b], halves[2 * b + 1]
            if start + size <= half_rows:
                return first[start : start + size, :]
            if start >= half_rows:
                return second[start - half_rows : start - half_rows + size, :]
            return jnp.concatenate(
                [first[start:, :], second[: start + size - half_rows, :]], axis=0
            )

        def score_group(g, carry, b=b):
            start = pl.multiple_of(g * group, group)
            left = tiles[b, pl.ds(start, group)].reshape(group * tile_rows, feature)
            for at in range(0, query_rows, width):
                size = min(width, query_rows - at)
                similar = lax.dot_general(
                    left, chunk(at, size), (((1,), (1,)), ((), ())),
                    preferred_element_type=jnp.float32,
                )
                nearest = jnp.max(similar.reshape(group, tile_rows // 8, 8, size), axis=1)
                best[pl.ds(start, group), :, at : at + size] = nearest
            return carry

        lax.fori_loop(0, pl.cdiv(count, group), score_group, 0)
        nearest = jnp.max(best[...], axis=1)
        total = jnp.zeros((slots, LANES), jnp.float32)
        for part in split_exact(nearest):
            total += jnp.dot(part, pick[...], preferred_element_type=jnp.float32)
        used = lax.broadcasted_iota(jnp.int32, (slots, LANES), 0) < count
        out[b] = jnp.where(used, total / float(query_tok), 0.0)


def score(offsets, slots, per_device, query_tok, plan, lens, rows, halves, own, other):
    blocks = len(offsets)
    per_owner, tile_rows, feature = own.shape
    query_rows = 2 * halves[0].shape[0]
    flops = 2 * blocks * slots * tile_rows * feature * query_rows
    return pl.pallas_call(
        functools.partial(
            score_kernel, blocks, slots, math.gcd(slots, 4), 256, per_device, query_tok, offsets
        ),
        out_shape=jax.ShapeDtypeStruct((blocks, slots, LANES), jnp.float32),
        grid_spec=pltpu.PrefetchScalarGridSpec(
            num_scalar_prefetch=3,
            grid=(),
            in_specs=[pl.BlockSpec(memory_space=pltpu.VMEM)] * (2 * blocks)
            + [pl.BlockSpec(memory_space=pl.ANY)] * 2,
            out_specs=pl.BlockSpec(memory_space=pltpu.VMEM),
            scratch_shapes=[
                pltpu.VMEM((blocks, slots, tile_rows, feature), jnp.bfloat16),
                pltpu.VMEM((slots, 8, query_rows), jnp.float32),
                pltpu.VMEM((query_rows, LANES), jnp.bfloat16),
                pltpu.SemaphoreType.DMA((blocks, slots)),
            ],
        ),
        compiler_params=pltpu.CompilerParams(vmem_limit_bytes=VMEM_LIMIT),
        cost_estimate=pl.CostEstimate(
            flops=3 * flops,
            bytes_accessed=blocks * (slots * tile_rows + query_rows) * feature * 2,
            transcendentals=0,
        ),
        name="score",
    )(plan, lens, rows, *halves, own, other)


def sort_descending(parts, lanes):
    parts = list(parts)
    many = len(parts)
    number = many * 8
    sub = lax.broadcasted_iota(jnp.int32, (8, lanes), 0)
    size = 2
    while size <= number:
        reach = size // 2
        while reach >= 1:
            if reach < many:
                for v in range(many):
                    if v & reach:
                        continue
                    a, b = parts[v], parts[v | reach]
                    high, low = jnp.maximum(a, b), jnp.minimum(a, b)
                    if size >= number:
                        parts[v], parts[v | reach] = high, low
                    elif size < many:
                        down = (v & size) == 0
                        parts[v], parts[v | reach] = (high, low) if down else (low, high)
                    else:
                        down = (sub & (size // many)) == 0
                        parts[v] = jnp.where(down, high, low)
                        parts[v | reach] = jnp.where(down, low, high)
            else:
                step = reach // many
                is_first = (sub & step) == 0
                if size >= number:
                    keep_high = is_first
                else:
                    keep_high = is_first == ((sub & (size // many)) == 0)
                for v in range(many):
                    x = parts[v]
                    partner = jnp.where(is_first, pltpu.roll(x, 8 - step, 0), pltpu.roll(x, step, 0))
                    parts[v] = jnp.where(keep_high, jnp.maximum(x, partner), jnp.minimum(x, partner))
            reach //= 2
        size *= 2
    return parts


def finish_kernel(arrays, per_device, topk, slot_of, *refs):
    returned = refs[:arrays]
    scores, best_scores, spread, ranked = refs[arrays:]
    number = slot_of.shape[0]
    at = 0
    for ref in returned:
        rows = ref.shape[0] * ref.shape[1]
        spread[at : at + rows, :] = ref[...].reshape(rows, LANES)
        at += rows
    total = spread.shape[0]
    lane = lax.broadcasted_iota(jnp.int32, (number, total), 1)
    choose = (slot_of[...] == lane).astype(jnp.float32).astype(jnp.bfloat16)
    by_candidate = jnp.zeros((number, LANES), jnp.float32)
    for part in split_exact(spread[...]):
        by_candidate += jnp.dot(choose, part, preferred_element_type=jnp.float32)
    scores[...] = by_candidate.T[:per_device, :]
    many = number // 8
    parts = sort_descending([by_candidate[8 * v : 8 * v + 8, :] for v in range(many)], LANES)
    for v in range(many):
        ranked[pl.ds(v, 8, stride=many), :] = parts[v]
    best_scores[...] = ranked[...].T[:per_device, :topk]


def finish(per_device, slot_of, returned):
    number = slot_of.shape[0]
    total = sum(r.shape[0] * r.shape[1] for r in returned)
    return pl.pallas_call(
        functools.partial(finish_kernel, len(returned), per_device, TOPK),
        out_shape=(
            jax.ShapeDtypeStruct((per_device, number), jnp.float32),
            jax.ShapeDtypeStruct((per_device, TOPK), jnp.float32),
        ),
        in_specs=[pl.BlockSpec(memory_space=pltpu.VMEM)] * (1 + len(returned)),
        out_specs=(pl.BlockSpec(memory_space=pltpu.VMEM),) * 2,
        scratch_shapes=[
            pltpu.VMEM((total, LANES), jnp.float32),
            pltpu.VMEM((number, LANES), jnp.float32),
        ],
        compiler_params=pltpu.CompilerParams(vmem_limit_bytes=VMEM_LIMIT),
        name="finish",
    )(slot_of, *returned)


def local(queries, passages, lengths, candidates):
    peers = lax.axis_size("corpus")
    chips = peers // CORES
    per_owner, tile_rows, feature = passages.shape
    per_device, query_tok = queries.shape[0], queries.shape[1]
    number = candidates.shape[1]
    capacity = max(2, 3 * number // (2 * peers))
    slots = -(-CORES * capacity // 8) * 8
    per_chip = CORES * per_owner
    order = ring_order(chips)
    place = [order.index(chip) for chip in range(chips)]

    def moved(x, distance):
        pairs = [
            (order[i] * CORES + core, order[(i + distance) % chips] * CORES + core)
            for i in range(chips)
            for core in range(CORES)
        ]
        return lax.ppermute(x, "corpus", pairs)

    swap = [(i, i ^ 1) for i in range(peers)]
    me = lax.axis_index("corpus")
    core = me % CORES
    chip = me // CORES
    my_place = jnp.asarray(place, jnp.int32)[chip]

    half = per_device // 2
    first = queries[:half].reshape(half * query_tok, feature)
    second = queries[half:].reshape(half * query_tok, feature)
    arrived = {0: (first, second)}
    middle = chips // 2

    def send_on(step):
        if step < middle:
            arrived[step] = tuple(moved(x, 1) for x in arrived[step - 1])
            arrived[-step] = tuple(moved(x, -1) for x in arrived[1 - step])
        else:
            arrived[step] = (moved(arrived[step - 1][0], 1), moved(arrived[1 - step][1], -1))

    send_on(1)
    other = lax.ppermute(passages, "corpus", swap)
    facts = lax.all_gather(
        jnp.concatenate([candidates[0], lengths])[None, :], "corpus", axis=0, tiled=True
    ).reshape(chips, CORES, number + per_owner)
    listed = lax.dynamic_index_in_dim(facts, core, 1, keepdims=False)[:, :number]
    other_lengths = lax.dynamic_slice(
        facts, (chip, 1 - core, number), (1, 1, per_owner)
    ).reshape(per_owner)
    lens = jnp.concatenate([lengths, other_lengths])

    position = jnp.arange(number, dtype=jnp.int32)
    before = position[None, :] < position[:, None]
    mine = listed // per_chip == chip
    rank = jnp.sum((mine[:, None, :] & before[None]).astype(jnp.int32), axis=2)
    tile = listed % per_chip
    tile = jnp.where(tile // per_owner == core, tile % per_owner, per_owner + tile % per_owner)
    at_slot = mine[:, None, :] & (rank[:, None, :] == jnp.arange(slots, dtype=jnp.int32)[None, :, None])
    plan = jnp.max(jnp.where(at_slot, tile[:, None, :], 0), axis=2)
    count = jnp.sum(mine.astype(jnp.int32), axis=1, keepdims=True)
    plan = jnp.concatenate([plan, count], axis=1)
    rows = jnp.asarray(order, jnp.int32)[(my_place - jnp.arange(chips, dtype=jnp.int32)) % chips]

    ids = candidates[0]
    chip_of = ids // per_chip
    rank_in = jnp.sum(((chip_of[:, None] == chip_of[None, :]) & before).astype(jnp.int32), axis=1)
    ahead = (jnp.asarray(place, jnp.int32)[chip_of] - my_place) % chips
    slot_of = (ahead * slots + rank_in)[:, None]

    def run(offsets):
        halves = [x for offset in offsets for x in arrived[offset]]
        return score(
            tuple(offset % chips for offset in offsets), slots, per_device, query_tok,
            plan, lens, rows, halves, passages, other,
        )

    back = {}

    def keep(offsets, fresh):
        for k, offset in enumerate(offsets):
            result = fresh[k : k + 1]
            back[offset % chips] = moved(result, -offset) if offset else result

    for step in range(1, middle + 1):
        if step < middle:
            send_on(step + 1)
        offsets = (0, 1, -1) if step == 1 else (middle,) if step == middle else (step, -step)
        fresh = run(offsets)
        if step < middle:
            names = [step + 1, -step - 1] if step + 1 < middle else [middle]
            held, fresh = lax.optimization_barrier(([arrived[name] for name in names], fresh))
            arrived.update(zip(names, held))
        keep(offsets, fresh)
    return finish(per_device, slot_of, [back[j] for j in range(chips)])


def solution(mesh):
    return jax.shard_map(
        local,
        mesh=mesh,
        in_specs=(
            P(("groups", "corpus"), None, None),
            P(("groups", "corpus"), None, None),
            P(("groups", "corpus")),
            P(("groups", "corpus"), None),
        ),
        out_specs=(P(("groups", "corpus"), None), P(("groups", "corpus"), None)),
        check_vma=False,
    )
```

```python
import functools

import jax
import jax.numpy as jnp
from jax import lax
from jax.experimental import pallas as pl
from jax.experimental.pallas import tpu as pltpu
from jax.sharding import PartitionSpec as P

TOPK = 100
CORES = 2
LANES = 128
FACT_ROWS = 16
VMEM_LIMIT = 32 * 1024 * 1024


def ring_order(chips):
    return list(range(0, chips, 2)) + list(range(1, chips, 2))[::-1]


def ring_place(chip, chips):
    return jnp.where(chip % 2 == 0, chip // 2, chips - (chip + 1) // 2)


def split_exact(x):
    high = x.astype(jnp.bfloat16)
    rest = x - high.astype(jnp.float32)
    middle = rest.astype(jnp.bfloat16)
    low = (rest - middle.astype(jnp.float32)).astype(jnp.bfloat16)
    return high, middle, low


def pack_kernel(per_owner, queries, candidates, block):
    query_rows = queries.shape[0]
    for at in range(0, query_rows, LANES):
        block[at : at + LANES, :] = queries[at : at + LANES, :].T
    ids = jnp.broadcast_to(candidates[...], (FACT_ROWS, candidates.shape[1]))
    row = lax.broadcasted_iota(jnp.int32, ids.shape, 0)
    facts = jnp.where(row == 0, ids // per_owner, jnp.where(row == 1, ids % per_owner, 0))
    block[query_rows:, :] = facts.astype(jnp.float32).astype(jnp.bfloat16)


def pack(queries, candidates, per_owner):
    rows, feature = queries.shape
    return pl.pallas_call(
        functools.partial(pack_kernel, per_owner),
        out_shape=jax.ShapeDtypeStruct((rows + FACT_ROWS, feature), queries.dtype),
        in_specs=[pl.BlockSpec(memory_space=pltpu.VMEM)] * 2,
        out_specs=pl.BlockSpec(memory_space=pltpu.VMEM),
        compiler_params=pltpu.CompilerParams(vmem_limit_bytes=VMEM_LIMIT),
        name="pack",
    )(queries, candidates)


def ready_kernel(chips, slots, candidates, passages, slot_of, own, sem):
    load = pltpu.make_async_copy(passages, own, sem)
    load.start()
    number = candidates.shape[1]
    per_owner = passages.shape[0]
    my_place = ring_place(lax.axis_index("corpus") // CORES, chips)
    wide = jnp.broadcast_to(candidates[...], (number, number)) // (CORES * per_owner)
    tall = wide.astype(jnp.float32).T.astype(jnp.int32)
    row = lax.broadcasted_iota(jnp.int32, (number, number), 0)
    lane = lax.broadcasted_iota(jnp.int32, (number, number), 1)
    earlier = jnp.where((wide == tall) & (lane < row), 1.0, 0.0)
    rank = jnp.sum(earlier, axis=1, keepdims=True).astype(jnp.int32)
    ahead = ring_place(tall, chips) - my_place
    ahead = jnp.where(ahead < 0, ahead + chips, ahead)
    slot_of[...] = ahead * slots + rank
    load.wait()


def ready(candidates, passages, chips, slots):
    number = candidates.shape[1]
    return pl.pallas_call(
        functools.partial(ready_kernel, chips, slots),
        out_shape=(
            jax.ShapeDtypeStruct((number, number), jnp.int32),
            jax.ShapeDtypeStruct(passages.shape, passages.dtype),
        ),
        in_specs=[
            pl.BlockSpec(memory_space=pltpu.VMEM), pl.BlockSpec(memory_space=pl.ANY)
        ],
        out_specs=(pl.BlockSpec(memory_space=pltpu.VMEM),) * 2,
        scratch_shapes=[pltpu.SemaphoreType.DMA],
        compiler_params=pltpu.CompilerParams(vmem_limit_bytes=VMEM_LIMIT),
        name="ready",
    )(candidates, passages)


def score_kernel(pieces, slots, query_tok, *refs):
    blocks = len(pieces)
    arrays = sum(pieces)
    own_lens, other_lens, own, other = refs[:4]
    held = refs[4 : 4 + arrays]
    outs = refs[4 + arrays : 4 + arrays + blocks]
    mixed, left, nearest, plan_v, plan, sem = refs[4 + arrays + blocks :]
    per_owner, tile_rows, feature = own.shape
    query_rows = nearest.shape[1]
    me = lax.axis_index("corpus")
    first_owner = me // CORES * CORES

    chunks, facts = [], []
    at = 0
    for count in pieces:
        where = [(ref, r) for ref in held[at : at + count] for r in range(0, ref.shape[0], LANES)]
        facts.append(where[-1])
        chunks.append(where[:-1])
        at += count

    sub = lax.broadcasted_iota(jnp.int32, (8, LANES), 0)
    lane = lax.broadcasted_iota(jnp.int32, (8, LANES), 1)
    owner = jnp.full((8, LANES), -1.0, jnp.float32)
    local_id = jnp.zeros((8, LANES), jnp.float32)
    for b, (ref, r) in enumerate(facts):
        fact = ref[r : r + FACT_ROWS, :].astype(jnp.float32)
        owner = jnp.where(sub == b, fact[0:1, :], owner)
        local_id = jnp.where(sub == b, fact[1:2, :], local_id)
    owner = owner.astype(jnp.int32)
    mine = (owner >= first_owner) & (owner < first_owner + CORES)
    ones = jnp.where(mine, 1.0, 0.0)
    rank = ones
    shift = 1
    while shift < LANES:
        rank = rank + jnp.where(lane >= shift, pltpu.roll(rank, shift, 1), 0.0)
        shift *= 2
    rank = jnp.where(mine, rank - 1.0, -1.0)
    tile = local_id + jnp.where(owner == me, 0.0, float(per_owner))
    wanted = jnp.where(lane == slots, jnp.sum(ones, axis=1, keepdims=True), 0.0)
    for s in range(slots):
        found = jnp.sum(jnp.where(rank == float(s), tile, 0.0), axis=1, keepdims=True)
        wanted = jnp.where(lane == s, found, wanted)
    plan_v[...] = wanted.astype(jnp.int32)
    to_scalar = pltpu.make_async_copy(plan_v, plan, sem)
    to_scalar.start()
    to_scalar.wait()

    tile_row = lax.broadcasted_iota(jnp.int32, (tile_rows, feature), 0)
    slot_row = lax.broadcasted_iota(jnp.int32, (slots, LANES), 0)
    slot_lane = lax.broadcasted_iota(jnp.int32, (slots, LANES), 1)
    for b in range(blocks):
        count = plan[b, slots]

        def score_group(g, carry, b=b):
            start = pl.multiple_of(g * 8, 8)
            for t in range(8):
                at = plan[b, start + t]
                here = at < per_owner
                at_own = jnp.minimum(at, per_owner - 1)
                at_other = jnp.maximum(at - per_owner, 0)
                length = jnp.where(here, own_lens[at_own], other_lens[at_other])
                tile = jnp.where(
                    here, own[at_own].astype(jnp.float32), other[at_other].astype(jnp.float32)
                )
                tile = jnp.where(tile_row < length, tile, tile[0:1, :])
                mixed[pl.ds(t, tile_rows, stride=8), :] = tile
            left[...] = mixed[...].astype(jnp.bfloat16)
            for c in range(0, len(chunks[b]), 2):
                pair = [ref[r : r + LANES, :] for ref, r in chunks[b][c : c + 2]]
                similar = jnp.dot(
                    left[...], jnp.concatenate(pair, axis=1), preferred_element_type=jnp.float32
                )
                width = similar.shape[1]
                nearest[pl.ds(start, 8), c * LANES : c * LANES + width] = jnp.max(
                    similar.reshape(tile_rows, 8, width), axis=0
                )
            return carry

        lax.fori_loop(0, pl.cdiv(count, 8), score_group, 0)
        total = jnp.zeros((slots, LANES), jnp.float32)
        for k in range(query_rows // LANES):
            x = nearest[:, k * LANES : (k + 1) * LANES]
            shift = query_tok // 2
            while shift >= 1:
                x = x + pltpu.roll(x, LANES - shift, 1)
                shift //= 2
            if k:
                x = pltpu.roll(x, k, 1)
            total = jnp.where(slot_lane % query_tok == k, x, total)
        outs[b][...] = jnp.where(slot_row < count, total / float(query_tok), 0.0)


def score(held, slots, query_tok, own_lens, other_lens, own, other):
    pieces = tuple(len(arrays) for arrays in held)
    flat = [x for arrays in held for x in arrays]
    blocks = len(pieces)
    _, tile_rows, feature = own.shape
    query_rows = sum(x.shape[0] for x in held[0]) - FACT_ROWS
    flops = 2 * blocks * slots * tile_rows * feature * query_rows
    return pl.pallas_call(
        functools.partial(score_kernel, pieces, slots, query_tok),
        out_shape=(jax.ShapeDtypeStruct((slots, LANES), jnp.float32),) * blocks,
        in_specs=[pl.BlockSpec(memory_space=pltpu.SMEM)] * 2
        + [pl.BlockSpec(memory_space=pltpu.VMEM)] * (2 + len(flat)),
        out_specs=(pl.BlockSpec(memory_space=pltpu.VMEM),) * blocks,
        scratch_shapes=[
            pltpu.VMEM((8 * tile_rows, feature), jnp.float32),
            pltpu.VMEM((8 * tile_rows, feature), jnp.bfloat16),
            pltpu.VMEM((slots, query_rows), jnp.float32),
            pltpu.VMEM((8, LANES), jnp.int32),
            pltpu.SMEM((8, LANES), jnp.int32),
            pltpu.SemaphoreType.DMA,
        ],
        compiler_params=pltpu.CompilerParams(vmem_limit_bytes=VMEM_LIMIT),
        cost_estimate=pl.CostEstimate(
            flops=3 * flops,
            bytes_accessed=blocks * (slots * tile_rows + query_rows) * feature * 2,
            transcendentals=0,
        ),
        name="score",
    )(own_lens, other_lens, own, other, *flat)


def sort_descending(parts, lanes):
    parts = list(parts)
    many = len(parts)
    number = many * 8
    sub = lax.broadcasted_iota(jnp.int32, (8, lanes), 0)
    size = 2
    while size <= number:
        reach = size // 2
        while reach >= 1:
            if reach < many:
                for v in range(many):
                    if v & reach:
                        continue
                    a, b = parts[v], parts[v | reach]
                    high, low = jnp.maximum(a, b), jnp.minimum(a, b)
                    if size >= number:
                        parts[v], parts[v | reach] = high, low
                    elif size < many:
                        down = (v & size) == 0
                        parts[v], parts[v | reach] = (high, low) if down else (low, high)
                    else:
                        down = (sub & (size // many)) == 0
                        parts[v] = jnp.where(down, high, low)
                        parts[v | reach] = jnp.where(down, low, high)
            else:
                step = reach // many
                is_first = (sub & step) == 0
                if size >= number:
                    keep_high = is_first
                else:
                    keep_high = is_first == ((sub & (size // many)) == 0)
                for v in range(many):
                    x = parts[v]
                    partner = jnp.where(is_first, pltpu.roll(x, 8 - step, 0), pltpu.roll(x, step, 0))
                    parts[v] = jnp.where(keep_high, jnp.maximum(x, partner), jnp.minimum(x, partner))
            reach //= 2
        size *= 2
    return parts


def finish_kernel(arrays, per_device, query_tok, topk, slot_of, *refs):
    returned = refs[:arrays]
    scores, best_scores, spread, ranked, rows = refs[arrays:]
    number = slot_of.shape[0]
    step = returned[0].shape[0]
    for at, ref in enumerate(returned):
        spread[at * step : (at + 1) * step, :] = ref[...]
    total = spread.shape[0]
    lane = lax.broadcasted_iota(jnp.int32, (number, total), 1)
    choose = (slot_of[:, 0:1] == lane).astype(jnp.float32).astype(jnp.bfloat16)
    by_candidate = jnp.zeros((number, LANES), jnp.float32)
    for part in split_exact(spread[...]):
        by_candidate += jnp.dot(choose, part, preferred_element_type=jnp.float32)

    def in_order(x):
        x = x.T
        each = LANES // query_tok
        for m in range(each):
            rows[pl.ds(m, query_tok, stride=each), :] = x[m * query_tok : (m + 1) * query_tok, :]
        return rows[...]

    scores[...] = in_order(by_candidate)[:per_device, :]
    many = number // 8
    parts = sort_descending([by_candidate[8 * v : 8 * v + 8, :] for v in range(many)], LANES)
    for v in range(many):
        ranked[pl.ds(v, 8, stride=many), :] = parts[v]
    best_scores[...] = in_order(ranked[...])[:per_device, :topk]


def finish(per_device, query_tok, slot_of, returned):
    number = slot_of.shape[0]
    total = sum(r.shape[0] for r in returned)
    return pl.pallas_call(
        functools.partial(finish_kernel, len(returned), per_device, query_tok, TOPK),
        out_shape=(
            jax.ShapeDtypeStruct((per_device, number), jnp.float32),
            jax.ShapeDtypeStruct((per_device, TOPK), jnp.float32),
        ),
        in_specs=[pl.BlockSpec(memory_space=pltpu.VMEM)] * (1 + len(returned)),
        out_specs=(pl.BlockSpec(memory_space=pltpu.VMEM),) * 2,
        scratch_shapes=[
            pltpu.VMEM((total, LANES), jnp.float32),
            pltpu.VMEM((number, LANES), jnp.float32),
            pltpu.VMEM((LANES, number), jnp.float32),
        ],
        compiler_params=pltpu.CompilerParams(vmem_limit_bytes=VMEM_LIMIT),
        name="finish",
    )(slot_of, *returned)


def local(queries, passages, lengths, candidates):
    peers = lax.axis_size("corpus")
    chips = peers // CORES
    per_owner, tile_rows, feature = passages.shape
    per_device, query_tok = queries.shape[0], queries.shape[1]
    number = candidates.shape[1]
    capacity = max(2, 3 * number // (2 * peers))
    slots = -(-CORES * capacity // 8) * 8
    order = ring_order(chips)

    def moved(x, distance):
        pairs = [
            (order[i] * CORES + core, order[(i + distance) % chips] * CORES + core)
            for i in range(chips)
            for core in range(CORES)
        ]
        return lax.ppermute(x, "corpus", pairs)

    swap = [(i, i ^ 1) for i in range(peers)]
    other = lax.ppermute(passages, "corpus", swap)
    other_lengths = lax.ppermute(lengths, "corpus", swap)
    slot_of, own = ready(candidates, passages, chips, slots)

    block = pack(queries.reshape(per_device * query_tok, feature), candidates, per_owner)
    half = per_device * query_tok // LANES // 2 * LANES
    middle = chips // 2
    arrived = {0: [block]}

    def send_on(step):
        if step < middle:
            arrived[step] = [moved(x, 1) for x in arrived[step - 1]]
            arrived[-step] = [moved(x, -1) for x in arrived[1 - step]]
        else:
            arrived[step] = [
                moved(arrived[step - 1][0][:half], 1), moved(arrived[1 - step][0][half:], -1)
            ]

    send_on(1)
    back = {}
    for step in range(1, middle + 1):
        if step < middle:
            send_on(step + 1)
        offsets = (0, 1, -1) if step == 1 else (middle,) if step == middle else (step, -step)
        fresh = score(
            [arrived[offset] for offset in offsets], slots, query_tok,
            lengths, other_lengths, own, other,
        )
        if step < middle:
            names = [step + 1, -step - 1] if step + 1 < middle else [middle]
            held, fresh = lax.optimization_barrier(([arrived[name] for name in names], fresh))
            arrived.update(zip(names, held))
        for offset, result in zip(offsets, fresh):
            back[offset % chips] = moved(result, -offset) if offset else result
    return finish(per_device, query_tok, slot_of, [back[j] for j in range(chips)])


def solution(mesh):
    return jax.shard_map(
        local,
        mesh=mesh,
        in_specs=(
            P(("groups", "corpus"), None, None),
            P(("groups", "corpus"), None, None),
            P(("groups", "corpus")),
            P(("groups", "corpus"), None),
        ),
        out_specs=(P(("groups", "corpus"), None), P(("groups", "corpus"), None)),
        check_vma=False,
    )
```

```python
import functools

import jax
import jax.numpy as jnp
from jax import lax
from jax.experimental import pallas as pl
from jax.experimental.pallas import tpu as pltpu
from jax.sharding import PartitionSpec as P

TOPK = 100
CORES = 2
LANES = 128
FACT_ROWS = 16
GROUP = 4
VMEM_LIMIT = 32 * 1024 * 1024


def ring_order(chips):
    return list(range(0, chips, 2)) + list(range(1, chips, 2))[::-1]


def ring_place(chip, chips):
    return jnp.where(chip % 2 == 0, chip // 2, chips - (chip + 1) // 2)


def split_exact(x):
    high = x.astype(jnp.bfloat16)
    rest = x - high.astype(jnp.float32)
    middle = rest.astype(jnp.bfloat16)
    low = (rest - middle.astype(jnp.float32)).astype(jnp.bfloat16)
    return high, middle, low


def pack_kernel(per_owner, queries_in, candidates_in, block, queries, candidates, sems):
    loads = [
        pltpu.make_async_copy(queries_in, queries, sems.at[0]),
        pltpu.make_async_copy(candidates_in, candidates, sems.at[1]),
    ]
    for load in loads:
        load.start()
    for load in loads:
        load.wait()
    query_rows = queries.shape[0]
    for at in range(0, query_rows, LANES):
        block[at : at + LANES, :] = queries[at : at + LANES, :].T
    ids = jnp.broadcast_to(candidates[...], (FACT_ROWS, candidates.shape[1]))
    row = lax.broadcasted_iota(jnp.int32, ids.shape, 0)
    facts = jnp.where(row == 0, ids // per_owner, jnp.where(row == 1, ids % per_owner, 0))
    block[query_rows:, :] = facts.astype(jnp.float32).astype(jnp.bfloat16)


def pack(queries, candidates, per_owner):
    rows, feature = queries.shape
    return pl.pallas_call(
        functools.partial(pack_kernel, per_owner),
        out_shape=jax.ShapeDtypeStruct((rows + FACT_ROWS, feature), queries.dtype),
        in_specs=[pl.BlockSpec(memory_space=pl.ANY)] * 2,
        out_specs=pl.BlockSpec(memory_space=pltpu.VMEM),
        scratch_shapes=[
            pltpu.VMEM(queries.shape, queries.dtype),
            pltpu.VMEM(candidates.shape, candidates.dtype),
            pltpu.SemaphoreType.DMA((2,)),
        ],
        compiler_params=pltpu.CompilerParams(vmem_limit_bytes=56 * 1024 * 1024),
        name="pack",
    )(queries, candidates)


def fill_tiles(source, source_at, lens, filled, filled_at, first, number):
    row = lax.broadcasted_iota(jnp.int32, source.shape[1:], 0)

    def some(i, carry):
        for k in range(4):
            at = first + 4 * i + k
            tile = source[source_at + at].astype(jnp.float32)
            tile = jnp.where(row < lens[at], tile, tile[0:1, :])
            filled[filled_at + at] = tile.astype(jnp.bfloat16)
        return carry

    lax.fori_loop(0, number // 4, some, 0)


def ready_kernel(chips, slots, parts, lens, candidates, passages, slot_of, filled, sems):
    per_owner = passages.shape[0]
    size = per_owner // parts
    loads = [
        pltpu.make_async_copy(
            passages.at[pl.ds(i * size, size)], filled.at[pl.ds(i * size, size)], sems.at[i]
        )
        for i in range(parts)
    ]
    for load in loads:
        load.start()
    number = candidates.shape[1]
    my_place = ring_place(lax.axis_index("corpus") // CORES, chips)
    wide = jnp.broadcast_to(candidates[...], (number, number)) // (CORES * per_owner)
    tall = wide.astype(jnp.float32).T.astype(jnp.int32)
    row = lax.broadcasted_iota(jnp.int32, (number, number), 0)
    lane = lax.broadcasted_iota(jnp.int32, (number, number), 1)
    earlier = jnp.where((wide == tall) & (lane < row), 1.0, 0.0)
    rank = jnp.sum(earlier, axis=1, keepdims=True).astype(jnp.int32)
    ahead = ring_place(tall, chips) - my_place
    ahead = jnp.where(ahead < 0, ahead + chips, ahead)
    slot_of[...] = ahead * slots + rank
    for i, load in enumerate(loads):
        load.wait()
        fill_tiles(filled, 0, lens, filled, 0, i * size, size)


def ready(lengths, candidates, passages, chips, slots):
    number = candidates.shape[1]
    per_owner = passages.shape[0]
    parts = 4 if per_owner % 16 == 0 else 1
    return pl.pallas_call(
        functools.partial(ready_kernel, chips, slots, parts),
        out_shape=(
            jax.ShapeDtypeStruct((number, number), jnp.int32),
            jax.ShapeDtypeStruct((CORES * per_owner,) + passages.shape[1:], passages.dtype),
        ),
        in_specs=[
            pl.BlockSpec(memory_space=pltpu.SMEM),
            pl.BlockSpec(memory_space=pltpu.VMEM),
            pl.BlockSpec(memory_space=pl.ANY),
        ],
        out_specs=(pl.BlockSpec(memory_space=pltpu.VMEM),) * 2,
        scratch_shapes=[pltpu.SemaphoreType.DMA((parts,))],
        compiler_params=pltpu.CompilerParams(vmem_limit_bytes=VMEM_LIMIT),
        name="ready",
    )(lengths, candidates, passages)


def join_kernel(lens, other, held, filled):
    fill_tiles(other, 0, lens, filled, other.shape[0], 0, other.shape[0])


def join(lengths, other, filled):
    return pl.pallas_call(
        join_kernel,
        out_shape=jax.ShapeDtypeStruct(filled.shape, filled.dtype),
        in_specs=[
            pl.BlockSpec(memory_space=pltpu.SMEM),
            pl.BlockSpec(memory_space=pltpu.VMEM),
            pl.BlockSpec(memory_space=pltpu.VMEM),
        ],
        out_specs=pl.BlockSpec(memory_space=pltpu.VMEM),
        input_output_aliases={2: 0},
        compiler_params=pltpu.CompilerParams(vmem_limit_bytes=VMEM_LIMIT),
        name="join",
    )(lengths, other, filled)


def score_kernel(pieces, slots, query_tok, *refs):
    blocks = len(pieces)
    arrays = sum(pieces)
    tiles = refs[0]
    held = refs[1 : 1 + arrays]
    outs = refs[1 + arrays : 1 + arrays + blocks]
    nearest, plan_v, plan, sem = refs[1 + arrays + blocks :]
    per_chip, tile_rows, feature = tiles.shape
    per_owner = per_chip // CORES
    me = lax.axis_index("corpus")
    first_owner = me // CORES * CORES

    chunks, facts = [], []
    at = 0
    for count in pieces:
        where = [(ref, r) for ref in held[at : at + count] for r in range(0, ref.shape[0], LANES)]
        facts.append(where[-1])
        chunks.append(where[:-1])
        at += count

    sub = lax.broadcasted_iota(jnp.int32, (8, LANES), 0)
    lane = lax.broadcasted_iota(jnp.int32, (8, LANES), 1)
    owner = jnp.full((8, LANES), -1.0, jnp.float32)
    local_id = jnp.zeros((8, LANES), jnp.float32)
    for b, (ref, r) in enumerate(facts):
        fact = ref[r : r + FACT_ROWS, :].astype(jnp.float32)
        owner = jnp.where(sub == b, fact[0:1, :], owner)
        local_id = jnp.where(sub == b, fact[1:2, :], local_id)
    owner = owner.astype(jnp.int32)
    mine = (owner >= first_owner) & (owner < first_owner + CORES)
    ones = jnp.where(mine, 1.0, 0.0)
    rank = ones
    shift = 1
    while shift < LANES:
        rank = rank + jnp.where(lane >= shift, pltpu.roll(rank, shift, 1), 0.0)
        shift *= 2
    rank = jnp.where(mine, rank - 1.0, -1.0)
    tile = local_id + jnp.where(owner == me, 0.0, float(per_owner))
    wanted = jnp.where(lane == slots, jnp.sum(ones, axis=1, keepdims=True), 0.0)
    for s in range(slots):
        found = jnp.sum(jnp.where(rank == float(s), tile, 0.0), axis=1, keepdims=True)
        wanted = jnp.where(lane == s, found, wanted)
    plan_v[...] = wanted.astype(jnp.int32)
    to_scalar = pltpu.make_async_copy(plan_v, plan, sem)
    to_scalar.start()
    to_scalar.wait()

    slot_row = lax.broadcasted_iota(jnp.int32, (slots, LANES), 0)
    slot_lane = lax.broadcasted_iota(jnp.int32, (slots, LANES), 1)
    for b in range(blocks):
        count = plan[b, slots]

        def score_group(g, carry, b=b):
            left = jnp.concatenate([tiles[plan[b, g * GROUP + t]] for t in range(GROUP)], axis=0)
            start = pl.multiple_of(g * (8 * GROUP), 8 * GROUP)
            for c in range(0, len(chunks[b]), 2):
                pair = [ref[r : r + LANES, :] for ref, r in chunks[b][c : c + 2]]
                similar = jnp.dot(
                    left, jnp.concatenate(pair, axis=1), preferred_element_type=jnp.float32
                )
                width = similar.shape[1]
                rows = jnp.max(similar.reshape(GROUP, tile_rows // 8, 8, width), axis=1)
                rows = rows.reshape(8 * GROUP, width)
                for k in range(width // LANES):
                    nearest[c + k, pl.ds(start, 8 * GROUP), :] = rows[:, k * LANES : (k + 1) * LANES]
            return carry

        lax.fori_loop(0, pl.cdiv(count, GROUP), score_group, 0)
        total = jnp.zeros((slots, LANES), jnp.float32)
        for k in range(nearest.shape[0]):
            x = nearest[k, pl.ds(0, slots, stride=8), :]
            for sublane in range(1, 8):
                x = jnp.maximum(x, nearest[k, pl.ds(sublane, slots, stride=8), :])
            shift = query_tok // 2
            while shift >= 1:
                x = x + pltpu.roll(x, LANES - shift, 1)
                shift //= 2
            if k:
                x = pltpu.roll(x, k, 1)
            total = jnp.where(slot_lane % query_tok == k, x, total)
        outs[b][...] = jnp.where(slot_row < count, total / float(query_tok), 0.0)


def score(held, slots, query_tok, tiles):
    pieces = tuple(len(arrays) for arrays in held)
    flat = [x for arrays in held for x in arrays]
    blocks = len(pieces)
    _, tile_rows, feature = tiles.shape
    query_rows = sum(x.shape[0] for x in held[0]) - FACT_ROWS
    flops = 2 * blocks * slots * tile_rows * feature * query_rows
    return pl.pallas_call(
        functools.partial(score_kernel, pieces, slots, query_tok),
        out_shape=(jax.ShapeDtypeStruct((slots, LANES), jnp.float32),) * blocks,
        in_specs=[pl.BlockSpec(memory_space=pltpu.VMEM)] * (1 + len(flat)),
        out_specs=(pl.BlockSpec(memory_space=pltpu.VMEM),) * blocks,
        scratch_shapes=[
            pltpu.VMEM((query_rows // LANES, 8 * slots, LANES), jnp.float32),
            pltpu.VMEM((8, LANES), jnp.int32),
            pltpu.SMEM((8, LANES), jnp.int32),
            pltpu.SemaphoreType.DMA,
        ],
        compiler_params=pltpu.CompilerParams(vmem_limit_bytes=VMEM_LIMIT),
        cost_estimate=pl.CostEstimate(
            flops=3 * flops,
            bytes_accessed=blocks * (slots * tile_rows + query_rows) * feature * 2,
            transcendentals=0,
        ),
        name="score",
    )(tiles, *flat)


def sort_descending(parts, lanes):
    parts = list(parts)
    many = len(parts)
    number = many * 8
    sub = lax.broadcasted_iota(jnp.int32, (8, lanes), 0)
    size = 2
    while size <= number:
        reach = size // 2
        while reach >= 1:
            if reach < many:
                for v in range(many):
                    if v & reach:
                        continue
                    a, b = parts[v], parts[v | reach]
                    high, low = jnp.maximum(a, b), jnp.minimum(a, b)
                    if size >= number:
                        parts[v], parts[v | reach] = high, low
                    elif size < many:
                        down = (v & size) == 0
                        parts[v], parts[v | reach] = (high, low) if down else (low, high)
                    else:
                        down = (sub & (size // many)) == 0
                        parts[v] = jnp.where(down, high, low)
                        parts[v | reach] = jnp.where(down, low, high)
            else:
                step = reach // many
                is_first = (sub & step) == 0
                if size >= number:
                    keep_high = is_first
                else:
                    keep_high = is_first == ((sub & (size // many)) == 0)
                for v in range(many):
                    x = parts[v]
                    partner = jnp.where(is_first, pltpu.roll(x, 8 - step, 0), pltpu.roll(x, step, 0))
                    parts[v] = jnp.where(keep_high, jnp.maximum(x, partner), jnp.minimum(x, partner))
            reach //= 2
        size *= 2
    return parts


def finish_kernel(arrays, per_device, query_tok, topk, slot_of, *refs):
    returned = refs[:arrays]
    scores, best_scores, spread, ranked, rows = refs[arrays:]
    number = slot_of.shape[0]
    step = returned[0].shape[0]
    for at, ref in enumerate(returned):
        spread[at * step : (at + 1) * step, :] = ref[...]
    total = spread.shape[0]
    lane = lax.broadcasted_iota(jnp.int32, (number, total), 1)
    choose = (slot_of[:, 0:1] == lane).astype(jnp.float32).astype(jnp.bfloat16)
    by_candidate = jnp.zeros((number, LANES), jnp.float32)
    for part in split_exact(spread[...]):
        by_candidate += jnp.dot(choose, part, preferred_element_type=jnp.float32)

    def in_order(x):
        x = x.T
        each = LANES // query_tok
        for m in range(each):
            rows[pl.ds(m, query_tok, stride=each), :] = x[m * query_tok : (m + 1) * query_tok, :]
        return rows[...]

    scores[...] = in_order(by_candidate)[:per_device, :]
    many = number // 8
    parts = sort_descending([by_candidate[8 * v : 8 * v + 8, :] for v in range(many)], LANES)
    for v in range(many):
        ranked[pl.ds(v, 8, stride=many), :] = parts[v]
    best_scores[...] = in_order(ranked[...])[:per_device, :topk]


def finish(per_device, query_tok, slot_of, returned):
    number = slot_of.shape[0]
    total = sum(r.shape[0] for r in returned)
    return pl.pallas_call(
        functools.partial(finish_kernel, len(returned), per_device, query_tok, TOPK),
        out_shape=(
            jax.ShapeDtypeStruct((per_device, number), jnp.float32),
            jax.ShapeDtypeStruct((per_device, TOPK), jnp.float32),
        ),
        in_specs=[pl.BlockSpec(memory_space=pltpu.VMEM)] * (1 + len(returned)),
        out_specs=(pl.BlockSpec(memory_space=pltpu.VMEM),) * 2,
        scratch_shapes=[
            pltpu.VMEM((total, LANES), jnp.float32),
            pltpu.VMEM((number, LANES), jnp.float32),
            pltpu.VMEM((LANES, number), jnp.float32),
        ],
        compiler_params=pltpu.CompilerParams(vmem_limit_bytes=VMEM_LIMIT),
        name="finish",
    )(slot_of, *returned)


def local(queries, passages, lengths, candidates):
    peers = lax.axis_size("corpus")
    chips = peers // CORES
    per_owner, tile_rows, feature = passages.shape
    per_device, query_tok = queries.shape[0], queries.shape[1]
    number = candidates.shape[1]
    capacity = max(2, 3 * number // (2 * peers))
    slots = -(-CORES * capacity // 8) * 8
    order = ring_order(chips)

    def moved(x, distance):
        pairs = [
            (order[i] * CORES + core, order[(i + distance) % chips] * CORES + core)
            for i in range(chips)
            for core in range(CORES)
        ]
        return lax.ppermute(x, "corpus", pairs)

    swap = [(i, i ^ 1) for i in range(peers)]
    other = lax.ppermute(passages, "corpus", swap)
    other_lengths = lax.ppermute(lengths, "corpus", swap)
    slot_of, own = ready(lengths, candidates, passages, chips, slots)
    tiles = join(other_lengths, other, own)

    block = pack(queries.reshape(per_device * query_tok, feature), candidates, per_owner)
    half = per_device * query_tok // LANES // 2 * LANES
    middle = chips // 2
    arrived = {0: [block]}

    def send_on(step):
        if step < middle:
            arrived[step] = [moved(x, 1) for x in arrived[step - 1]]
            arrived[-step] = [moved(x, -1) for x in arrived[1 - step]]
        else:
            arrived[step] = [
                moved(arrived[step - 1][0][:half], 1), moved(arrived[1 - step][0][half:], -1)
            ]

    send_on(1)
    back = {}
    for step in range(1, middle + 1):
        if step < middle:
            send_on(step + 1)
        offsets = (0, 1, -1) if step == 1 else (middle,) if step == middle else (step, -step)
        fresh = score([arrived[offset] for offset in offsets], slots, query_tok, tiles)
        if step < middle:
            names = [step + 1, -step - 1] if step + 1 < middle else [middle]
            earlier = [(1 - step) % chips, (step - 1) % chips] if step > 1 else []
            held, fresh, came = lax.optimization_barrier(
                ([arrived[name] for name in names], fresh, [back[j] for j in earlier])
            )
            arrived.update(zip(names, held))
            back.update(zip(earlier, came))
        for offset, result in zip(offsets, fresh):
            back[offset % chips] = moved(result, -offset) if offset else result
    return finish(per_device, query_tok, slot_of, [back[j] for j in range(chips)])


def solution(mesh):
    return jax.shard_map(
        local,
        mesh=mesh,
        in_specs=(
            P(("groups", "corpus"), None, None),
            P(("groups", "corpus"), None, None),
            P(("groups", "corpus")),
            P(("groups", "corpus"), None),
        ),
        out_specs=(P(("groups", "corpus"), None), P(("groups", "corpus"), None)),
        check_vma=False,
    )
```

```python
import functools

import jax
import jax.numpy as jnp
from jax import lax
from jax.experimental import pallas as pl
from jax.experimental.pallas import tpu as pltpu
from jax.sharding import PartitionSpec as P

TOPK = 100
CORES = 2
LANES = 128
FACT_ROWS = 16
GROUP = 4
VMEM_LIMIT = 32 * 1024 * 1024


def ring_order(chips):
    return list(range(0, chips, 2)) + list(range(1, chips, 2))[::-1]


def ring_place(chip, chips):
    return jnp.where(chip % 2 == 0, chip // 2, chips - (chip + 1) // 2)


def split_exact(x):
    high = x.astype(jnp.bfloat16)
    rest = x - high.astype(jnp.float32)
    middle = rest.astype(jnp.bfloat16)
    low = (rest - middle.astype(jnp.float32)).astype(jnp.bfloat16)
    return high, middle, low


def pack_kernel(per_owner, queries_in, candidates_in, block, queries, candidates, sems):
    loads = [
        pltpu.make_async_copy(queries_in, queries, sems.at[0]),
        pltpu.make_async_copy(candidates_in, candidates, sems.at[1]),
    ]
    for load in loads:
        load.start()
    for load in loads:
        load.wait()
    query_rows = queries.shape[0]
    for at in range(0, query_rows, LANES):
        block[at : at + LANES, :] = queries[at : at + LANES, :].T
    ids = jnp.broadcast_to(candidates[...], (FACT_ROWS, candidates.shape[1]))
    row = lax.broadcasted_iota(jnp.int32, ids.shape, 0)
    facts = jnp.where(row == 0, ids // per_owner, jnp.where(row == 1, ids % per_owner, 0))
    block[query_rows:, :] = facts.astype(jnp.float32).astype(jnp.bfloat16)


def pack(queries, candidates, per_owner):
    rows, feature = queries.shape
    return pl.pallas_call(
        functools.partial(pack_kernel, per_owner),
        out_shape=jax.ShapeDtypeStruct((rows + FACT_ROWS, feature), queries.dtype),
        in_specs=[pl.BlockSpec(memory_space=pl.ANY)] * 2,
        out_specs=pl.BlockSpec(memory_space=pltpu.VMEM),
        scratch_shapes=[
            pltpu.VMEM(queries.shape, queries.dtype),
            pltpu.VMEM(candidates.shape, candidates.dtype),
            pltpu.SemaphoreType.DMA((2,)),
        ],
        compiler_params=pltpu.CompilerParams(vmem_limit_bytes=56 * 1024 * 1024),
        name="pack",
    )(queries, candidates)


def fill_tiles(source, source_at, lens, filled, filled_at, first, number):
    row = lax.broadcasted_iota(jnp.int32, source.shape[1:], 0)

    def some(i, carry):
        for k in range(4):
            at = first + 4 * i + k
            tile = source[source_at + at].astype(jnp.float32)
            tile = jnp.where(row < lens[at], tile, tile[0:1, :])
            filled[filled_at + at] = tile.astype(jnp.bfloat16)
        return carry

    lax.fori_loop(0, number // 4, some, 0)


def ready_kernel(chips, slots, parts, lens, candidates, passages, slot_of, filled, sems):
    per_owner = passages.shape[0]
    size = per_owner // parts
    loads = [
        pltpu.make_async_copy(
            passages.at[pl.ds(i * size, size)], filled.at[pl.ds(i * size, size)], sems.at[i]
        )
        for i in range(parts)
    ]
    for load in loads:
        load.start()
    number = candidates.shape[1]
    wide = jnp.broadcast_to(candidates[...], (number, number)) // (CORES * per_owner)
    tall = wide.astype(jnp.float32).T.astype(jnp.int32)
    row = lax.broadcasted_iota(jnp.int32, (number, number), 0)
    lane = lax.broadcasted_iota(jnp.int32, (number, number), 1)
    earlier = jnp.where((wide == tall) & (lane < row), 1.0, 0.0)
    rank = jnp.sum(earlier, axis=1, keepdims=True).astype(jnp.int32)
    slot_of[...] = ring_place(tall, chips) * slots + rank
    for i, load in enumerate(loads):
        load.wait()
        fill_tiles(filled, 0, lens, filled, 0, i * size, size)


def ready(lengths, candidates, passages, chips, slots):
    number = candidates.shape[1]
    per_owner = passages.shape[0]
    parts = 4 if per_owner % 16 == 0 else 1
    return pl.pallas_call(
        functools.partial(ready_kernel, chips, slots, parts),
        out_shape=(
            jax.ShapeDtypeStruct((number, number), jnp.int32),
            jax.ShapeDtypeStruct((CORES * per_owner,) + passages.shape[1:], passages.dtype),
        ),
        in_specs=[
            pl.BlockSpec(memory_space=pltpu.SMEM),
            pl.BlockSpec(memory_space=pltpu.VMEM),
            pl.BlockSpec(memory_space=pl.ANY),
        ],
        out_specs=(pl.BlockSpec(memory_space=pltpu.VMEM),) * 2,
        scratch_shapes=[pltpu.SemaphoreType.DMA((parts,))],
        compiler_params=pltpu.CompilerParams(vmem_limit_bytes=VMEM_LIMIT),
        name="ready",
    )(lengths, candidates, passages)


def join_kernel(lens, other, held, filled):
    fill_tiles(other, 0, lens, filled, other.shape[0], 0, other.shape[0])


def join(lengths, other, filled):
    return pl.pallas_call(
        join_kernel,
        out_shape=jax.ShapeDtypeStruct(filled.shape, filled.dtype),
        in_specs=[
            pl.BlockSpec(memory_space=pltpu.SMEM),
            pl.BlockSpec(memory_space=pltpu.VMEM),
            pl.BlockSpec(memory_space=pltpu.VMEM),
        ],
        out_specs=pl.BlockSpec(memory_space=pltpu.VMEM),
        input_output_aliases={2: 0},
        compiler_params=pltpu.CompilerParams(vmem_limit_bytes=VMEM_LIMIT),
        name="join",
    )(lengths, other, filled)


def score_kernel(pieces, offsets, slots, query_tok, has_earlier, *refs):
    blocks = len(pieces)
    arrays = sum(pieces)
    tiles = refs[0]
    held = refs[1 : 1 + arrays]
    out, weights, nearest, plan_v, plan, sem, weight_sems = refs[1 + arrays + has_earlier :]
    per_chip, tile_rows, feature = tiles.shape
    per_owner = per_chip // CORES
    chips = out.shape[0]
    me = lax.axis_index("corpus")
    first_owner = me // CORES * CORES
    my_place = ring_place(me // CORES, chips)

    loads, facts = [], []
    at = 0
    for b, count in enumerate(pieces):
        row = 0
        for ref in held[at : at + count]:
            rows = min(ref.shape[0], weights.shape[1] - row)
            loads.append(
                pltpu.make_async_copy(
                    ref.at[pl.ds(0, rows)], weights.at[b, pl.ds(row, rows)], weight_sems.at[len(loads)]
                )
            )
            loads[-1].start()
            row += rows
        facts.append((ref, rows))
        at += count

    sub = lax.broadcasted_iota(jnp.int32, (8, LANES), 0)
    lane = lax.broadcasted_iota(jnp.int32, (8, LANES), 1)
    owner = jnp.full((8, LANES), -1.0, jnp.float32)
    local_id = jnp.zeros((8, LANES), jnp.float32)
    for b, (ref, r) in enumerate(facts):
        fact = ref[r : r + FACT_ROWS, :].astype(jnp.float32)
        owner = jnp.where(sub == b, fact[0:1, :], owner)
        local_id = jnp.where(sub == b, fact[1:2, :], local_id)
    owner = owner.astype(jnp.int32)
    mine = (owner >= first_owner) & (owner < first_owner + CORES)
    ones = jnp.where(mine, 1.0, 0.0)
    tri_row = lax.broadcasted_iota(jnp.int32, (LANES, LANES), 0)
    tri_lane = lax.broadcasted_iota(jnp.int32, (LANES, LANES), 1)
    before = jnp.where(tri_row < tri_lane, 1.0, 0.0).astype(jnp.bfloat16)
    rank = jnp.dot(ones.astype(jnp.bfloat16), before, preferred_element_type=jnp.float32)
    rank = jnp.where(mine, rank, -1.0)
    tile = local_id + jnp.where(owner == me, 0.0, float(per_owner))
    wanted = jnp.where(lane == slots, jnp.sum(ones, axis=1, keepdims=True), 0.0)
    for s in range(slots):
        found = jnp.sum(jnp.where(rank == float(s), tile, 0.0), axis=1, keepdims=True)
        wanted = jnp.where(lane == s, found, wanted)
    plan_v[...] = wanted.astype(jnp.int32)
    to_scalar = pltpu.make_async_copy(plan_v, plan, sem)
    to_scalar.start()
    to_scalar.wait()
    for load in loads:
        load.wait()

    slot_row = lax.broadcasted_iota(jnp.int32, (slots, LANES), 0)
    slot_lane = lax.broadcasted_iota(jnp.int32, (slots, LANES), 1)
    most = slots // GROUP
    least = max(1, most // 2)

    def score_block(b, carry):
        count = plan[b, slots]
        groups = pl.cdiv(count, GROUP)

        def score_groups(number):
            rows = number * GROUP * 8

            def columns(c, carry):
                left = jnp.concatenate([tiles[plan[b, t]] for t in range(number * GROUP)], axis=0)
                at = pl.multiple_of(c * (2 * LANES), 2 * LANES)
                pair = [weights[b, pl.ds(at + k * LANES, LANES), :] for k in range(2)]
                similar = jnp.dot(
                    left, jnp.concatenate(pair, axis=1), preferred_element_type=jnp.float32
                )
                best = jnp.max(similar.reshape(number * GROUP, tile_rows // 8, 8, 2 * LANES), axis=1)
                best = best.reshape(rows, 2 * LANES)
                for k in range(2):
                    nearest[2 * c + k, 0:rows, :] = best[:, k * LANES : (k + 1) * LANES]
                return carry

            lax.fori_loop(0, weights.shape[1] // (2 * LANES), columns, 0)

        for number in range(least, most + 1):
            wanted_now = (groups <= number) if number == least else (groups == number)
            pl.when(wanted_now)(functools.partial(score_groups, number))

        total = jnp.zeros((slots, LANES), jnp.float32)
        for k in range(nearest.shape[0]):
            x = nearest[k, pl.ds(0, slots, stride=8), :]
            for sublane in range(1, 8):
                x = jnp.maximum(x, nearest[k, pl.ds(sublane, slots, stride=8), :])
            shift = query_tok // 2
            while shift >= 1:
                x = x + pltpu.roll(x, LANES - shift, 1)
                shift //= 2
            if k:
                x = pltpu.roll(x, k, 1)
            total = jnp.where(slot_lane % query_tok == k, x, total)
        offset = offsets[-1]
        for k in range(blocks - 1):
            offset = jnp.where(b == k, offsets[k], offset)
        place = my_place - offset
        place = jnp.where(place < 0, place + chips, place)
        out[place] = jnp.where(slot_row < count, total / float(query_tok), 0.0)
        return carry

    lax.fori_loop(0, blocks, score_block, 0)


def score(held, offsets, slots, query_tok, chips, tiles, earlier):
    pieces = tuple(len(arrays) for arrays in held)
    flat = [x for arrays in held for x in arrays]
    blocks = len(pieces)
    _, tile_rows, feature = tiles.shape
    query_rows = sum(x.shape[0] for x in held[0]) - FACT_ROWS
    flops = 2 * blocks * slots * tile_rows * feature * query_rows
    kept = [] if earlier is None else [earlier]
    return pl.pallas_call(
        functools.partial(score_kernel, pieces, offsets, slots, query_tok, len(kept)),
        out_shape=jax.ShapeDtypeStruct((chips, slots, LANES), jnp.float32),
        in_specs=[pl.BlockSpec(memory_space=pltpu.VMEM)] * (1 + len(flat) + len(kept)),
        out_specs=pl.BlockSpec(memory_space=pltpu.VMEM),
        input_output_aliases={1 + len(flat): 0} if kept else {},
        scratch_shapes=[
            pltpu.VMEM((blocks, query_rows, feature), tiles.dtype),
            pltpu.VMEM((query_rows // LANES, 8 * slots, LANES), jnp.float32),
            pltpu.VMEM((8, LANES), jnp.int32),
            pltpu.SMEM((8, LANES), jnp.int32),
            pltpu.SemaphoreType.DMA,
            pltpu.SemaphoreType.DMA((len(flat),)),
        ],
        compiler_params=pltpu.CompilerParams(vmem_limit_bytes=VMEM_LIMIT),
        cost_estimate=pl.CostEstimate(
            flops=3 * flops,
            bytes_accessed=blocks * (slots * tile_rows + query_rows) * feature * 2,
            transcendentals=0,
        ),
        name="score",
    )(tiles, *flat, *kept)


def sort_descending(parts, lanes):
    parts = list(parts)
    many = len(parts)
    number = many * 8
    sub = lax.broadcasted_iota(jnp.int32, (8, lanes), 0)
    size = 2
    while size <= number:
        reach = size // 2
        while reach >= 1:
            if reach < many:
                for v in range(many):
                    if v & reach:
                        continue
                    a, b = parts[v], parts[v | reach]
                    high, low = jnp.maximum(a, b), jnp.minimum(a, b)
                    if size >= number:
                        parts[v], parts[v | reach] = high, low
                    elif size < many:
                        down = (v & size) == 0
                        parts[v], parts[v | reach] = (high, low) if down else (low, high)
                    else:
                        down = (sub & (size // many)) == 0
                        parts[v] = jnp.where(down, high, low)
                        parts[v | reach] = jnp.where(down, low, high)
            else:
                step = reach // many
                is_first = (sub & step) == 0
                if size >= number:
                    keep_high = is_first
                else:
                    keep_high = is_first == ((sub & (size // many)) == 0)
                for v in range(many):
                    x = parts[v]
                    partner = jnp.where(is_first, pltpu.roll(x, 8 - step, 0), pltpu.roll(x, step, 0))
                    parts[v] = jnp.where(keep_high, jnp.maximum(x, partner), jnp.minimum(x, partner))
            reach //= 2
        size *= 2
    return parts


def finish_kernel(per_device, query_tok, topk, slot_of, returned, scores, best_scores, ranked, rows):
    number = slot_of.shape[0]
    spread = returned[...].reshape(returned.shape[0] * returned.shape[1], LANES)
    total = spread.shape[0]
    lane = lax.broadcasted_iota(jnp.int32, (number, total), 1)
    choose = (slot_of[:, 0:1] == lane).astype(jnp.float32).astype(jnp.bfloat16)
    by_candidate = jnp.zeros((number, LANES), jnp.float32)
    for part in split_exact(spread):
        by_candidate += jnp.dot(choose, part, preferred_element_type=jnp.float32)

    def in_order(x):
        x = x.T
        each = LANES // query_tok
        for m in range(each):
            rows[pl.ds(m, query_tok, stride=each), :] = x[m * query_tok : (m + 1) * query_tok, :]
        return rows[...]

    scores[...] = in_order(by_candidate)[:per_device, :]
    many = number // 8
    parts = sort_descending([by_candidate[8 * v : 8 * v + 8, :] for v in range(many)], LANES)
    for v in range(many):
        ranked[pl.ds(v, 8, stride=many), :] = parts[v]
    best_scores[...] = in_order(ranked[...])[:per_device, :topk]


def finish(per_device, query_tok, slot_of, returned):
    number = slot_of.shape[0]
    return pl.pallas_call(
        functools.partial(finish_kernel, per_device, query_tok, TOPK),
        out_shape=(
            jax.ShapeDtypeStruct((per_device, number), jnp.float32),
            jax.ShapeDtypeStruct((per_device, TOPK), jnp.float32),
        ),
        in_specs=[pl.BlockSpec(memory_space=pltpu.VMEM)] * 2,
        out_specs=(pl.BlockSpec(memory_space=pltpu.VMEM),) * 2,
        scratch_shapes=[
            pltpu.VMEM((number, LANES), jnp.float32),
            pltpu.VMEM((LANES, number), jnp.float32),
        ],
        compiler_params=pltpu.CompilerParams(vmem_limit_bytes=VMEM_LIMIT),
        name="finish",
    )(slot_of, returned)


def local(queries, passages, lengths, candidates):
    peers = lax.axis_size("corpus")
    chips = peers // CORES
    per_owner, tile_rows, feature = passages.shape
    per_device, query_tok = queries.shape[0], queries.shape[1]
    number = candidates.shape[1]
    capacity = max(2, 3 * number // (2 * peers))
    slots = -(-CORES * capacity // 8) * 8
    order = ring_order(chips)

    def moved(x, distance):
        pairs = [
            (order[i] * CORES + core, order[(i + distance) % chips] * CORES + core)
            for i in range(chips)
            for core in range(CORES)
        ]
        return lax.ppermute(x, "corpus", pairs)

    swap = [(i, i ^ 1) for i in range(peers)]
    other = lax.ppermute(passages, "corpus", swap)
    other_lengths = lax.ppermute(lengths, "corpus", swap)
    slot_of, own = ready(lengths, candidates, passages, chips, slots)
    tiles = join(other_lengths, other, own)

    block = pack(queries.reshape(per_device * query_tok, feature), candidates, per_owner)
    half = per_device * query_tok // LANES // 2 * LANES
    middle = chips // 2
    arrived = {0: [block]}

    def send_on(step):
        if step < middle:
            arrived[step] = [moved(x, 1) for x in arrived[step - 1]]
            arrived[-step] = [moved(x, -1) for x in arrived[1 - step]]
        else:
            arrived[step] = [
                moved(arrived[step - 1][0][:half], 1), moved(arrived[1 - step][0][half:], -1)
            ]

    send_on(1)
    fresh = None
    for step in range(1, middle + 1):
        if step < middle:
            send_on(step + 1)
        offsets = (0, 1, -1) if step == 1 else (middle,) if step == middle else (step, -step)
        fresh = score(
            [arrived[offset] for offset in offsets], tuple(offset % chips for offset in offsets),
            slots, query_tok, chips, tiles, fresh,
        )
        if step < middle:
            names = [step + 1, -step - 1] if step + 1 < middle else [middle]
            held, fresh = lax.optimization_barrier(([arrived[name] for name in names], fresh))
            arrived.update(zip(names, held))
    by_place = [[order[i] * CORES + k for i in range(chips)] for k in range(CORES)]
    returned = lax.all_to_all(
        fresh, "corpus", split_axis=0, concat_axis=0, tiled=True, axis_index_groups=by_place
    )
    return finish(per_device, query_tok, slot_of, returned)


def solution(mesh):
    return jax.shard_map(
        local,
        mesh=mesh,
        in_specs=(
            P(("groups", "corpus"), None, None),
            P(("groups", "corpus"), None, None),
            P(("groups", "corpus")),
            P(("groups", "corpus"), None),
        ),
        out_specs=(P(("groups", "corpus"), None), P(("groups", "corpus"), None)),
        check_vma=False,
    )
```

```python
import functools

import jax
import jax.numpy as jnp
from jax import lax
from jax.experimental import pallas as pl
from jax.experimental.pallas import tpu as pltpu
from jax.sharding import PartitionSpec as P

TOPK = 100
CORES = 2
LANES = 128
GROUP = 8
VMEM_LIMIT = 32 * 1024 * 1024


def ring_order(chips):
    return list(range(0, chips, 2)) + list(range(1, chips, 2))[::-1]


def ring_place(chip, chips):
    return jnp.where(chip % 2 == 0, chip // 2, chips - (chip + 1) // 2)


def split_exact(x):
    high = x.astype(jnp.bfloat16)
    rest = x - high.astype(jnp.float32)
    middle = rest.astype(jnp.bfloat16)
    low = (rest - middle.astype(jnp.float32)).astype(jnp.bfloat16)
    return high, middle, low


def pack_kernel(per_owner, chips, slots, queries_in, candidates_in, block, queries, candidates, sems):
    loads = [
        pltpu.make_async_copy(queries_in, queries, sems.at[0]),
        pltpu.make_async_copy(candidates_in, candidates, sems.at[1]),
    ]
    for load in loads:
        load.start()
    for load in loads:
        load.wait()
    query_rows = queries.shape[0]
    for at in range(0, query_rows, LANES):
        block[at : at + LANES, :] = queries[at : at + LANES, :].T
    fact_rows = block.shape[0] - query_rows
    number = candidates.shape[1]
    per_chip = CORES * per_owner
    ids = jnp.broadcast_to(candidates[...], (fact_rows, number))
    row = lax.broadcasted_iota(jnp.int32, ids.shape, 0)
    lane = lax.broadcasted_iota(jnp.int32, ids.shape, 1)
    chosen = ring_place(ids // per_chip, chips) == row
    ones = jnp.where(chosen, 1.0, 0.0)
    before = jnp.where(
        lax.broadcasted_iota(jnp.int32, (number, number), 0)
        < lax.broadcasted_iota(jnp.int32, (number, number), 1), 1.0, 0.0,
    )
    rank = jnp.dot(
        ones.astype(jnp.bfloat16), before.astype(jnp.bfloat16), preferred_element_type=jnp.float32
    )
    rank = jnp.where(chosen, rank, -1.0)
    tile = (ids % per_chip).astype(jnp.float32)
    wanted = jnp.where(lane == slots, jnp.sum(ones, axis=1, keepdims=True), 0.0)
    for s in range(slots):
        found = jnp.sum(jnp.where(rank == float(s), tile, 0.0), axis=1, keepdims=True)
        wanted = jnp.where(lane == s, found, wanted)
    block[query_rows:, :] = wanted.astype(jnp.bfloat16)


def fact_rows_of(chips):
    return -(-chips // 16) * 16


def pack(queries, candidates, per_owner, chips, slots):
    rows, feature = queries.shape
    return pl.pallas_call(
        functools.partial(pack_kernel, per_owner, chips, slots),
        out_shape=jax.ShapeDtypeStruct((rows + fact_rows_of(chips), feature), queries.dtype),
        in_specs=[pl.BlockSpec(memory_space=pl.ANY)] * 2,
        out_specs=pl.BlockSpec(memory_space=pltpu.VMEM),
        scratch_shapes=[
            pltpu.VMEM(queries.shape, queries.dtype),
            pltpu.VMEM(candidates.shape, candidates.dtype),
            pltpu.SemaphoreType.DMA((2,)),
        ],
        compiler_params=pltpu.CompilerParams(vmem_limit_bytes=56 * 1024 * 1024),
        name="pack",
    )(queries, candidates)


def fill_tiles(source, source_at, lens, filled, filled_at, first, number):
    row = lax.broadcasted_iota(jnp.int32, source.shape[1:], 0)

    def some(i, carry):
        for k in range(4):
            at = first + 4 * i + k
            tile = source[source_at + at].astype(jnp.float32)
            tile = jnp.where(row < lens[at], tile, tile[0:1, :])
            filled[filled_at + at] = tile.astype(jnp.bfloat16)
        return carry

    lax.fori_loop(0, number // 4, some, 0)


def ready_kernel(chips, slots, parts, lens, candidates, passages, slot_of, filled, sems):
    per_owner = passages.shape[0]
    size = per_owner // parts
    base = lax.axis_index("corpus") % CORES * per_owner
    loads = [
        pltpu.make_async_copy(
            passages.at[pl.ds(i * size, size)], filled.at[pl.ds(base + i * size, size)], sems.at[i]
        )
        for i in range(parts)
    ]
    for load in loads:
        load.start()
    number = candidates.shape[1]
    my_place = ring_place(lax.axis_index("corpus") // CORES, chips)
    wide = jnp.broadcast_to(candidates[...], (number, number)) // (CORES * per_owner)
    tall = wide.astype(jnp.float32).T.astype(jnp.int32)
    row = lax.broadcasted_iota(jnp.int32, (number, number), 0)
    lane = lax.broadcasted_iota(jnp.int32, (number, number), 1)
    earlier = jnp.where((wide == tall) & (lane < row), 1.0, 0.0)
    rank = jnp.sum(earlier, axis=1, keepdims=True).astype(jnp.int32)
    ahead = ring_place(tall, chips) - my_place
    ahead = jnp.where(ahead < 0, ahead + chips, ahead)
    slot_of[...] = ahead * slots + rank
    for i, load in enumerate(loads):
        load.wait()
        fill_tiles(filled, base, lens, filled, base, i * size, size)


def ready(lengths, candidates, passages, chips, slots):
    number = candidates.shape[1]
    per_owner = passages.shape[0]
    parts = 4 if per_owner % 16 == 0 else 1
    return pl.pallas_call(
        functools.partial(ready_kernel, chips, slots, parts),
        out_shape=(
            jax.ShapeDtypeStruct((number, number), jnp.int32),
            jax.ShapeDtypeStruct((CORES * per_owner,) + passages.shape[1:], passages.dtype),
        ),
        in_specs=[
            pl.BlockSpec(memory_space=pltpu.SMEM),
            pl.BlockSpec(memory_space=pltpu.VMEM),
            pl.BlockSpec(memory_space=pl.ANY),
        ],
        out_specs=(pl.BlockSpec(memory_space=pltpu.VMEM),) * 2,
        scratch_shapes=[pltpu.SemaphoreType.DMA((parts,))],
        compiler_params=pltpu.CompilerParams(vmem_limit_bytes=VMEM_LIMIT),
        name="ready",
    )(lengths, candidates, passages)


def join_kernel(lens, other, held, filled):
    per_owner = other.shape[0]
    base = (1 - lax.axis_index("corpus") % CORES) * per_owner
    fill_tiles(other, 0, lens, filled, base, 0, per_owner)


def join(lengths, other, filled):
    return pl.pallas_call(
        join_kernel,
        out_shape=jax.ShapeDtypeStruct(filled.shape, filled.dtype),
        in_specs=[
            pl.BlockSpec(memory_space=pltpu.SMEM),
            pl.BlockSpec(memory_space=pltpu.VMEM),
            pl.BlockSpec(memory_space=pltpu.VMEM),
        ],
        out_specs=pl.BlockSpec(memory_space=pltpu.VMEM),
        input_output_aliases={2: 0},
        compiler_params=pltpu.CompilerParams(vmem_limit_bytes=VMEM_LIMIT),
        name="join",
    )(lengths, other, filled)


def score_kernel(pieces, slots, query_tok, chips, *refs):
    blocks = len(pieces)
    arrays = sum(pieces)
    tiles = refs[0]
    held = refs[1 : 1 + arrays]
    outs = refs[1 + arrays : 1 + arrays + blocks]
    weights, nearest, plan_v, plan, sem, weight_sems = refs[1 + arrays + blocks :]
    tile_rows = tiles.shape[1]
    my_place = ring_place(lax.axis_index("corpus") // CORES, chips)
    fact_rows = fact_rows_of(chips)

    loads = []
    fact_row = lax.broadcasted_iota(jnp.int32, (fact_rows, LANES), 0)
    at = 0
    for b, count in enumerate(pieces):
        row = 0
        for ref in held[at : at + count]:
            rows = min(ref.shape[0], weights.shape[1] - row)
            loads.append(
                pltpu.make_async_copy(
                    ref.at[pl.ds(0, rows)], weights.at[b, pl.ds(row, rows)], weight_sems.at[len(loads)]
                )
            )
            row += rows
        fact = ref[rows : rows + fact_rows, :].astype(jnp.float32)
        fact = jnp.sum(jnp.where(fact_row == my_place, fact, 0.0), axis=0, keepdims=True)
        plan_v[b : b + 1, :] = fact.astype(jnp.int32)
        at += count
    to_scalar = pltpu.make_async_copy(plan_v, plan, sem)
    to_scalar.start()
    for load in loads:
        load.start()
    to_scalar.wait()
    for load in loads:
        load.wait()

    slot_row = lax.broadcasted_iota(jnp.int32, (slots, LANES), 0)
    slot_lane = lax.broadcasted_iota(jnp.int32, (slots, LANES), 1)

    def score_block(b, carry):
        count = plan[b, slots]

        def score_tiles(first, number):
            left = jnp.concatenate([tiles[plan[b, first + t]] for t in range(number)], axis=0)
            start = pl.multiple_of(first * 8, 8 * number)
            for c in range(0, nearest.shape[0], 2):
                pair = [weights[b, k * LANES : (k + 1) * LANES, :] for k in (c, c + 1)]
                similar = jnp.dot(
                    left, jnp.concatenate(pair, axis=1), preferred_element_type=jnp.float32
                )
                best = jnp.max(similar.reshape(number, tile_rows // 8, 8, 2 * LANES), axis=1)
                best = best.reshape(number * 8, 2 * LANES)
                for k in range(2):
                    nearest[c + k, pl.ds(start, number * 8), :] = best[:, k * LANES : (k + 1) * LANES]

        whole = count // GROUP
        rest = count - whole * GROUP
        small = (rest > 0) & (rest <= GROUP // 2)
        turns = pl.cdiv(count, GROUP) - small.astype(jnp.int32)

        def turn(g, carry):
            score_tiles(pl.multiple_of(g * GROUP, GROUP), GROUP)
            return carry

        lax.fori_loop(0, turns, turn, 0)
        pl.when(small)(lambda: score_tiles(pl.multiple_of(whole * GROUP, GROUP), GROUP // 2))

        total = jnp.zeros((slots, LANES), jnp.float32)
        for k in range(nearest.shape[0]):
            x = nearest[k, pl.ds(0, slots, stride=8), :]
            for sublane in range(1, 8):
                x = jnp.maximum(x, nearest[k, pl.ds(sublane, slots, stride=8), :])
            shift = query_tok // 2
            while shift >= 1:
                x = x + pltpu.roll(x, LANES - shift, 1)
                shift //= 2
            if k:
                x = pltpu.roll(x, k, 1)
            total = jnp.where(slot_lane % query_tok == k, x, total)
        total = jnp.where(slot_row < count, total / float(query_tok), 0.0)
        for k in range(blocks):

            @pl.when(b == k)
            def _(k=k):
                outs[k][...] = total

        return carry

    lax.fori_loop(0, blocks, score_block, 0)


def score(held, slots, query_tok, chips, tiles):
    pieces = tuple(len(arrays) for arrays in held)
    flat = [x for arrays in held for x in arrays]
    blocks = len(pieces)
    _, tile_rows, feature = tiles.shape
    query_rows = sum(x.shape[0] for x in held[0]) - fact_rows_of(chips)
    flops = 2 * blocks * slots * tile_rows * feature * query_rows
    return pl.pallas_call(
        functools.partial(score_kernel, pieces, slots, query_tok, chips),
        out_shape=(jax.ShapeDtypeStruct((slots, LANES), jnp.float32),) * blocks,
        in_specs=[pl.BlockSpec(memory_space=pltpu.VMEM)] * (1 + len(flat)),
        out_specs=(pl.BlockSpec(memory_space=pltpu.VMEM),) * blocks,
        scratch_shapes=[
            pltpu.VMEM((blocks, query_rows, feature), tiles.dtype),
            pltpu.VMEM((query_rows // LANES, 8 * slots, LANES), jnp.float32),
            pltpu.VMEM((8, LANES), jnp.int32),
            pltpu.SMEM((8, LANES), jnp.int32),
            pltpu.SemaphoreType.DMA,
            pltpu.SemaphoreType.DMA((len(flat),)),
        ],
        compiler_params=pltpu.CompilerParams(vmem_limit_bytes=VMEM_LIMIT),
        cost_estimate=pl.CostEstimate(
            flops=3 * flops,
            bytes_accessed=blocks * (slots * tile_rows + query_rows) * feature * 2,
            transcendentals=0,
        ),
        name="score",
    )(tiles, *flat)


def sort_descending(parts, lanes):
    parts = list(parts)
    many = len(parts)
    number = many * 8
    sub = lax.broadcasted_iota(jnp.int32, (8, lanes), 0)
    size = 2
    while size <= number:
        reach = size // 2
        while reach >= 1:
            if reach < many:
                for v in range(many):
                    if v & reach:
                        continue
                    a, b = parts[v], parts[v | reach]
                    high, low = jnp.maximum(a, b), jnp.minimum(a, b)
                    if size >= number:
                        parts[v], parts[v | reach] = high, low
                    elif size < many:
                        down = (v & size) == 0
                        parts[v], parts[v | reach] = (high, low) if down else (low, high)
                    else:
                        down = (sub & (size // many)) == 0
                        parts[v] = jnp.where(down, high, low)
                        parts[v | reach] = jnp.where(down, low, high)
            else:
                step = reach // many
                is_first = (sub & step) == 0
                if size >= number:
                    keep_high = is_first
                else:
                    keep_high = is_first == ((sub & (size // many)) == 0)
                for v in range(many):
                    x = parts[v]
                    partner = jnp.where(is_first, pltpu.roll(x, 8 - step, 0), pltpu.roll(x, step, 0))
                    parts[v] = jnp.where(keep_high, jnp.maximum(x, partner), jnp.minimum(x, partner))
            reach //= 2
        size *= 2
    return parts


def finish_kernel(arrays, per_device, query_tok, topk, slot_of, *refs):
    returned = refs[:arrays]
    scores, best_scores, spread, ranked, rows = refs[arrays:]
    number = slot_of.shape[0]
    step = returned[0].shape[0]
    for at, ref in enumerate(returned):
        spread[at * step : (at + 1) * step, :] = ref[...]
    total = spread.shape[0]
    lane = lax.broadcasted_iota(jnp.int32, (number, total), 1)
    choose = (slot_of[:, 0:1] == lane).astype(jnp.float32).astype(jnp.bfloat16)
    by_candidate = jnp.zeros((number, LANES), jnp.float32)
    for part in split_exact(spread[...]):
        by_candidate += jnp.dot(choose, part, preferred_element_type=jnp.float32)

    def in_order(x):
        x = x.T
        each = LANES // query_tok
        for m in range(each):
            rows[pl.ds(m, query_tok, stride=each), :] = x[m * query_tok : (m + 1) * query_tok, :]
        return rows[...]

    scores[...] = in_order(by_candidate)[:per_device, :]
    many = number // 8
    parts = sort_descending([by_candidate[8 * v : 8 * v + 8, :] for v in range(many)], LANES)
    for v in range(many):
        ranked[pl.ds(v, 8, stride=many), :] = parts[v]
    best_scores[...] = in_order(ranked[...])[:per_device, :topk]


def finish(per_device, query_tok, slot_of, returned):
    number = slot_of.shape[0]
    total = sum(r.shape[0] for r in returned)
    return pl.pallas_call(
        functools.partial(finish_kernel, len(returned), per_device, query_tok, TOPK),
        out_shape=(
            jax.ShapeDtypeStruct((per_device, number), jnp.float32),
            jax.ShapeDtypeStruct((per_device, TOPK), jnp.float32),
        ),
        in_specs=[pl.BlockSpec(memory_space=pltpu.VMEM)] * (1 + len(returned)),
        out_specs=(pl.BlockSpec(memory_space=pltpu.VMEM),) * 2,
        scratch_shapes=[
            pltpu.VMEM((total, LANES), jnp.float32),
            pltpu.VMEM((number, LANES), jnp.float32),
            pltpu.VMEM((LANES, number), jnp.float32),
        ],
        compiler_params=pltpu.CompilerParams(vmem_limit_bytes=VMEM_LIMIT),
        name="finish",
    )(slot_of, *returned)


def local(queries, passages, lengths, candidates):
    peers = lax.axis_size("corpus")
    chips = peers // CORES
    per_owner, tile_rows, feature = passages.shape
    per_device, query_tok = queries.shape[0], queries.shape[1]
    number = candidates.shape[1]
    capacity = max(2, 3 * number // (2 * peers))
    slots = -(-CORES * capacity // 8) * 8
    order = ring_order(chips)

    def moved(x, distance):
        pairs = [
            (order[i] * CORES + core, order[(i + distance) % chips] * CORES + core)
            for i in range(chips)
            for core in range(CORES)
        ]
        return lax.ppermute(x, "corpus", pairs)

    swap = [(i, i ^ 1) for i in range(peers)]
    other = lax.ppermute(passages, "corpus", swap)
    other_lengths = lax.ppermute(lengths, "corpus", swap)
    slot_of, own = ready(lengths, candidates, passages, chips, slots)
    tiles = join(other_lengths, other, own)

    block = pack(
        queries.reshape(per_device * query_tok, feature), candidates, per_owner, chips, slots
    )
    half = per_device * query_tok // LANES // 2 * LANES
    middle = chips // 2
    arrived = {0: [block]}

    def send_on(step):
        if step < middle:
            arrived[step] = [moved(x, 1) for x in arrived[step - 1]]
            arrived[-step] = [moved(x, -1) for x in arrived[1 - step]]
        else:
            arrived[step] = [
                moved(arrived[step - 1][0][:half], 1), moved(arrived[1 - step][0][half:], -1)
            ]

    send_on(1)
    back = {}
    for step in range(middle + 1):
        if 0 < step < middle:
            send_on(step + 1)
        offsets = (step,) if step in (0, middle) else (step, -step)
        fresh = score([arrived[offset] for offset in offsets], slots, query_tok, chips, tiles)
        earlier = [(step - 1) % chips, (1 - step) % chips] if step > 1 else []
        names = [] if step == middle else [step + 1, -step - 1] if step + 1 < middle else [middle]
        held, fresh, came = lax.optimization_barrier(
            ([arrived[name] for name in names], fresh, [back[j] for j in earlier])
        )
        arrived.update(zip(names, held))
        back.update(zip(earlier, came))
        for offset, result in zip(offsets, fresh):
            back[offset % chips] = moved(result, -offset) if offset else result
    return finish(per_device, query_tok, slot_of, [back[j] for j in range(chips)])


def solution(mesh):
    return jax.shard_map(
        local,
        mesh=mesh,
        in_specs=(
            P(("groups", "corpus"), None, None),
            P(("groups", "corpus"), None, None),
            P(("groups", "corpus")),
            P(("groups", "corpus"), None),
        ),
        out_specs=(P(("groups", "corpus"), None), P(("groups", "corpus"), None)),
        check_vma=False,
    )
```

```python
import functools

import jax
import jax.numpy as jnp
from jax import lax
from jax.experimental import pallas as pl
from jax.experimental.pallas import tpu as pltpu
from jax.sharding import PartitionSpec as P

TOPK = 100
CORES = 2
LANES = 128
GROUP = 8
VMEM_LIMIT = 32 * 1024 * 1024


def ring_order(chips):
    return list(range(0, chips, 2)) + list(range(1, chips, 2))[::-1]


def ring_place(chip, chips):
    return jnp.where(chip % 2 == 0, chip // 2, chips - (chip + 1) // 2)


def split_exact(x):
    high = x.astype(jnp.bfloat16)
    rest = x - high.astype(jnp.float32)
    middle = rest.astype(jnp.bfloat16)
    low = (rest - middle.astype(jnp.float32)).astype(jnp.bfloat16)
    return high, middle, low


def pack_kernel(per_owner, chips, slots, queries_in, candidates_in, block, queries, candidates, sems):
    loads = [
        pltpu.make_async_copy(queries_in, queries, sems.at[0]),
        pltpu.make_async_copy(candidates_in, candidates, sems.at[1]),
    ]
    for load in loads:
        load.start()
    for load in loads:
        load.wait()
    query_rows = queries.shape[0]
    for at in range(0, query_rows, LANES):
        block[at : at + LANES, :] = queries[at : at + LANES, :].T
    fact_rows = block.shape[0] - query_rows
    number = candidates.shape[1]
    per_chip = CORES * per_owner
    ids = jnp.broadcast_to(candidates[...], (fact_rows, number))
    row = lax.broadcasted_iota(jnp.int32, ids.shape, 0)
    lane = lax.broadcasted_iota(jnp.int32, ids.shape, 1)
    chosen = ring_place(ids // per_chip, chips) == row
    ones = jnp.where(chosen, 1.0, 0.0)
    before = jnp.where(
        lax.broadcasted_iota(jnp.int32, (number, number), 0)
        < lax.broadcasted_iota(jnp.int32, (number, number), 1), 1.0, 0.0,
    )
    rank = jnp.dot(
        ones.astype(jnp.bfloat16), before.astype(jnp.bfloat16), preferred_element_type=jnp.float32
    )
    rank = jnp.where(chosen, rank, -1.0)
    tile = (ids % per_chip).astype(jnp.float32)
    wanted = jnp.where(lane == slots, jnp.sum(ones, axis=1, keepdims=True), 0.0)
    for s in range(slots):
        found = jnp.sum(jnp.where(rank == float(s), tile, 0.0), axis=1, keepdims=True)
        wanted = jnp.where(lane == s, found, wanted)
    block[query_rows:, :] = wanted.astype(jnp.bfloat16)


def fact_rows_of(chips):
    return -(-chips // 16) * 16


def pack(queries, candidates, per_owner, chips, slots):
    rows, feature = queries.shape
    return pl.pallas_call(
        functools.partial(pack_kernel, per_owner, chips, slots),
        out_shape=jax.ShapeDtypeStruct((rows + fact_rows_of(chips), feature), queries.dtype),
        in_specs=[pl.BlockSpec(memory_space=pl.ANY)] * 2,
        out_specs=pl.BlockSpec(memory_space=pltpu.VMEM),
        scratch_shapes=[
            pltpu.VMEM(queries.shape, queries.dtype),
            pltpu.VMEM(candidates.shape, candidates.dtype),
            pltpu.SemaphoreType.DMA((2,)),
        ],
        compiler_params=pltpu.CompilerParams(vmem_limit_bytes=56 * 1024 * 1024),
        name="pack",
    )(queries, candidates)


def fill_tiles(source, lens, filled, filled_at, first, number):
    row = lax.broadcasted_iota(jnp.int32, source.shape[1:], 0)

    def some(i, carry):
        for k in range(4):
            at = first + 4 * i + k
            tile = source[at].astype(jnp.float32)
            tile = jnp.where(row < lens[at], tile, tile[0:1, :])
            filled[filled_at + at] = tile.astype(jnp.bfloat16)
        return carry

    lax.fori_loop(0, number // 4, some, 0)


def ready_kernel(chips, slots, parts, lens, candidates, passages, slot_of, filled, sems):
    per_owner = passages.shape[0]
    size = per_owner // parts
    loads = [
        pltpu.make_async_copy(
            passages.at[pl.ds(i * size, size)], filled.at[pl.ds(i * size, size)], sems.at[i]
        )
        for i in range(parts)
    ]
    for load in loads:
        load.start()
    number = candidates.shape[1]
    my_place = ring_place(lax.axis_index("corpus") // CORES, chips)
    wide = jnp.broadcast_to(candidates[...], (number, number)) // (CORES * per_owner)
    tall = wide.astype(jnp.float32).T.astype(jnp.int32)
    row = lax.broadcasted_iota(jnp.int32, (number, number), 0)
    lane = lax.broadcasted_iota(jnp.int32, (number, number), 1)
    earlier = jnp.where((wide == tall) & (lane < row), 1.0, 0.0)
    rank = jnp.sum(earlier, axis=1, keepdims=True).astype(jnp.int32)
    ahead = ring_place(tall, chips) - my_place
    ahead = jnp.where(ahead < 0, ahead + chips, ahead)
    slot_of[...] = ahead * slots + rank
    for i, load in enumerate(loads):
        load.wait()
        fill_tiles(filled, lens, filled, 0, i * size, size)


def ready(lengths, candidates, passages, chips, slots):
    number = candidates.shape[1]
    per_owner = passages.shape[0]
    parts = 4 if per_owner % 16 == 0 else 1
    return pl.pallas_call(
        functools.partial(ready_kernel, chips, slots, parts),
        out_shape=(
            jax.ShapeDtypeStruct((number, number), jnp.int32),
            jax.ShapeDtypeStruct(passages.shape, passages.dtype),
        ),
        in_specs=[
            pl.BlockSpec(memory_space=pltpu.SMEM),
            pl.BlockSpec(memory_space=pltpu.VMEM),
            pl.BlockSpec(memory_space=pl.ANY),
        ],
        out_specs=(pl.BlockSpec(memory_space=pltpu.VMEM),) * 2,
        scratch_shapes=[pltpu.SemaphoreType.DMA((parts,))],
        compiler_params=pltpu.CompilerParams(vmem_limit_bytes=VMEM_LIMIT),
        name="ready",
    )(lengths, candidates, passages)


def join_kernel(lens, other, own, filled, sem):
    per_owner = other.shape[0]
    core = lax.axis_index("corpus") % CORES
    keep = pltpu.make_async_copy(own, filled.at[pl.ds(core * per_owner, per_owner)], sem)
    keep.start()
    fill_tiles(other, lens, filled, (1 - core) * per_owner, 0, per_owner)
    keep.wait()


def join(lengths, other, own):
    return pl.pallas_call(
        join_kernel,
        out_shape=jax.ShapeDtypeStruct((CORES * own.shape[0],) + own.shape[1:], own.dtype),
        in_specs=[
            pl.BlockSpec(memory_space=pltpu.SMEM),
            pl.BlockSpec(memory_space=pltpu.VMEM),
            pl.BlockSpec(memory_space=pltpu.VMEM),
        ],
        out_specs=pl.BlockSpec(memory_space=pltpu.VMEM),
        scratch_shapes=[pltpu.SemaphoreType.DMA],
        compiler_params=pltpu.CompilerParams(vmem_limit_bytes=VMEM_LIMIT),
        name="join",
    )(lengths, other, own)


def lane_step(chunks, query_tok):
    return query_tok // pl.next_power_of_2(chunks)


def token_sums(parts, query_tok):
    lane = lax.broadcasted_iota(jnp.int32, parts[0].shape, 1)
    parts = list(parts)
    parts += [None] * (pl.next_power_of_2(len(parts)) - len(parts))
    shift = query_tok // 2
    while shift >= 1:
        low = (lane & shift) == 0
        half = max(1, len(parts) // 2)
        merged = []
        for k in range(half):
            a = parts[k]
            b = parts[k + half] if len(parts) > 1 else None
            if a is None:
                merged.append(None)
                continue
            x = a + pltpu.roll(a, LANES - shift, 1)
            if b is not None:
                x = jnp.where(low, x, b + pltpu.roll(b, shift, 1))
            merged.append(x)
        parts = merged
        shift //= 2
    return parts[0]


def score_kernel(pieces, slots, query_tok, chips, *refs):
    blocks = len(pieces)
    arrays = sum(pieces)
    tiles = refs[0]
    held = refs[1 : 1 + arrays]
    outs = refs[1 + arrays : 1 + arrays + blocks]
    weights, nearest, plan_v, plan, sem, weight_sems = refs[1 + arrays + blocks :]
    tile_rows = tiles.shape[1]
    my_place = ring_place(lax.axis_index("corpus") // CORES, chips)
    fact_rows = fact_rows_of(chips)

    loads = []
    fact_row = lax.broadcasted_iota(jnp.int32, (fact_rows, LANES), 0)
    at = 0
    for b, count in enumerate(pieces):
        row = 0
        for ref in held[at : at + count]:
            rows = min(ref.shape[0], weights.shape[1] - row)
            loads.append(
                pltpu.make_async_copy(
                    ref.at[pl.ds(0, rows)], weights.at[b, pl.ds(row, rows)], weight_sems.at[len(loads)]
                )
            )
            row += rows
        fact = ref[rows : rows + fact_rows, :].astype(jnp.float32)
        fact = jnp.sum(jnp.where(fact_row == my_place, fact, 0.0), axis=0, keepdims=True)
        plan_v[b : b + 1, :] = fact.astype(jnp.int32)
        at += count
    to_scalar = pltpu.make_async_copy(plan_v, plan, sem)
    to_scalar.start()
    for load in loads:
        load.start()
    to_scalar.wait()
    for load in loads:
        load.wait()

    slot_row = lax.broadcasted_iota(jnp.int32, (slots, LANES), 0)

    def score_block(b, carry):
        count = plan[b, slots]

        def score_tiles(first, number):
            left = jnp.concatenate([tiles[plan[b, first + t]] for t in range(number)], axis=0)
            start = pl.multiple_of(first * 8, 8 * number)
            for c in range(0, nearest.shape[0], 2):
                pair = [weights[b, k * LANES : (k + 1) * LANES, :] for k in (c, c + 1)]
                similar = jnp.dot(
                    left, jnp.concatenate(pair, axis=1), preferred_element_type=jnp.float32
                )
                best = jnp.max(similar.reshape(number, tile_rows // 8, 8, 2 * LANES), axis=1)
                best = best.reshape(number * 8, 2 * LANES)
                for k in range(2):
                    nearest[c + k, pl.ds(start, number * 8), :] = best[:, k * LANES : (k + 1) * LANES]

        whole = count // GROUP
        rest = count - whole * GROUP
        small = (rest > 0) & (rest <= GROUP // 2)
        turns = pl.cdiv(count, GROUP) - small.astype(jnp.int32)

        def turn(g, carry):
            score_tiles(pl.multiple_of(g * GROUP, GROUP), GROUP)
            return carry

        lax.fori_loop(0, turns, turn, 0)
        pl.when(small)(lambda: score_tiles(pl.multiple_of(whole * GROUP, GROUP), GROUP // 2))

        parts = []
        for k in range(nearest.shape[0]):
            x = nearest[k, pl.ds(0, slots, stride=8), :]
            for sublane in range(1, 8):
                x = jnp.maximum(x, nearest[k, pl.ds(sublane, slots, stride=8), :])
            parts.append(x)
        total = token_sums(parts, query_tok)
        total = jnp.where(slot_row < count, total / float(query_tok), 0.0)
        for k in range(blocks):

            @pl.when(b == k)
            def _(k=k):
                outs[k][...] = total

        return carry

    lax.fori_loop(0, blocks, score_block, 0)


def score(held, slots, query_tok, chips, tiles):
    pieces = tuple(len(arrays) for arrays in held)
    flat = [x for arrays in held for x in arrays]
    blocks = len(pieces)
    _, tile_rows, feature = tiles.shape
    query_rows = sum(x.shape[0] for x in held[0]) - fact_rows_of(chips)
    flops = 2 * blocks * slots * tile_rows * feature * query_rows
    return pl.pallas_call(
        functools.partial(score_kernel, pieces, slots, query_tok, chips),
        out_shape=(jax.ShapeDtypeStruct((slots, LANES), jnp.float32),) * blocks,
        in_specs=[pl.BlockSpec(memory_space=pltpu.VMEM)] * (1 + len(flat)),
        out_specs=(pl.BlockSpec(memory_space=pltpu.VMEM),) * blocks,
        scratch_shapes=[
            pltpu.VMEM((blocks, query_rows, feature), tiles.dtype),
            pltpu.VMEM((query_rows // LANES, 8 * slots, LANES), jnp.float32),
            pltpu.VMEM((8, LANES), jnp.int32),
            pltpu.SMEM((8, LANES), jnp.int32),
            pltpu.SemaphoreType.DMA,
            pltpu.SemaphoreType.DMA((len(flat),)),
        ],
        compiler_params=pltpu.CompilerParams(vmem_limit_bytes=VMEM_LIMIT),
        cost_estimate=pl.CostEstimate(
            flops=3 * flops,
            bytes_accessed=blocks * (slots * tile_rows + query_rows) * feature * 2,
            transcendentals=0,
        ),
        name="score",
    )(tiles, *flat)


def sort_descending(parts, lanes):
    parts = list(parts)
    many = len(parts)
    number = many * 8
    sub = lax.broadcasted_iota(jnp.int32, (8, lanes), 0)
    size = 2
    while size <= number:
        reach = size // 2
        while reach >= 1:
            if reach < many:
                for v in range(many):
                    if v & reach:
                        continue
                    a, b = parts[v], parts[v | reach]
                    high, low = jnp.maximum(a, b), jnp.minimum(a, b)
                    if size >= number:
                        parts[v], parts[v | reach] = high, low
                    elif size < many:
                        down = (v & size) == 0
                        parts[v], parts[v | reach] = (high, low) if down else (low, high)
                    else:
                        down = (sub & (size // many)) == 0
                        parts[v] = jnp.where(down, high, low)
                        parts[v | reach] = jnp.where(down, low, high)
            else:
                step = reach // many
                is_first = (sub & step) == 0
                if size >= number:
                    keep_high = is_first
                else:
                    keep_high = is_first == ((sub & (size // many)) == 0)
                for v in range(many):
                    x = parts[v]
                    partner = jnp.where(is_first, pltpu.roll(x, 8 - step, 0), pltpu.roll(x, step, 0))
                    parts[v] = jnp.where(keep_high, jnp.maximum(x, partner), jnp.minimum(x, partner))
            reach //= 2
        size *= 2
    return parts


def finish_kernel(arrays, per_device, query_tok, topk, slot_of, *refs):
    returned = refs[:arrays]
    scores, best_scores, spread, ranked, rows, turned = refs[arrays:]
    number = slot_of.shape[0]
    step = returned[0].shape[0]
    for at, ref in enumerate(returned):
        spread[at * step : (at + 1) * step, :] = ref[...]
    total = spread.shape[0]
    lane = lax.broadcasted_iota(jnp.int32, (number, total), 1)
    choose = (slot_of[:, 0:1] == lane).astype(jnp.float32).astype(jnp.bfloat16)
    by_candidate = jnp.zeros((number, LANES), jnp.float32)
    for part in split_exact(spread[...]):
        by_candidate += jnp.dot(choose, part, preferred_element_type=jnp.float32)

    each = LANES // query_tok
    step = lane_step(-(-per_device // each), query_tok)
    many_rows = query_tok // step

    def in_order(x):
        turned[...] = x.T
        for m in range(each):
            rows[pl.ds(m, many_rows, stride=each), :] = turned[
                pl.ds(m * query_tok, many_rows, stride=step), :
            ]
        return rows[...]

    scores[...] = in_order(by_candidate)[:per_device, :]
    many = number // 8
    parts = sort_descending([by_candidate[8 * v : 8 * v + 8, :] for v in range(many)], LANES)
    for v in range(many):
        ranked[pl.ds(v, 8, stride=many), :] = parts[v]
    best_scores[...] = in_order(ranked[...])[:per_device, :topk]


def finish(per_device, query_tok, slot_of, returned):
    number = slot_of.shape[0]
    total = sum(r.shape[0] for r in returned)
    return pl.pallas_call(
        functools.partial(finish_kernel, len(returned), per_device, query_tok, TOPK),
        out_shape=(
            jax.ShapeDtypeStruct((per_device, number), jnp.float32),
            jax.ShapeDtypeStruct((per_device, TOPK), jnp.float32),
        ),
        in_specs=[pl.BlockSpec(memory_space=pltpu.VMEM)] * (1 + len(returned)),
        out_specs=(pl.BlockSpec(memory_space=pltpu.VMEM),) * 2,
        scratch_shapes=[
            pltpu.VMEM((total, LANES), jnp.float32),
            pltpu.VMEM((number, LANES), jnp.float32),
            pltpu.VMEM((LANES, number), jnp.float32),
            pltpu.VMEM((LANES, number), jnp.float32),
        ],
        compiler_params=pltpu.CompilerParams(vmem_limit_bytes=VMEM_LIMIT),
        name="finish",
    )(slot_of, *returned)


def local(queries, passages, lengths, candidates):
    peers = lax.axis_size("corpus")
    chips = peers // CORES
    per_owner, tile_rows, feature = passages.shape
    per_device, query_tok = queries.shape[0], queries.shape[1]
    number = candidates.shape[1]
    capacity = max(2, 3 * number // (2 * peers))
    slots = -(-CORES * capacity // 8) * 8
    order = ring_order(chips)

    def moved(x, distance):
        pairs = [
            (order[i] * CORES + core, order[(i + distance) % chips] * CORES + core)
            for i in range(chips)
            for core in range(CORES)
        ]
        return lax.ppermute(x, "corpus", pairs)

    swap = [(i, i ^ 1) for i in range(peers)]
    other = lax.ppermute(passages, "corpus", swap)
    other_lengths = lax.ppermute(lengths, "corpus", swap)
    slot_of, own = ready(lengths, candidates, passages, chips, slots)
    tiles = join(other_lengths, other, own)

    block = pack(
        queries.reshape(per_device * query_tok, feature), candidates, per_owner, chips, slots
    )
    half = per_device * query_tok // LANES // 2 * LANES
    middle = chips // 2
    arrived = {0: [block]}

    def send_on(step):
        if step < middle:
            arrived[step] = [moved(x, 1) for x in arrived[step - 1]]
            arrived[-step] = [moved(x, -1) for x in arrived[1 - step]]
        else:
            arrived[step] = [
                moved(arrived[step - 1][0][:half], 1), moved(arrived[1 - step][0][half:], -1)
            ]

    send_on(1)
    back = {}
    for step in range(middle + 1):
        if 0 < step < middle:
            send_on(step + 1)
        offsets = (step,) if step in (0, middle) else (step, -step)
        fresh = score([arrived[offset] for offset in offsets], slots, query_tok, chips, tiles)
        for offset, result in zip(offsets, fresh):
            back[offset % chips] = moved(result, -offset) if offset else result
        names = [] if step == middle else [step + 1, -step - 1] if step + 1 < middle else [middle]
        earlier = [1, -1] if step == 1 else [step - 1, 1 - step] if 2 < step < middle else []
        earlier = [offset % chips for offset in earlier]
        held, came, _ = lax.optimization_barrier(
            ([arrived[name] for name in names], [back[j] for j in earlier], fresh)
        )
        arrived.update(zip(names, held))
        back.update(zip(earlier, came))
    return finish(per_device, query_tok, slot_of, [back[j] for j in range(chips)])


def solution(mesh):
    return jax.shard_map(
        local,
        mesh=mesh,
        in_specs=(
            P(("groups", "corpus"), None, None),
            P(("groups", "corpus"), None, None),
            P(("groups", "corpus")),
            P(("groups", "corpus"), None),
        ),
        out_specs=(P(("groups", "corpus"), None), P(("groups", "corpus"), None)),
        check_vma=False,
    )
```

```python
import functools

import jax
import jax.numpy as jnp
from jax import lax
from jax.experimental import pallas as pl
from jax.experimental.pallas import tpu as pltpu
from jax.sharding import PartitionSpec as P

TOPK = 100
CORES = 2
LANES = 128
GROUP = 8
VMEM_LIMIT = 32 * 1024 * 1024
READY_LIMIT = 48 * 1024 * 1024


def ring_order(chips):
    return list(range(0, chips, 2)) + list(range(1, chips, 2))[::-1]


def ring_place(chip, chips):
    return jnp.where(chip % 2 == 0, chip // 2, chips - (chip + 1) // 2)


def split_exact(x):
    high = x.astype(jnp.bfloat16)
    rest = x - high.astype(jnp.float32)
    middle = rest.astype(jnp.bfloat16)
    low = (rest - middle.astype(jnp.float32)).astype(jnp.bfloat16)
    return high, middle, low


def pack_kernel(per_owner, chips, slots, queries_in, candidates_in, out, queries, candidates, block, in_sems, out_sems):
    query_rows = queries.shape[0]
    half = query_rows // LANES // 2 * LANES
    spans = [(0, half), (half, query_rows - half)]
    listed = pltpu.make_async_copy(candidates_in, candidates, in_sems.at[2])
    listed.start()
    loads = [
        pltpu.make_async_copy(
            queries_in.at[pl.ds(at, rows)], queries.at[pl.ds(at, rows)], in_sems.at[i]
        )
        for i, (at, rows) in enumerate(spans)
    ]
    for load in loads:
        load.start()
    listed.wait()
    fact_rows = block.shape[0] - query_rows
    number = candidates.shape[1]
    per_chip = CORES * per_owner
    ids = jnp.broadcast_to(candidates[...], (fact_rows, number))
    row = lax.broadcasted_iota(jnp.int32, ids.shape, 0)
    lane = lax.broadcasted_iota(jnp.int32, ids.shape, 1)
    chosen = ring_place(ids // per_chip, chips) == row
    ones = jnp.where(chosen, 1.0, 0.0)
    before = jnp.where(
        lax.broadcasted_iota(jnp.int32, (number, number), 0)
        < lax.broadcasted_iota(jnp.int32, (number, number), 1), 1.0, 0.0,
    )
    rank = jnp.dot(
        ones.astype(jnp.bfloat16), before.astype(jnp.bfloat16), preferred_element_type=jnp.float32
    )
    rank = jnp.where(chosen, rank, -1.0)
    tile = (ids % per_chip).astype(jnp.float32)
    wanted = jnp.where(lane == slots, jnp.sum(ones, axis=1, keepdims=True), 0.0)
    for s in range(slots):
        found = jnp.sum(jnp.where(rank == float(s), tile, 0.0), axis=1, keepdims=True)
        wanted = jnp.where(lane == s, found, wanted)
    block[query_rows:, :] = wanted.astype(jnp.bfloat16)
    stores = []
    for i, (at, rows) in enumerate(spans):
        loads[i].wait()
        for row_at in range(at, at + rows, LANES):
            block[row_at : row_at + LANES, :] = queries[row_at : row_at + LANES, :].T
        if i:
            rows += fact_rows
        stores.append(
            pltpu.make_async_copy(block.at[pl.ds(at, rows)], out.at[pl.ds(at, rows)], out_sems.at[i])
        )
        stores[-1].start()
    for store in stores:
        store.wait()


def fact_rows_of(chips):
    return -(-chips // 16) * 16


def pack(queries, candidates, per_owner, chips, slots):
    rows, feature = queries.shape
    return pl.pallas_call(
        functools.partial(pack_kernel, per_owner, chips, slots),
        out_shape=jax.ShapeDtypeStruct((rows + fact_rows_of(chips), feature), queries.dtype),
        in_specs=[pl.BlockSpec(memory_space=pl.ANY)] * 2,
        out_specs=pl.BlockSpec(memory_space=pl.ANY),
        scratch_shapes=[
            pltpu.VMEM(queries.shape, queries.dtype),
            pltpu.VMEM(candidates.shape, candidates.dtype),
            pltpu.VMEM((rows + fact_rows_of(chips), feature), queries.dtype),
            pltpu.SemaphoreType.DMA((3,)),
            pltpu.SemaphoreType.DMA((2,)),
        ],
        compiler_params=pltpu.CompilerParams(vmem_limit_bytes=56 * 1024 * 1024),
        name="pack",
    )(queries, candidates)


def fill_tiles(source, lens, filled, filled_at, first, number):
    row = lax.broadcasted_iota(jnp.int32, source.shape[1:], 0)

    def some(i, carry):
        for k in range(4):
            at = first + 4 * i + k
            tile = source[at].astype(jnp.float32)
            tile = jnp.where(row < lens[at], tile, tile[0:1, :])
            filled[filled_at + at] = tile.astype(jnp.bfloat16)
        return carry

    lax.fori_loop(0, number // 4, some, 0)


def ready_kernel(chips, slots, parts, lens, candidates, passages, slot_of, filled, sems):
    per_owner = passages.shape[0]
    size = per_owner // parts
    loads = [
        pltpu.make_async_copy(
            passages.at[pl.ds(i * size, size)], filled.at[pl.ds(i * size, size)], sems.at[i]
        )
        for i in range(parts)
    ]
    for load in loads:
        load.start()
    number = candidates.shape[1]
    my_place = ring_place(lax.axis_index("corpus") // CORES, chips)
    wide = jnp.broadcast_to(candidates[...], (number, number)) // (CORES * per_owner)
    tall = wide.astype(jnp.float32).T.astype(jnp.int32)
    row = lax.broadcasted_iota(jnp.int32, (number, number), 0)
    lane = lax.broadcasted_iota(jnp.int32, (number, number), 1)
    earlier = jnp.where((wide == tall) & (lane < row), 1.0, 0.0)
    rank = jnp.sum(earlier, axis=1, keepdims=True).astype(jnp.int32)
    ahead = ring_place(tall, chips) - my_place
    ahead = jnp.where(ahead < 0, ahead + chips, ahead)
    slot_of[...] = ahead * slots + rank
    for i, load in enumerate(loads):
        load.wait()
        fill_tiles(filled, lens, filled, 0, i * size, size)


def ready(lengths, candidates, passages, chips, slots):
    number = candidates.shape[1]
    per_owner = passages.shape[0]
    parts = 4 if per_owner % 16 == 0 else 1
    return pl.pallas_call(
        functools.partial(ready_kernel, chips, slots, parts),
        out_shape=(
            jax.ShapeDtypeStruct((number, number), jnp.int32),
            jax.ShapeDtypeStruct(passages.shape, passages.dtype),
        ),
        in_specs=[
            pl.BlockSpec(memory_space=pltpu.SMEM),
            pl.BlockSpec(memory_space=pltpu.VMEM),
            pl.BlockSpec(memory_space=pl.ANY),
        ],
        out_specs=(pl.BlockSpec(memory_space=pltpu.VMEM),) * 2,
        scratch_shapes=[pltpu.SemaphoreType.DMA((parts,))],
        compiler_params=pltpu.CompilerParams(vmem_limit_bytes=READY_LIMIT),
        name="ready",
    )(lengths, candidates, passages)


def join_kernel(lens, other, own, filled, sem):
    per_owner = other.shape[0]
    core = lax.axis_index("corpus") % CORES
    keep = pltpu.make_async_copy(own, filled.at[pl.ds(core * per_owner, per_owner)], sem)
    keep.start()
    fill_tiles(other, lens, filled, (1 - core) * per_owner, 0, per_owner)
    keep.wait()


def join(lengths, other, own):
    return pl.pallas_call(
        join_kernel,
        out_shape=jax.ShapeDtypeStruct((CORES * own.shape[0],) + own.shape[1:], own.dtype),
        in_specs=[
            pl.BlockSpec(memory_space=pltpu.SMEM),
            pl.BlockSpec(memory_space=pltpu.VMEM),
            pl.BlockSpec(memory_space=pltpu.VMEM),
        ],
        out_specs=pl.BlockSpec(memory_space=pltpu.VMEM),
        scratch_shapes=[pltpu.SemaphoreType.DMA],
        compiler_params=pltpu.CompilerParams(vmem_limit_bytes=VMEM_LIMIT),
        name="join",
    )(lengths, other, own)


def lane_step(chunks, query_tok):
    return query_tok // pl.next_power_of_2(chunks)


def token_sums(parts, query_tok):
    lane = lax.broadcasted_iota(jnp.int32, parts[0].shape, 1)
    parts = list(parts)
    parts += [None] * (pl.next_power_of_2(len(parts)) - len(parts))
    shift = query_tok // 2
    while shift >= 1:
        low = (lane & shift) == 0
        half = max(1, len(parts) // 2)
        merged = []
        for k in range(half):
            a = parts[k]
            b = parts[k + half] if len(parts) > 1 else None
            if a is None:
                merged.append(None)
                continue
            x = a + pltpu.roll(a, LANES - shift, 1)
            if b is not None:
                x = jnp.where(low, x, b + pltpu.roll(b, shift, 1))
            merged.append(x)
        parts = merged
        shift //= 2
    return parts[0]


def score_kernel(pieces, slots, query_tok, chips, *refs):
    blocks = len(pieces)
    arrays = sum(pieces)
    tiles = refs[0]
    held = refs[1 : 1 + arrays]
    outs = refs[1 + arrays : 1 + arrays + blocks]
    weights, nearest, plan_v, plan, sem, weight_sems = refs[1 + arrays + blocks :]
    tile_rows = tiles.shape[1]
    my_place = ring_place(lax.axis_index("corpus") // CORES, chips)
    fact_rows = fact_rows_of(chips)

    loads = []
    fact_row = lax.broadcasted_iota(jnp.int32, (fact_rows, LANES), 0)
    at = 0
    for b, count in enumerate(pieces):
        row = 0
        for ref in held[at : at + count]:
            rows = min(ref.shape[0], weights.shape[1] - row)
            loads.append(
                pltpu.make_async_copy(
                    ref.at[pl.ds(0, rows)], weights.at[b, pl.ds(row, rows)], weight_sems.at[len(loads)]
                )
            )
            row += rows
        fact = ref[rows : rows + fact_rows, :].astype(jnp.float32)
        fact = jnp.sum(jnp.where(fact_row == my_place, fact, 0.0), axis=0, keepdims=True)
        plan_v[b : b + 1, :] = fact.astype(jnp.int32)
        at += count
    to_scalar = pltpu.make_async_copy(plan_v, plan, sem)
    to_scalar.start()
    for load in loads:
        load.start()
    to_scalar.wait()

    slot_row = lax.broadcasted_iota(jnp.int32, (slots, LANES), 0)

    def score_block(b, carry):
        count = plan[b, slots]
        for k in range(blocks):

            @pl.when(b == k)
            def _(k=k):
                for load in loads[sum(pieces[:k]) : sum(pieces[: k + 1])]:
                    load.wait()

        def score_tiles(first, number):
            left = jnp.concatenate([tiles[plan[b, first + t]] for t in range(number)], axis=0)
            start = pl.multiple_of(first * 8, 8 * number)
            for c in range(0, nearest.shape[0], 2):
                pair = [weights[b, k * LANES : (k + 1) * LANES, :] for k in (c, c + 1)]
                similar = jnp.dot(
                    left, jnp.concatenate(pair, axis=1), preferred_element_type=jnp.float32
                )
                best = jnp.max(similar.reshape(number, tile_rows // 8, 8, 2 * LANES), axis=1)
                best = best.reshape(number * 8, 2 * LANES)
                for k in range(2):
                    nearest[c + k, pl.ds(start, number * 8), :] = best[:, k * LANES : (k + 1) * LANES]

        whole = count // GROUP
        rest = count - whole * GROUP
        small = (rest > 0) & (rest <= GROUP // 2)
        turns = pl.cdiv(count, GROUP) - small.astype(jnp.int32)

        def turn(g, carry):
            score_tiles(pl.multiple_of(g * GROUP, GROUP), GROUP)
            return carry

        lax.fori_loop(0, turns, turn, 0)
        pl.when(small)(lambda: score_tiles(pl.multiple_of(whole * GROUP, GROUP), GROUP // 2))

        parts = []
        for k in range(nearest.shape[0]):
            x = nearest[k, pl.ds(0, slots, stride=8), :]
            for sublane in range(1, 8):
                x = jnp.maximum(x, nearest[k, pl.ds(sublane, slots, stride=8), :])
            parts.append(x)
        total = token_sums(parts, query_tok)
        total = jnp.where(slot_row < count, total / float(query_tok), 0.0)
        for k in range(blocks):

            @pl.when(b == k)
            def _(k=k):
                outs[k][...] = total

        return carry

    lax.fori_loop(0, blocks, score_block, 0)


def score(held, slots, query_tok, chips, tiles):
    pieces = tuple(len(arrays) for arrays in held)
    flat = [x for arrays in held for x in arrays]
    blocks = len(pieces)
    _, tile_rows, feature = tiles.shape
    query_rows = sum(x.shape[0] for x in held[0]) - fact_rows_of(chips)
    flops = 2 * blocks * slots * tile_rows * feature * query_rows
    return pl.pallas_call(
        functools.partial(score_kernel, pieces, slots, query_tok, chips),
        out_shape=(jax.ShapeDtypeStruct((slots, LANES), jnp.float32),) * blocks,
        in_specs=[pl.BlockSpec(memory_space=pltpu.VMEM)] * (1 + len(flat)),
        out_specs=(pl.BlockSpec(memory_space=pltpu.VMEM),) * blocks,
        scratch_shapes=[
            pltpu.VMEM((blocks, query_rows, feature), tiles.dtype),
            pltpu.VMEM((query_rows // LANES, 8 * slots, LANES), jnp.float32),
            pltpu.VMEM((8, LANES), jnp.int32),
            pltpu.SMEM((8, LANES), jnp.int32),
            pltpu.SemaphoreType.DMA,
            pltpu.SemaphoreType.DMA((len(flat),)),
        ],
        compiler_params=pltpu.CompilerParams(vmem_limit_bytes=VMEM_LIMIT),
        cost_estimate=pl.CostEstimate(
            flops=3 * flops,
            bytes_accessed=blocks * (slots * tile_rows + query_rows) * feature * 2,
            transcendentals=0,
        ),
        name="score",
    )(tiles, *flat)


def sort_descending(parts, lanes):
    parts = list(parts)
    many = len(parts)
    number = many * 8
    sub = lax.broadcasted_iota(jnp.int32, (8, lanes), 0)
    size = 2
    while size <= number:
        reach = size // 2
        while reach >= 1:
            if reach < many:
                for v in range(many):
                    if v & reach:
                        continue
                    a, b = parts[v], parts[v | reach]
                    high, low = jnp.maximum(a, b), jnp.minimum(a, b)
                    if size >= number:
                        parts[v], parts[v | reach] = high, low
                    elif size < many:
                        down = (v & size) == 0
                        parts[v], parts[v | reach] = (high, low) if down else (low, high)
                    else:
                        down = (sub & (size // many)) == 0
                        parts[v] = jnp.where(down, high, low)
                        parts[v | reach] = jnp.where(down, low, high)
            else:
                step = reach // many
                is_first = (sub & step) == 0
                if size >= number:
                    keep_high = is_first
                else:
                    keep_high = is_first == ((sub & (size // many)) == 0)
                for v in range(many):
                    x = parts[v]
                    partner = jnp.where(is_first, pltpu.roll(x, 8 - step, 0), pltpu.roll(x, step, 0))
                    parts[v] = jnp.where(keep_high, jnp.maximum(x, partner), jnp.minimum(x, partner))
            reach //= 2
        size *= 2
    return parts


def finish_kernel(arrays, per_device, query_tok, topk, slot_of, *refs):
    returned = refs[:arrays]
    scores, best_scores, spread, ranked, rows, turned = refs[arrays:]
    number = slot_of.shape[0]
    step = returned[0].shape[0]
    for at, ref in enumerate(returned):
        spread[at * step : (at + 1) * step, :] = ref[...]
    total = spread.shape[0]
    lane = lax.broadcasted_iota(jnp.int32, (number, total), 1)
    choose = (slot_of[:, 0:1] == lane).astype(jnp.float32).astype(jnp.bfloat16)
    by_candidate = jnp.zeros((number, LANES), jnp.float32)
    for part in split_exact(spread[...]):
        by_candidate += jnp.dot(choose, part, preferred_element_type=jnp.float32)

    each = LANES // query_tok
    step = lane_step(-(-per_device // each), query_tok)
    many_rows = query_tok // step

    def in_order(x):
        turned[...] = x.T
        for m in range(each):
            rows[pl.ds(m, many_rows, stride=each), :] = turned[
                pl.ds(m * query_tok, many_rows, stride=step), :
            ]
        return rows[...]

    scores[...] = in_order(by_candidate)[:per_device, :]
    many = number // 8
    parts = sort_descending([by_candidate[8 * v : 8 * v + 8, :] for v in range(many)], LANES)
    for v in range(many):
        ranked[pl.ds(v, 8, stride=many), :] = parts[v]
    best_scores[...] = in_order(ranked[...])[:per_device, :topk]


def finish(per_device, query_tok, slot_of, returned):
    number = slot_of.shape[0]
    total = sum(r.shape[0] for r in returned)
    return pl.pallas_call(
        functools.partial(finish_kernel, len(returned), per_device, query_tok, TOPK),
        out_shape=(
            jax.ShapeDtypeStruct((per_device, number), jnp.float32),
            jax.ShapeDtypeStruct((per_device, TOPK), jnp.float32),
        ),
        in_specs=[pl.BlockSpec(memory_space=pltpu.VMEM)] * (1 + len(returned)),
        out_specs=(pl.BlockSpec(memory_space=pltpu.VMEM),) * 2,
        scratch_shapes=[
            pltpu.VMEM((total, LANES), jnp.float32),
            pltpu.VMEM((number, LANES), jnp.float32),
            pltpu.VMEM((LANES, number), jnp.float32),
            pltpu.VMEM((LANES, number), jnp.float32),
        ],
        compiler_params=pltpu.CompilerParams(vmem_limit_bytes=VMEM_LIMIT),
        name="finish",
    )(slot_of, *returned)


def local(queries, passages, lengths, candidates):
    peers = lax.axis_size("corpus")
    chips = peers // CORES
    per_owner, tile_rows, feature = passages.shape
    per_device, query_tok = queries.shape[0], queries.shape[1]
    number = candidates.shape[1]
    capacity = max(2, 3 * number // (2 * peers))
    slots = -(-CORES * capacity // 8) * 8
    order = ring_order(chips)

    def moved(x, distance):
        pairs = [
            (order[i] * CORES + core, order[(i + distance) % chips] * CORES + core)
            for i in range(chips)
            for core in range(CORES)
        ]
        return lax.ppermute(x, "corpus", pairs)

    swap = [(i, i ^ 1) for i in range(peers)]
    other = lax.ppermute(passages, "corpus", swap)
    other_lengths = lax.ppermute(lengths, "corpus", swap)
    slot_of, own = ready(lengths, candidates, passages, chips, slots)
    tiles = join(other_lengths, other, own)

    block = pack(
        queries.reshape(per_device * query_tok, feature), candidates, per_owner, chips, slots
    )
    half = per_device * query_tok // LANES // 2 * LANES
    middle = chips // 2
    arrived = {0: [block]}

    def send_on(step):
        if step < middle:
            arrived[step] = [moved(x, 1) for x in arrived[step - 1]]
            arrived[-step] = [moved(x, -1) for x in arrived[1 - step]]
        else:
            arrived[step] = [
                moved(arrived[step - 1][0][:half], 1), moved(arrived[1 - step][0][half:], -1)
            ]

    send_on(1)
    back = {}
    for step in range(middle + 1):
        if 0 < step < middle:
            send_on(step + 1)
        offsets = (step,) if step in (0, middle) else (step, -step)
        fresh = score([arrived[offset] for offset in offsets], slots, query_tok, chips, tiles)
        for offset, result in zip(offsets, fresh):
            back[offset % chips] = moved(result, -offset) if offset else result
        names = [] if step == middle else [step + 1, -step - 1] if step + 1 < middle else [middle]
        earlier = [1, -1] if step == 1 else [step - 1, 1 - step] if 2 < step < middle else []
        earlier = [offset % chips for offset in earlier]
        held, came, _ = lax.optimization_barrier(
            ([arrived[name] for name in names], [back[j] for j in earlier], fresh)
        )
        arrived.update(zip(names, held))
        back.update(zip(earlier, came))
    return finish(per_device, query_tok, slot_of, [back[j] for j in range(chips)])


def solution(mesh):
    return jax.shard_map(
        local,
        mesh=mesh,
        in_specs=(
            P(("groups", "corpus"), None, None),
            P(("groups", "corpus"), None, None),
            P(("groups", "corpus")),
            P(("groups", "corpus"), None),
        ),
        out_specs=(P(("groups", "corpus"), None), P(("groups", "corpus"), None)),
        check_vma=False,
    )
```

```python
import functools

import jax
import jax.numpy as jnp
from jax import lax
from jax.experimental import pallas as pl
from jax.experimental.pallas import tpu as pltpu
from jax.sharding import PartitionSpec as P

TOPK = 100
CORES = 2
LANES = 128
GROUP = 8
VMEM_LIMIT = 32 * 1024 * 1024
READY_LIMIT = 48 * 1024 * 1024


def ring_order(chips):
    return list(range(0, chips, 2)) + list(range(1, chips, 2))[::-1]


def ring_place(chip, chips):
    return jnp.where(chip % 2 == 0, chip // 2, chips - (chip + 1) // 2)


def split_exact(x):
    high = x.astype(jnp.bfloat16)
    rest = x - high.astype(jnp.float32)
    middle = rest.astype(jnp.bfloat16)
    low = (rest - middle.astype(jnp.float32)).astype(jnp.bfloat16)
    return high, middle, low


def pack_kernel(per_owner, chips, slots, queries_in, candidates_in, out, queries, candidates, block, in_sems, out_sems):
    query_rows = queries.shape[0]
    half = query_rows // LANES // 2 * LANES
    spans = [(0, half), (half, query_rows - half)]
    listed = pltpu.make_async_copy(candidates_in, candidates, in_sems.at[2])
    listed.start()
    loads = [
        pltpu.make_async_copy(
            queries_in.at[pl.ds(at, rows)], queries.at[pl.ds(at, rows)], in_sems.at[i]
        )
        for i, (at, rows) in enumerate(spans)
    ]
    for load in loads:
        load.start()
    listed.wait()
    fact_rows = block.shape[0] - query_rows
    number = candidates.shape[1]
    per_chip = CORES * per_owner
    ids = jnp.broadcast_to(candidates[...], (fact_rows, number))
    row = lax.broadcasted_iota(jnp.int32, ids.shape, 0)
    lane = lax.broadcasted_iota(jnp.int32, ids.shape, 1)
    chosen = ring_place(ids // per_chip, chips) == row
    ones = jnp.where(chosen, 1.0, 0.0)
    before = jnp.where(
        lax.broadcasted_iota(jnp.int32, (number, number), 0)
        < lax.broadcasted_iota(jnp.int32, (number, number), 1), 1.0, 0.0,
    )
    rank = jnp.dot(
        ones.astype(jnp.bfloat16), before.astype(jnp.bfloat16), preferred_element_type=jnp.float32
    )
    rank = jnp.where(chosen, rank, -1.0)
    tile = (ids % per_chip).astype(jnp.float32)
    wanted = jnp.where(lane == slots, jnp.sum(ones, axis=1, keepdims=True), 0.0)
    for s in range(slots):
        found = jnp.sum(jnp.where(rank == float(s), tile, 0.0), axis=1, keepdims=True)
        wanted = jnp.where(lane == s, found, wanted)
    block[query_rows:, :] = wanted.astype(jnp.bfloat16)
    stores = []
    for i, (at, rows) in enumerate(spans):
        loads[i].wait()
        for row_at in range(at, at + rows, LANES):
            block[row_at : row_at + LANES, :] = queries[row_at : row_at + LANES, :].T
        if i:
            rows += fact_rows
        stores.append(
            pltpu.make_async_copy(block.at[pl.ds(at, rows)], out.at[pl.ds(at, rows)], out_sems.at[i])
        )
        stores[-1].start()
    for store in stores:
        store.wait()


def fact_rows_of(chips):
    return -(-chips // 16) * 16


def pack(queries, candidates, per_owner, chips, slots):
    rows, feature = queries.shape
    return pl.pallas_call(
        functools.partial(pack_kernel, per_owner, chips, slots),
        out_shape=jax.ShapeDtypeStruct((rows + fact_rows_of(chips), feature), queries.dtype),
        in_specs=[pl.BlockSpec(memory_space=pl.ANY)] * 2,
        out_specs=pl.BlockSpec(memory_space=pl.ANY),
        scratch_shapes=[
            pltpu.VMEM(queries.shape, queries.dtype),
            pltpu.VMEM(candidates.shape, candidates.dtype),
            pltpu.VMEM((rows + fact_rows_of(chips), feature), queries.dtype),
            pltpu.SemaphoreType.DMA((3,)),
            pltpu.SemaphoreType.DMA((2,)),
        ],
        compiler_params=pltpu.CompilerParams(vmem_limit_bytes=56 * 1024 * 1024),
        name="pack",
    )(queries, candidates)


def fill_tiles(source, lens, filled, filled_at, first, number):
    row = lax.broadcasted_iota(jnp.int32, source.shape[1:], 0)

    def some(i, carry):
        for k in range(4):
            at = first + 4 * i + k
            tile = source[at].astype(jnp.float32)
            tile = jnp.where(row < lens[at], tile, tile[0:1, :])
            filled[filled_at + at] = tile.astype(jnp.bfloat16)
        return carry

    lax.fori_loop(0, number // 4, some, 0)


def ready_kernel(chips, slots, parts, lens, candidates, passages, slot_of, filled, sems):
    per_owner = passages.shape[0]
    size = per_owner // parts
    loads = [
        pltpu.make_async_copy(
            passages.at[pl.ds(i * size, size)], filled.at[pl.ds(i * size, size)], sems.at[i]
        )
        for i in range(parts)
    ]
    for load in loads:
        load.start()
    number = candidates.shape[1]
    my_place = ring_place(lax.axis_index("corpus") // CORES, chips)
    wide = jnp.broadcast_to(candidates[...], (number, number)) // (CORES * per_owner)
    tall = wide.astype(jnp.float32).T.astype(jnp.int32)
    row = lax.broadcasted_iota(jnp.int32, (number, number), 0)
    lane = lax.broadcasted_iota(jnp.int32, (number, number), 1)
    earlier = jnp.where((wide == tall) & (lane < row), 1.0, 0.0)
    rank = jnp.sum(earlier, axis=1, keepdims=True).astype(jnp.int32)
    ahead = ring_place(tall, chips) - my_place
    ahead = jnp.where(ahead < 0, ahead + chips, ahead)
    slot_of[...] = ahead * slots + rank
    for i, load in enumerate(loads):
        load.wait()
        fill_tiles(filled, lens, filled, 0, i * size, size)


def ready(lengths, candidates, passages, chips, slots):
    number = candidates.shape[1]
    per_owner = passages.shape[0]
    parts = 4 if per_owner % 16 == 0 else 1
    return pl.pallas_call(
        functools.partial(ready_kernel, chips, slots, parts),
        out_shape=(
            jax.ShapeDtypeStruct((number, number), jnp.int32),
            jax.ShapeDtypeStruct(passages.shape, passages.dtype),
        ),
        in_specs=[
            pl.BlockSpec(memory_space=pltpu.SMEM),
            pl.BlockSpec(memory_space=pltpu.VMEM),
            pl.BlockSpec(memory_space=pl.ANY),
        ],
        out_specs=(pl.BlockSpec(memory_space=pltpu.VMEM),) * 2,
        scratch_shapes=[pltpu.SemaphoreType.DMA((parts,))],
        compiler_params=pltpu.CompilerParams(vmem_limit_bytes=READY_LIMIT),
        name="ready",
    )(lengths, candidates, passages)


def join_kernel(lens, other, own, filled, sem):
    per_owner = other.shape[0]
    core = lax.axis_index("corpus") % CORES
    keep = pltpu.make_async_copy(own, filled.at[pl.ds(core * per_owner, per_owner)], sem)
    keep.start()
    fill_tiles(other, lens, filled, (1 - core) * per_owner, 0, per_owner)
    keep.wait()


def join(lengths, other, own):
    return pl.pallas_call(
        join_kernel,
        out_shape=jax.ShapeDtypeStruct((CORES * own.shape[0],) + own.shape[1:], own.dtype),
        in_specs=[
            pl.BlockSpec(memory_space=pltpu.SMEM),
            pl.BlockSpec(memory_space=pltpu.VMEM),
            pl.BlockSpec(memory_space=pltpu.VMEM),
        ],
        out_specs=pl.BlockSpec(memory_space=pltpu.VMEM),
        scratch_shapes=[pltpu.SemaphoreType.DMA],
        compiler_params=pltpu.CompilerParams(vmem_limit_bytes=VMEM_LIMIT),
        name="join",
    )(lengths, other, own)


def lane_step(chunks, query_tok):
    return query_tok // pl.next_power_of_2(chunks)


def token_sums(parts, query_tok):
    lane = lax.broadcasted_iota(jnp.int32, parts[0].shape, 1)
    parts = list(parts)
    parts += [None] * (pl.next_power_of_2(len(parts)) - len(parts))
    shift = query_tok // 2
    while shift >= 1:
        low = (lane & shift) == 0
        half = max(1, len(parts) // 2)
        merged = []
        for k in range(half):
            a = parts[k]
            b = parts[k + half] if len(parts) > 1 else None
            if a is None:
                merged.append(None)
                continue
            x = a + pltpu.roll(a, LANES - shift, 1)
            if b is not None:
                x = jnp.where(low, x, b + pltpu.roll(b, shift, 1))
            merged.append(x)
        parts = merged
        shift //= 2
    return parts[0]


def score_kernel(pieces, slots, query_tok, chips, *refs):
    blocks = len(pieces)
    arrays = sum(pieces)
    tiles = refs[0]
    held = refs[1 : 1 + arrays]
    outs = refs[1 + arrays : 1 + arrays + blocks]
    weights, nearest, plan_v, plan, sem, weight_sems = refs[1 + arrays + blocks :]
    tile_rows = tiles.shape[1]
    my_place = ring_place(lax.axis_index("corpus") // CORES, chips)
    fact_rows = fact_rows_of(chips)

    loads = []
    fact_row = lax.broadcasted_iota(jnp.int32, (fact_rows, LANES), 0)
    at = 0
    for b, count in enumerate(pieces):
        row = 0
        for ref in held[at : at + count]:
            rows = min(ref.shape[0], weights.shape[1] - row)
            loads.append(
                pltpu.make_async_copy(
                    ref.at[pl.ds(0, rows)], weights.at[b, pl.ds(row, rows)], weight_sems.at[len(loads)]
                )
            )
            row += rows
        fact = ref[rows : rows + fact_rows, :].astype(jnp.float32)
        fact = jnp.sum(jnp.where(fact_row == my_place, fact, 0.0), axis=0, keepdims=True)
        plan_v[b : b + 1, :] = fact.astype(jnp.int32)
        at += count
    to_scalar = pltpu.make_async_copy(plan_v, plan, sem)
    to_scalar.start()
    for load in loads:
        load.start()
    to_scalar.wait()

    slot_row = lax.broadcasted_iota(jnp.int32, (slots, LANES), 0)

    def score_block(b, carry):
        count = plan[b, slots]
        for k in range(blocks):

            @pl.when(b == k)
            def _(k=k):
                for load in loads[sum(pieces[:k]) : sum(pieces[: k + 1])]:
                    load.wait()

        def score_tiles(first, number):
            left = jnp.concatenate([tiles[plan[b, first + t]] for t in range(number)], axis=0)
            start = pl.multiple_of(first * 8, 8 * number)
            for c in range(0, nearest.shape[0], 2):
                pair = [weights[b, k * LANES : (k + 1) * LANES, :] for k in (c, c + 1)]
                similar = jnp.dot(
                    left, jnp.concatenate(pair, axis=1), preferred_element_type=jnp.float32
                )
                best = jnp.max(similar.reshape(number, tile_rows // 8, 8, 2 * LANES), axis=1)
                best = best.reshape(number * 8, 2 * LANES)
                for k in range(2):
                    nearest[c + k, pl.ds(start, number * 8), :] = best[:, k * LANES : (k + 1) * LANES]

        whole = count // GROUP
        rest = count - whole * GROUP
        small = (rest > 0) & (rest <= GROUP // 2)
        turns = pl.cdiv(count, GROUP) - small.astype(jnp.int32)

        def turn(g, carry):
            score_tiles(pl.multiple_of(g * GROUP, GROUP), GROUP)
            return carry

        lax.fori_loop(0, turns, turn, 0)
        pl.when(small)(lambda: score_tiles(pl.multiple_of(whole * GROUP, GROUP), GROUP // 2))

        parts = []
        for k in range(nearest.shape[0]):
            x = nearest[k, pl.ds(0, slots, stride=8), :]
            for sublane in range(1, 8):
                x = jnp.maximum(x, nearest[k, pl.ds(sublane, slots, stride=8), :])
            parts.append(x)
        total = token_sums(parts, query_tok)
        total = jnp.where(slot_row < count, total / float(query_tok), 0.0)
        for k in range(blocks):

            @pl.when(b == k)
            def _(k=k):
                outs[k][...] = total

        return carry

    lax.fori_loop(0, blocks, score_block, 0)


def score(held, slots, query_tok, chips, tiles):
    pieces = tuple(len(arrays) for arrays in held)
    flat = [x for arrays in held for x in arrays]
    blocks = len(pieces)
    _, tile_rows, feature = tiles.shape
    query_rows = sum(x.shape[0] for x in held[0]) - fact_rows_of(chips)
    flops = 2 * blocks * slots * tile_rows * feature * query_rows
    return pl.pallas_call(
        functools.partial(score_kernel, pieces, slots, query_tok, chips),
        out_shape=(jax.ShapeDtypeStruct((slots, LANES), jnp.float32),) * blocks,
        in_specs=[pl.BlockSpec(memory_space=pltpu.VMEM)] * (1 + len(flat)),
        out_specs=(pl.BlockSpec(memory_space=pltpu.VMEM),) * blocks,
        scratch_shapes=[
            pltpu.VMEM((blocks, query_rows, feature), tiles.dtype),
            pltpu.VMEM((query_rows // LANES, 8 * slots, LANES), jnp.float32),
            pltpu.VMEM((8, LANES), jnp.int32),
            pltpu.SMEM((8, LANES), jnp.int32),
            pltpu.SemaphoreType.DMA,
            pltpu.SemaphoreType.DMA((len(flat),)),
        ],
        compiler_params=pltpu.CompilerParams(vmem_limit_bytes=VMEM_LIMIT),
        cost_estimate=pl.CostEstimate(
            flops=3 * flops,
            bytes_accessed=blocks * (slots * tile_rows + query_rows) * feature * 2,
            transcendentals=0,
        ),
        name="score",
    )(tiles, *flat)


def sort_descending(parts, lanes):
    parts = list(parts)
    many = len(parts)
    number = many * 8
    sub = lax.broadcasted_iota(jnp.int32, (8, lanes), 0)
    size = 2
    while size <= number:
        reach = size // 2
        while reach >= 1:
            if reach < many:
                for v in range(many):
                    if v & reach:
                        continue
                    a, b = parts[v], parts[v | reach]
                    high, low = jnp.maximum(a, b), jnp.minimum(a, b)
                    if size >= number:
                        parts[v], parts[v | reach] = high, low
                    elif size < many:
                        down = (v & size) == 0
                        parts[v], parts[v | reach] = (high, low) if down else (low, high)
                    else:
                        down = (sub & (size // many)) == 0
                        parts[v] = jnp.where(down, high, low)
                        parts[v | reach] = jnp.where(down, low, high)
            else:
                step = reach // many
                is_first = (sub & step) == 0
                if size >= number:
                    keep_high = is_first
                else:
                    keep_high = is_first == ((sub & (size // many)) == 0)
                for v in range(many):
                    x = parts[v]
                    partner = jnp.where(is_first, pltpu.roll(x, 8 - step, 0), pltpu.roll(x, step, 0))
                    parts[v] = jnp.where(keep_high, jnp.maximum(x, partner), jnp.minimum(x, partner))
            reach //= 2
        size *= 2
    return parts


def finish_kernel(arrays, per_device, query_tok, topk, slot_of, *refs):
    returned = refs[:arrays]
    scores, best_scores, spread, ranked, rows, turned = refs[arrays:]
    number = slot_of.shape[0]
    step = returned[0].shape[0]
    for at, ref in enumerate(returned):
        spread[at * step : (at + 1) * step, :] = ref[...]
    total = spread.shape[0]
    lane = lax.broadcasted_iota(jnp.int32, (number, total), 1)
    choose = (slot_of[:, 0:1] == lane).astype(jnp.float32).astype(jnp.bfloat16)
    by_candidate = jnp.zeros((number, LANES), jnp.float32)
    for part in split_exact(spread[...]):
        by_candidate += jnp.dot(choose, part, preferred_element_type=jnp.float32)

    each = LANES // query_tok
    step = lane_step(-(-per_device // each), query_tok)
    many_rows = query_tok // step

    def in_order(x):
        turned[...] = x.T
        for m in range(each):
            rows[pl.ds(m, many_rows, stride=each), :] = turned[
                pl.ds(m * query_tok, many_rows, stride=step), :
            ]
        return rows[...]

    scores[...] = in_order(by_candidate)[:per_device, :]
    many = number // 8
    parts = sort_descending([by_candidate[8 * v : 8 * v + 8, :] for v in range(many)], LANES)
    for v in range(many):
        ranked[pl.ds(v, 8, stride=many), :] = parts[v]
    best_scores[...] = in_order(ranked[...])[:per_device, :topk]


def finish(per_device, query_tok, slot_of, returned):
    number = slot_of.shape[0]
    total = sum(r.shape[0] for r in returned)
    return pl.pallas_call(
        functools.partial(finish_kernel, len(returned), per_device, query_tok, TOPK),
        out_shape=(
            jax.ShapeDtypeStruct((per_device, number), jnp.float32),
            jax.ShapeDtypeStruct((per_device, TOPK), jnp.float32),
        ),
        in_specs=[pl.BlockSpec(memory_space=pltpu.VMEM)] * (1 + len(returned)),
        out_specs=(pl.BlockSpec(memory_space=pltpu.VMEM),) * 2,
        scratch_shapes=[
            pltpu.VMEM((total, LANES), jnp.float32),
            pltpu.VMEM((number, LANES), jnp.float32),
            pltpu.VMEM((LANES, number), jnp.float32),
            pltpu.VMEM((LANES, number), jnp.float32),
        ],
        compiler_params=pltpu.CompilerParams(vmem_limit_bytes=VMEM_LIMIT),
        name="finish",
    )(slot_of, *returned)


def local(queries, passages, lengths, candidates):
    peers = lax.axis_size("corpus")
    chips = peers // CORES
    per_owner, tile_rows, feature = passages.shape
    per_device, query_tok = queries.shape[0], queries.shape[1]
    number = candidates.shape[1]
    capacity = max(2, 3 * number // (2 * peers))
    slots = -(-CORES * capacity // 8) * 8
    order = ring_order(chips)

    def moved(x, distance):
        pairs = [
            (order[i] * CORES + core, order[(i + distance) % chips] * CORES + core)
            for i in range(chips)
            for core in range(CORES)
        ]
        return lax.ppermute(x, "corpus", pairs)

    swap = [(i, i ^ 1) for i in range(peers)]
    other = lax.ppermute(passages, "corpus", swap)
    other_lengths = lax.ppermute(lengths, "corpus", swap)
    slot_of, own = ready(lengths, candidates, passages, chips, slots)
    tiles = join(other_lengths, other, own)

    block = pack(
        queries.reshape(per_device * query_tok, feature), candidates, per_owner, chips, slots
    )
    half = per_device * query_tok // LANES // 2 * LANES
    middle = chips // 2
    arrived = {0: [block]}

    def send_on(step):
        if step < middle:
            arrived[step] = [moved(x, 1) for x in arrived[step - 1]]
            arrived[-step] = [moved(x, -1) for x in arrived[1 - step]]
        else:
            arrived[step] = [
                moved(arrived[step - 1][0][:half], 1), moved(arrived[1 - step][0][half:], -1)
            ]

    send_on(1)
    scored, back = {}, {}

    def send_back(offsets):
        return {offset % chips: moved(scored[offset], -offset) for offset in offsets}

    for step in range(middle + 1):
        if 0 < step < middle:
            send_on(step + 1)
        offsets = (step,) if step in (0, middle) else (step, -step)
        fresh = score([arrived[offset] for offset in offsets], slots, query_tok, chips, tiles)
        scored.update(zip(offsets, fresh))
        names = [] if step == middle else [step + 1, -step - 1] if step + 1 < middle else [middle]
        held, scored, back = lax.optimization_barrier(
            ([arrived[name] for name in names], scored, send_back(offsets) if step == 1 else back)
        )
        arrived.update(zip(names, held))
    back.update(send_back([offset for offset in scored if abs(offset) > 1]))
    back[0] = scored[0]
    return finish(per_device, query_tok, slot_of, [back[j] for j in range(chips)])


def solution(mesh):
    return jax.shard_map(
        local,
        mesh=mesh,
        in_specs=(
            P(("groups", "corpus"), None, None),
            P(("groups", "corpus"), None, None),
            P(("groups", "corpus")),
            P(("groups", "corpus"), None),
        ),
        out_specs=(P(("groups", "corpus"), None), P(("groups", "corpus"), None)),
        check_vma=False,
    )
```

```python
import functools

import jax
import jax.numpy as jnp
from jax import lax
from jax.experimental import pallas as pl
from jax.experimental.pallas import tpu as pltpu
from jax.sharding import PartitionSpec as P

TOPK = 100
CORES = 2
LANES = 128
GROUP = 8
VMEM_LIMIT = 32 * 1024 * 1024
READY_LIMIT = 48 * 1024 * 1024


def ring_order(chips):
    return list(range(0, chips, 2)) + list(range(1, chips, 2))[::-1]


def ring_place(chip, chips):
    return jnp.where(chip % 2 == 0, chip // 2, chips - (chip + 1) // 2)


def split_exact(x):
    high = x.astype(jnp.bfloat16)
    rest = x - high.astype(jnp.float32)
    middle = rest.astype(jnp.bfloat16)
    low = (rest - middle.astype(jnp.float32)).astype(jnp.bfloat16)
    return high, middle, low


def pack_kernel(per_owner, chips, slots, queries_in, candidates_in, out, queries, candidates, block, in_sems, out_sems):
    query_rows = queries.shape[0]
    half = query_rows // LANES // 2 * LANES
    spans = [(0, half), (half, query_rows - half)]
    listed = pltpu.make_async_copy(candidates_in, candidates, in_sems.at[2])
    listed.start()
    loads = [
        pltpu.make_async_copy(
            queries_in.at[pl.ds(at, rows)], queries.at[pl.ds(at, rows)], in_sems.at[i]
        )
        for i, (at, rows) in enumerate(spans)
    ]
    for load in loads:
        load.start()
    listed.wait()
    fact_rows = block.shape[0] - query_rows
    number = candidates.shape[1]
    per_chip = CORES * per_owner
    ids = jnp.broadcast_to(candidates[...], (fact_rows, number))
    row = lax.broadcasted_iota(jnp.int32, ids.shape, 0)
    lane = lax.broadcasted_iota(jnp.int32, ids.shape, 1)
    chosen = ring_place(ids // per_chip, chips) == row
    ones = jnp.where(chosen, 1.0, 0.0)
    before = jnp.where(
        lax.broadcasted_iota(jnp.int32, (number, number), 0)
        < lax.broadcasted_iota(jnp.int32, (number, number), 1), 1.0, 0.0,
    )
    rank = jnp.dot(
        ones.astype(jnp.bfloat16), before.astype(jnp.bfloat16), preferred_element_type=jnp.float32
    )
    rank = jnp.where(chosen, rank, -1.0)
    tile = (ids % per_chip).astype(jnp.float32)
    wanted = jnp.where(lane == slots, jnp.sum(ones, axis=1, keepdims=True), 0.0)
    for s in range(slots):
        found = jnp.sum(jnp.where(rank == float(s), tile, 0.0), axis=1, keepdims=True)
        wanted = jnp.where(lane == s, found, wanted)
    block[query_rows:, :] = wanted.astype(jnp.bfloat16)
    stores = []
    for i, (at, rows) in enumerate(spans):
        loads[i].wait()
        for row_at in range(at, at + rows, LANES):
            block[row_at : row_at + LANES, :] = queries[row_at : row_at + LANES, :].T
        if i:
            rows += fact_rows
        stores.append(
            pltpu.make_async_copy(block.at[pl.ds(at, rows)], out.at[pl.ds(at, rows)], out_sems.at[i])
        )
        stores[-1].start()
    for store in stores:
        store.wait()


def fact_rows_of(chips):
    return -(-chips // 16) * 16


def pack(queries, candidates, per_owner, chips, slots):
    rows, feature = queries.shape
    return pl.pallas_call(
        functools.partial(pack_kernel, per_owner, chips, slots),
        out_shape=jax.ShapeDtypeStruct((rows + fact_rows_of(chips), feature), queries.dtype),
        in_specs=[pl.BlockSpec(memory_space=pl.ANY)] * 2,
        out_specs=pl.BlockSpec(memory_space=pl.ANY),
        scratch_shapes=[
            pltpu.VMEM(queries.shape, queries.dtype),
            pltpu.VMEM(candidates.shape, candidates.dtype),
            pltpu.VMEM((rows + fact_rows_of(chips), feature), queries.dtype),
            pltpu.SemaphoreType.DMA((3,)),
            pltpu.SemaphoreType.DMA((2,)),
        ],
        compiler_params=pltpu.CompilerParams(vmem_limit_bytes=56 * 1024 * 1024),
        name="pack",
    )(queries, candidates)


def fill_tiles(source, lens, filled, filled_at, first, number):
    row = lax.broadcasted_iota(jnp.int32, source.shape[1:], 0)

    def some(i, carry):
        for k in range(4):
            at = first + 4 * i + k
            tile = source[at].astype(jnp.float32)
            tile = jnp.where(row < lens[at], tile, tile[0:1, :])
            filled[filled_at + at] = tile.astype(jnp.bfloat16)
        return carry

    lax.fori_loop(0, number // 4, some, 0)


def ready_kernel(chips, slots, parts, lens, candidates, passages, slot_of, filled, sems):
    per_owner = passages.shape[0]
    size = per_owner // parts
    loads = [
        pltpu.make_async_copy(
            passages.at[pl.ds(i * size, size)], filled.at[pl.ds(i * size, size)], sems.at[i]
        )
        for i in range(parts)
    ]
    for load in loads:
        load.start()
    number = candidates.shape[1]
    wide = jnp.broadcast_to(candidates[...], (number, number)) // (CORES * per_owner)
    tall = wide.astype(jnp.float32).T.astype(jnp.int32)
    row = lax.broadcasted_iota(jnp.int32, (number, number), 0)
    lane = lax.broadcasted_iota(jnp.int32, (number, number), 1)
    earlier = jnp.where((wide == tall) & (lane < row), 1.0, 0.0)
    rank = jnp.sum(earlier, axis=1, keepdims=True).astype(jnp.int32)
    slot_of[...] = ring_place(tall, chips) * slots + rank
    for i, load in enumerate(loads):
        load.wait()
        fill_tiles(filled, lens, filled, 0, i * size, size)


def ready(lengths, candidates, passages, chips, slots):
    number = candidates.shape[1]
    per_owner = passages.shape[0]
    parts = 4 if per_owner % 16 == 0 else 1
    return pl.pallas_call(
        functools.partial(ready_kernel, chips, slots, parts),
        out_shape=(
            jax.ShapeDtypeStruct((number, number), jnp.int32),
            jax.ShapeDtypeStruct(passages.shape, passages.dtype),
        ),
        in_specs=[
            pl.BlockSpec(memory_space=pltpu.SMEM),
            pl.BlockSpec(memory_space=pltpu.VMEM),
            pl.BlockSpec(memory_space=pl.ANY),
        ],
        out_specs=(pl.BlockSpec(memory_space=pltpu.VMEM),) * 2,
        scratch_shapes=[pltpu.SemaphoreType.DMA((parts,))],
        compiler_params=pltpu.CompilerParams(vmem_limit_bytes=READY_LIMIT),
        name="ready",
    )(lengths, candidates, passages)


def join_kernel(lens, other, own, filled, sem):
    per_owner = other.shape[0]
    core = lax.axis_index("corpus") % CORES
    keep = pltpu.make_async_copy(own, filled.at[pl.ds(core * per_owner, per_owner)], sem)
    keep.start()
    fill_tiles(other, lens, filled, (1 - core) * per_owner, 0, per_owner)
    keep.wait()


def join(lengths, other, own):
    return pl.pallas_call(
        join_kernel,
        out_shape=jax.ShapeDtypeStruct((CORES * own.shape[0],) + own.shape[1:], own.dtype),
        in_specs=[
            pl.BlockSpec(memory_space=pltpu.SMEM),
            pl.BlockSpec(memory_space=pltpu.VMEM),
            pl.BlockSpec(memory_space=pltpu.VMEM),
        ],
        out_specs=pl.BlockSpec(memory_space=pltpu.VMEM),
        scratch_shapes=[pltpu.SemaphoreType.DMA],
        compiler_params=pltpu.CompilerParams(vmem_limit_bytes=VMEM_LIMIT),
        name="join",
    )(lengths, other, own)


def lane_step(chunks, query_tok):
    return query_tok // pl.next_power_of_2(chunks)


def token_sums(parts, query_tok):
    lane = lax.broadcasted_iota(jnp.int32, parts[0].shape, 1)
    parts = list(parts)
    parts += [None] * (pl.next_power_of_2(len(parts)) - len(parts))
    shift = query_tok // 2
    while shift >= 1:
        low = (lane & shift) == 0
        half = max(1, len(parts) // 2)
        merged = []
        for k in range(half):
            a = parts[k]
            b = parts[k + half] if len(parts) > 1 else None
            if a is None:
                merged.append(None)
                continue
            x = a + pltpu.roll(a, LANES - shift, 1)
            if b is not None:
                x = jnp.where(low, x, b + pltpu.roll(b, shift, 1))
            merged.append(x)
        parts = merged
        shift //= 2
    return parts[0]


def score_kernel(pieces, offsets, slots, query_tok, chips, kept, *refs):
    blocks = len(pieces)
    arrays = sum(pieces)
    tiles = refs[0]
    held = refs[1 : 1 + arrays]
    out, weights, nearest, plan_v, plan, sem, weight_sems = refs[1 + arrays + kept :]
    tile_rows = tiles.shape[1]
    my_place = ring_place(lax.axis_index("corpus") // CORES, chips)
    fact_rows = fact_rows_of(chips)

    loads = []
    fact_row = lax.broadcasted_iota(jnp.int32, (fact_rows, LANES), 0)
    at = 0
    for b, count in enumerate(pieces):
        row = 0
        for ref in held[at : at + count]:
            rows = min(ref.shape[0], weights.shape[1] - row)
            loads.append(
                pltpu.make_async_copy(
                    ref.at[pl.ds(0, rows)], weights.at[b, pl.ds(row, rows)], weight_sems.at[len(loads)]
                )
            )
            row += rows
        fact = ref[rows : rows + fact_rows, :].astype(jnp.float32)
        fact = jnp.sum(jnp.where(fact_row == my_place, fact, 0.0), axis=0, keepdims=True)
        plan_v[b : b + 1, :] = fact.astype(jnp.int32)
        at += count
    to_scalar = pltpu.make_async_copy(plan_v, plan, sem)
    to_scalar.start()
    if kept:
        out[...] = refs[1 + arrays][...]
    else:
        out[...] = jnp.zeros(out.shape, out.dtype)
    for load in loads:
        load.start()
    to_scalar.wait()

    slot_row = lax.broadcasted_iota(jnp.int32, (slots, LANES), 0)

    def score_block(b, carry):
        count = plan[b, slots]
        for k in range(blocks):

            @pl.when(b == k)
            def _(k=k):
                for load in loads[sum(pieces[:k]) : sum(pieces[: k + 1])]:
                    load.wait()

        def score_tiles(first, number):
            left = jnp.concatenate([tiles[plan[b, first + t]] for t in range(number)], axis=0)
            start = pl.multiple_of(first * 8, 8 * number)
            for c in range(0, nearest.shape[0], 2):
                pair = [weights[b, k * LANES : (k + 1) * LANES, :] for k in (c, c + 1)]
                similar = jnp.dot(
                    left, jnp.concatenate(pair, axis=1), preferred_element_type=jnp.float32
                )
                best = jnp.max(similar.reshape(number, tile_rows // 8, 8, 2 * LANES), axis=1)
                best = best.reshape(number * 8, 2 * LANES)
                for k in range(2):
                    nearest[c + k, pl.ds(start, number * 8), :] = best[:, k * LANES : (k + 1) * LANES]

        whole = count // GROUP
        rest = count - whole * GROUP
        small = (rest > 0) & (rest <= GROUP // 2)
        turns = pl.cdiv(count, GROUP) - small.astype(jnp.int32)

        def turn(g, carry):
            score_tiles(pl.multiple_of(g * GROUP, GROUP), GROUP)
            return carry

        lax.fori_loop(0, turns, turn, 0)
        pl.when(small)(lambda: score_tiles(pl.multiple_of(whole * GROUP, GROUP), GROUP // 2))

        parts = []
        for k in range(nearest.shape[0]):
            x = nearest[k, pl.ds(0, slots, stride=8), :]
            for sublane in range(1, 8):
                x = jnp.maximum(x, nearest[k, pl.ds(sublane, slots, stride=8), :])
            parts.append(x)
        total = token_sums(parts, query_tok)
        total = jnp.where(slot_row < count, total / float(query_tok), 0.0)
        offset = offsets[-1]
        for k in range(blocks - 1):
            offset = jnp.where(b == k, offsets[k], offset)
        place = my_place - offset
        out[jnp.where(place < 0, place + chips, place)] = total
        return carry

    lax.fori_loop(0, blocks, score_block, 0)


def score(held, offsets, slots, query_tok, chips, tiles, *earlier):
    pieces = tuple(len(arrays) for arrays in held)
    flat = [x for arrays in held for x in arrays]
    blocks = len(pieces)
    _, tile_rows, feature = tiles.shape
    query_rows = sum(x.shape[0] for x in held[0]) - fact_rows_of(chips)
    flops = 2 * blocks * slots * tile_rows * feature * query_rows
    return pl.pallas_call(
        functools.partial(
            score_kernel, pieces, offsets, slots, query_tok, chips, len(earlier)
        ),
        out_shape=jax.ShapeDtypeStruct((chips, slots, LANES), jnp.float32),
        in_specs=[pl.BlockSpec(memory_space=pltpu.VMEM)] * (1 + len(flat) + len(earlier)),
        out_specs=pl.BlockSpec(memory_space=pltpu.VMEM),
        scratch_shapes=[
            pltpu.VMEM((blocks, query_rows, feature), tiles.dtype),
            pltpu.VMEM((query_rows // LANES, 8 * slots, LANES), jnp.float32),
            pltpu.VMEM((8, LANES), jnp.int32),
            pltpu.SMEM((8, LANES), jnp.int32),
            pltpu.SemaphoreType.DMA,
            pltpu.SemaphoreType.DMA((len(flat),)),
        ],
        compiler_params=pltpu.CompilerParams(vmem_limit_bytes=VMEM_LIMIT),
        cost_estimate=pl.CostEstimate(
            flops=3 * flops,
            bytes_accessed=blocks * (slots * tile_rows + query_rows) * feature * 2,
            transcendentals=0,
        ),
        name="score",
    )(tiles, *flat, *earlier)


def sort_descending(parts, lanes):
    parts = list(parts)
    many = len(parts)
    number = many * 8
    sub = lax.broadcasted_iota(jnp.int32, (8, lanes), 0)
    size = 2
    while size <= number:
        reach = size // 2
        while reach >= 1:
            if reach < many:
                for v in range(many):
                    if v & reach:
                        continue
                    a, b = parts[v], parts[v | reach]
                    high, low = jnp.maximum(a, b), jnp.minimum(a, b)
                    if size >= number:
                        parts[v], parts[v | reach] = high, low
                    elif size < many:
                        down = (v & size) == 0
                        parts[v], parts[v | reach] = (high, low) if down else (low, high)
                    else:
                        down = (sub & (size // many)) == 0
                        parts[v] = jnp.where(down, high, low)
                        parts[v | reach] = jnp.where(down, low, high)
            else:
                step = reach // many
                is_first = (sub & step) == 0
                if size >= number:
                    keep_high = is_first
                else:
                    keep_high = is_first == ((sub & (size // many)) == 0)
                for v in range(many):
                    x = parts[v]
                    partner = jnp.where(is_first, pltpu.roll(x, 8 - step, 0), pltpu.roll(x, step, 0))
                    parts[v] = jnp.where(keep_high, jnp.maximum(x, partner), jnp.minimum(x, partner))
            reach //= 2
        size *= 2
    return parts


def finish_kernel(
    per_device, query_tok, topk,
    slot_of, returned, scores, best_scores, ranked, rows, turned,
):
    number = slot_of.shape[0]
    spread = returned[...].reshape(returned.shape[0] * returned.shape[1], LANES)
    total = spread.shape[0]
    lane = lax.broadcasted_iota(jnp.int32, (number, total), 1)
    choose = (slot_of[:, 0:1] == lane).astype(jnp.float32).astype(jnp.bfloat16)
    by_candidate = jnp.zeros((number, LANES), jnp.float32)
    for part in split_exact(spread):
        by_candidate += jnp.dot(choose, part, preferred_element_type=jnp.float32)

    each = LANES // query_tok
    step = lane_step(-(-per_device // each), query_tok)
    many_rows = query_tok // step

    def in_order(x):
        turned[...] = x.T
        for m in range(each):
            rows[pl.ds(m, many_rows, stride=each), :] = turned[
                pl.ds(m * query_tok, many_rows, stride=step), :
            ]
        return rows[...]

    scores[...] = in_order(by_candidate)[:per_device, :]
    many = number // 8
    parts = sort_descending([by_candidate[8 * v : 8 * v + 8, :] for v in range(many)], LANES)
    for v in range(many):
        ranked[pl.ds(v, 8, stride=many), :] = parts[v]
    best_scores[...] = in_order(ranked[...])[:per_device, :topk]


def finish(per_device, query_tok, slot_of, returned):
    number = slot_of.shape[0]
    return pl.pallas_call(
        functools.partial(finish_kernel, per_device, query_tok, TOPK),
        out_shape=(
            jax.ShapeDtypeStruct((per_device, number), jnp.float32),
            jax.ShapeDtypeStruct((per_device, TOPK), jnp.float32),
        ),
        in_specs=[pl.BlockSpec(memory_space=pltpu.VMEM)] * 2,
        out_specs=(pl.BlockSpec(memory_space=pltpu.VMEM),) * 2,
        scratch_shapes=[
            pltpu.VMEM((number, LANES), jnp.float32),
            pltpu.VMEM((LANES, number), jnp.float32),
            pltpu.VMEM((LANES, number), jnp.float32),
        ],
        compiler_params=pltpu.CompilerParams(vmem_limit_bytes=VMEM_LIMIT),
        name="finish",
    )(slot_of, returned)


def local(queries, passages, lengths, candidates):
    peers = lax.axis_size("corpus")
    chips = peers // CORES
    per_owner, tile_rows, feature = passages.shape
    per_device, query_tok = queries.shape[0], queries.shape[1]
    number = candidates.shape[1]
    capacity = max(2, 3 * number // (2 * peers))
    slots = -(-CORES * capacity // 8) * 8
    order = ring_order(chips)

    def moved(x, distance):
        pairs = [
            (order[i] * CORES + core, order[(i + distance) % chips] * CORES + core)
            for i in range(chips)
            for core in range(CORES)
        ]
        return lax.ppermute(x, "corpus", pairs)

    swap = [(i, i ^ 1) for i in range(peers)]
    other = lax.ppermute(passages, "corpus", swap)
    other_lengths = lax.ppermute(lengths, "corpus", swap)
    slot_of, own = ready(lengths, candidates, passages, chips, slots)
    tiles = join(other_lengths, other, own)

    block = pack(
        queries.reshape(per_device * query_tok, feature), candidates, per_owner, chips, slots
    )
    half = per_device * query_tok // LANES // 2 * LANES
    middle = chips // 2
    arrived = {0: [block]}

    def send_on(step):
        if step < middle:
            arrived[step] = [moved(x, 1) for x in arrived[step - 1]]
            arrived[-step] = [moved(x, -1) for x in arrived[1 - step]]
        else:
            arrived[step] = [
                moved(arrived[step - 1][0][:half], 1), moved(arrived[1 - step][0][half:], -1)
            ]

    send_on(1)
    scored = []
    for step in range(middle + 1):
        if 0 < step < middle:
            send_on(step + 1)
        offsets = (step,) if step in (0, middle) else (step, -step)
        fresh = score(
            [arrived[offset] for offset in offsets], tuple(offset % chips for offset in offsets),
            slots, query_tok, chips, tiles, *scored,
        )
        names = [] if step == middle else [step + 1, -step - 1] if step + 1 < middle else [middle]
        held, fresh = lax.optimization_barrier(([arrived[name] for name in names], fresh))
        arrived.update(zip(names, held))
        scored = [fresh]
    by_place = [[order[i] * CORES + k for i in range(chips)] for k in range(CORES)]
    returned = lax.all_to_all(
        scored[0], "corpus", split_axis=0, concat_axis=0, tiled=True, axis_index_groups=by_place
    )
    return finish(per_device, query_tok, slot_of, returned)


def solution(mesh):
    return jax.shard_map(
        local,
        mesh=mesh,
        in_specs=(
            P(("groups", "corpus"), None, None),
            P(("groups", "corpus"), None, None),
            P(("groups", "corpus")),
            P(("groups", "corpus"), None),
        ),
        out_specs=(P(("groups", "corpus"), None), P(("groups", "corpus"), None)),
        check_vma=False,
    )
```

```python
import functools

import jax
import jax.numpy as jnp
from jax import lax
from jax.experimental import pallas as pl
from jax.experimental.pallas import tpu as pltpu
from jax.sharding import PartitionSpec as P

TOPK = 100
CORES = 2
LANES = 128
GROUP = 8
VMEM_LIMIT = 32 * 1024 * 1024
READY_LIMIT = 48 * 1024 * 1024


def ring_order(chips):
    return list(range(0, chips, 2)) + list(range(1, chips, 2))[::-1]


def ring_place(chip, chips):
    return jnp.where(chip % 2 == 0, chip // 2, chips - (chip + 1) // 2)


def split_exact(x):
    high = x.astype(jnp.bfloat16)
    rest = x - high.astype(jnp.float32)
    middle = rest.astype(jnp.bfloat16)
    low = (rest - middle.astype(jnp.float32)).astype(jnp.bfloat16)
    return high, middle, low


def pack_kernel(per_owner, chips, slots, queries_in, candidates_in, out, queries, candidates, block, in_sems, out_sems):
    query_rows = queries.shape[0]
    half = query_rows // LANES // 2 * LANES
    spans = [(0, half), (half, query_rows - half)]
    listed = pltpu.make_async_copy(candidates_in, candidates, in_sems.at[2])
    listed.start()
    loads = [
        pltpu.make_async_copy(
            queries_in.at[pl.ds(at, rows)], queries.at[pl.ds(at, rows)], in_sems.at[i]
        )
        for i, (at, rows) in enumerate(spans)
    ]
    for load in loads:
        load.start()
    listed.wait()
    fact_rows = block.shape[0] - query_rows
    number = candidates.shape[1]
    per_chip = CORES * per_owner
    ids = jnp.broadcast_to(candidates[...], (fact_rows, number))
    row = lax.broadcasted_iota(jnp.int32, ids.shape, 0)
    lane = lax.broadcasted_iota(jnp.int32, ids.shape, 1)
    chosen = ring_place(ids // per_chip, chips) == row
    ones = jnp.where(chosen, 1.0, 0.0)
    before = jnp.where(
        lax.broadcasted_iota(jnp.int32, (number, number), 0)
        < lax.broadcasted_iota(jnp.int32, (number, number), 1), 1.0, 0.0,
    )
    rank = jnp.dot(
        ones.astype(jnp.bfloat16), before.astype(jnp.bfloat16), preferred_element_type=jnp.float32
    )
    rank = jnp.where(chosen, rank, -1.0)
    tile = (ids % per_chip).astype(jnp.float32)
    wanted = jnp.where(lane == slots, jnp.sum(ones, axis=1, keepdims=True), 0.0)
    for s in range(slots):
        found = jnp.sum(jnp.where(rank == float(s), tile, 0.0), axis=1, keepdims=True)
        wanted = jnp.where(lane == s, found, wanted)
    block[query_rows:, :] = wanted.astype(jnp.bfloat16)
    stores = []
    for i, (at, rows) in enumerate(spans):
        loads[i].wait()
        for row_at in range(at, at + rows, LANES):
            block[row_at : row_at + LANES, :] = queries[row_at : row_at + LANES, :].T
        if i:
            rows += fact_rows
        stores.append(
            pltpu.make_async_copy(block.at[pl.ds(at, rows)], out.at[pl.ds(at, rows)], out_sems.at[i])
        )
        stores[-1].start()
    for store in stores:
        store.wait()


def fact_rows_of(chips):
    return -(-chips // 16) * 16


def pack(queries, candidates, per_owner, chips, slots):
    rows, feature = queries.shape
    return pl.pallas_call(
        functools.partial(pack_kernel, per_owner, chips, slots),
        out_shape=jax.ShapeDtypeStruct((rows + fact_rows_of(chips), feature), queries.dtype),
        in_specs=[pl.BlockSpec(memory_space=pl.ANY)] * 2,
        out_specs=pl.BlockSpec(memory_space=pl.ANY),
        scratch_shapes=[
            pltpu.VMEM(queries.shape, queries.dtype),
            pltpu.VMEM(candidates.shape, candidates.dtype),
            pltpu.VMEM((rows + fact_rows_of(chips), feature), queries.dtype),
            pltpu.SemaphoreType.DMA((3,)),
            pltpu.SemaphoreType.DMA((2,)),
        ],
        compiler_params=pltpu.CompilerParams(vmem_limit_bytes=56 * 1024 * 1024),
        name="pack",
    )(queries, candidates)


def fill_tiles(source, lens, filled, filled_at, first, number):
    row = lax.broadcasted_iota(jnp.int32, source.shape[1:], 0)

    def some(i, carry):
        for k in range(4):
            at = first + 4 * i + k
            tile = source[at].astype(jnp.float32)
            tile = jnp.where(row < lens[at], tile, tile[0:1, :])
            filled[filled_at + at] = tile.astype(jnp.bfloat16)
        return carry

    lax.fori_loop(0, number // 4, some, 0)


def ready_kernel(chips, slots, parts, lens, candidates, passages, slot_of, filled, sems):
    per_owner = passages.shape[0]
    size = per_owner // parts
    loads = [
        pltpu.make_async_copy(
            passages.at[pl.ds(i * size, size)], filled.at[pl.ds(i * size, size)], sems.at[i]
        )
        for i in range(parts)
    ]
    for load in loads:
        load.start()
    number = candidates.shape[1]
    my_place = ring_place(lax.axis_index("corpus") // CORES, chips)
    wide = jnp.broadcast_to(candidates[...], (number, number)) // (CORES * per_owner)
    tall = wide.astype(jnp.float32).T.astype(jnp.int32)
    row = lax.broadcasted_iota(jnp.int32, (number, number), 0)
    lane = lax.broadcasted_iota(jnp.int32, (number, number), 1)
    earlier = jnp.where((wide == tall) & (lane < row), 1.0, 0.0)
    rank = jnp.sum(earlier, axis=1, keepdims=True).astype(jnp.int32)
    ahead = ring_place(tall, chips) - my_place
    ahead = jnp.where(ahead < 0, ahead + chips, ahead)
    slot_of[...] = ahead * slots + rank
    for i, load in enumerate(loads):
        load.wait()
        fill_tiles(filled, lens, filled, 0, i * size, size)


def ready(lengths, candidates, passages, chips, slots):
    number = candidates.shape[1]
    per_owner = passages.shape[0]
    parts = 4 if per_owner % 16 == 0 else 1
    return pl.pallas_call(
        functools.partial(ready_kernel, chips, slots, parts),
        out_shape=(
            jax.ShapeDtypeStruct((number, number), jnp.int32),
            jax.ShapeDtypeStruct(passages.shape, passages.dtype),
        ),
        in_specs=[
            pl.BlockSpec(memory_space=pltpu.SMEM),
            pl.BlockSpec(memory_space=pltpu.VMEM),
            pl.BlockSpec(memory_space=pl.ANY),
        ],
        out_specs=(pl.BlockSpec(memory_space=pltpu.VMEM),) * 2,
        scratch_shapes=[pltpu.SemaphoreType.DMA((parts,))],
        compiler_params=pltpu.CompilerParams(vmem_limit_bytes=READY_LIMIT),
        name="ready",
    )(lengths, candidates, passages)


def join_kernel(lens, other, own, filled, sem):
    per_owner = other.shape[0]
    core = lax.axis_index("corpus") % CORES
    keep = pltpu.make_async_copy(own, filled.at[pl.ds(core * per_owner, per_owner)], sem)
    keep.start()
    fill_tiles(other, lens, filled, (1 - core) * per_owner, 0, per_owner)
    keep.wait()


def join(lengths, other, own):
    return pl.pallas_call(
        join_kernel,
        out_shape=jax.ShapeDtypeStruct((CORES * own.shape[0],) + own.shape[1:], own.dtype),
        in_specs=[
            pl.BlockSpec(memory_space=pltpu.SMEM),
            pl.BlockSpec(memory_space=pltpu.VMEM),
            pl.BlockSpec(memory_space=pltpu.VMEM),
        ],
        out_specs=pl.BlockSpec(memory_space=pltpu.VMEM),
        scratch_shapes=[pltpu.SemaphoreType.DMA],
        compiler_params=pltpu.CompilerParams(vmem_limit_bytes=VMEM_LIMIT),
        name="join",
    )(lengths, other, own)


def lane_step(chunks, query_tok):
    return query_tok // pl.next_power_of_2(chunks)


def token_sums(parts, query_tok):
    lane = lax.broadcasted_iota(jnp.int32, parts[0].shape, 1)
    parts = list(parts)
    parts += [None] * (pl.next_power_of_2(len(parts)) - len(parts))
    shift = query_tok // 2
    while shift >= 1:
        low = (lane & shift) == 0
        half = max(1, len(parts) // 2)
        merged = []
        for k in range(half):
            a = parts[k]
            b = parts[k + half] if len(parts) > 1 else None
            if a is None:
                merged.append(None)
                continue
            x = a + pltpu.roll(a, LANES - shift, 1)
            if b is not None:
                x = jnp.where(low, x, b + pltpu.roll(b, shift, 1))
            merged.append(x)
        parts = merged
        shift //= 2
    return parts[0]


def score_kernel(pieces, slots, query_tok, chips, *refs):
    blocks = len(pieces)
    arrays = sum(pieces)
    tiles = refs[0]
    held = refs[1 : 1 + arrays]
    outs = refs[1 + arrays : 1 + arrays + blocks]
    weights, nearest, plan_v, plan, sem, weight_sems = refs[1 + arrays + blocks :]
    tile_rows = tiles.shape[1]
    my_place = ring_place(lax.axis_index("corpus") // CORES, chips)
    fact_rows = fact_rows_of(chips)

    loads = []
    fact_row = lax.broadcasted_iota(jnp.int32, (fact_rows, LANES), 0)
    at = 0
    for b, count in enumerate(pieces):
        row = 0
        for ref in held[at : at + count]:
            rows = min(ref.shape[0], weights.shape[1] - row)
            loads.append(
                pltpu.make_async_copy(
                    ref.at[pl.ds(0, rows)], weights.at[b, pl.ds(row, rows)], weight_sems.at[len(loads)]
                )
            )
            row += rows
        fact = ref[rows : rows + fact_rows, :].astype(jnp.float32)
        fact = jnp.sum(jnp.where(fact_row == my_place, fact, 0.0), axis=0, keepdims=True)
        if b == 0:
            first_list = fact
        plan_v[b : b + 1, :] = fact.astype(jnp.int32)
        at += count
    for load in loads:
        load.start()
    to_scalar = pltpu.make_async_copy(plan_v, plan, sem)
    to_scalar.start()

    def score_tiles(b, first, picked):
        number = len(picked)
        left = jnp.concatenate([tiles[at] for at in picked], axis=0)
        start = pl.multiple_of(first * 8, 8 * number)
        for c in range(0, nearest.shape[0], 2):
            pair = [weights[b, k * LANES : (k + 1) * LANES, :] for k in (c, c + 1)]
            similar = jnp.dot(
                left, jnp.concatenate(pair, axis=1), preferred_element_type=jnp.float32
            )
            best = jnp.max(similar.reshape(number, tile_rows // 8, 8, 2 * LANES), axis=1)
            best = best.reshape(number * 8, 2 * LANES)
            for k in range(2):
                nearest[c + k, pl.ds(start, number * 8), :] = best[:, k * LANES : (k + 1) * LANES]

    list_lane = lax.broadcasted_iota(jnp.int32, (1, LANES), 1)
    picked = [
        jnp.sum(jnp.where(list_lane == t, first_list, 0.0)).astype(jnp.int32) for t in range(GROUP)
    ]
    for load in loads[: pieces[0]]:
        load.wait()
    score_tiles(0, 0, picked)
    to_scalar.wait()

    slot_row = lax.broadcasted_iota(jnp.int32, (slots, LANES), 0)

    def score_block(b, carry):
        count = plan[b, slots]
        for k in range(1, blocks):

            @pl.when(b == k)
            def _(k=k):
                for load in loads[sum(pieces[:k]) : sum(pieces[: k + 1])]:
                    load.wait()

        whole = count // GROUP
        rest = count - whole * GROUP
        small = (rest > 0) & (rest <= GROUP // 2)
        turns = pl.cdiv(count, GROUP) - small.astype(jnp.int32)

        def score_some(first, number):
            first = pl.multiple_of(first, GROUP)
            score_tiles(b, first, [plan[b, first + t] for t in range(number)])

        def turn(g, carry):
            score_some(g * GROUP, GROUP)
            return carry

        lax.fori_loop(jnp.where(b == 0, 1, 0), turns, turn, 0)
        pl.when(small)(lambda: score_some(whole * GROUP, GROUP // 2))

        parts = []
        for k in range(nearest.shape[0]):
            x = nearest[k, pl.ds(0, slots, stride=8), :]
            for sublane in range(1, 8):
                x = jnp.maximum(x, nearest[k, pl.ds(sublane, slots, stride=8), :])
            parts.append(x)
        total = token_sums(parts, query_tok)
        total = jnp.where(slot_row < count, total / float(query_tok), 0.0)
        for k in range(blocks):

            @pl.when(b == k)
            def _(k=k):
                outs[k][...] = total

        return carry

    lax.fori_loop(0, blocks, score_block, 0)


def score(held, slots, query_tok, chips, tiles):
    pieces = tuple(len(arrays) for arrays in held)
    flat = [x for arrays in held for x in arrays]
    blocks = len(pieces)
    _, tile_rows, feature = tiles.shape
    query_rows = sum(x.shape[0] for x in held[0]) - fact_rows_of(chips)
    flops = 2 * blocks * slots * tile_rows * feature * query_rows
    return pl.pallas_call(
        functools.partial(score_kernel, pieces, slots, query_tok, chips),
        out_shape=(jax.ShapeDtypeStruct((slots, LANES), jnp.float32),) * blocks,
        in_specs=[pl.BlockSpec(memory_space=pltpu.VMEM)] * (1 + len(flat)),
        out_specs=(pl.BlockSpec(memory_space=pltpu.VMEM),) * blocks,
        scratch_shapes=[
            pltpu.VMEM((blocks, query_rows, feature), tiles.dtype),
            pltpu.VMEM((query_rows // LANES, 8 * slots, LANES), jnp.float32),
            pltpu.VMEM((8, LANES), jnp.int32),
            pltpu.SMEM((8, LANES), jnp.int32),
            pltpu.SemaphoreType.DMA,
            pltpu.SemaphoreType.DMA((len(flat),)),
        ],
        compiler_params=pltpu.CompilerParams(vmem_limit_bytes=VMEM_LIMIT),
        cost_estimate=pl.CostEstimate(
            flops=3 * flops,
            bytes_accessed=blocks * (slots * tile_rows + query_rows) * feature * 2,
            transcendentals=0,
        ),
        name="score",
    )(tiles, *flat)


def sort_descending(parts, lanes):
    parts = list(parts)
    many = len(parts)
    number = many * 8
    sub = lax.broadcasted_iota(jnp.int32, (8, lanes), 0)
    size = 2
    while size <= number:
        reach = size // 2
        while reach >= 1:
            if reach < many:
                for v in range(many):
                    if v & reach:
                        continue
                    a, b = parts[v], parts[v | reach]
                    high, low = jnp.maximum(a, b), jnp.minimum(a, b)
                    if size >= number:
                        parts[v], parts[v | reach] = high, low
                    elif size < many:
                        down = (v & size) == 0
                        parts[v], parts[v | reach] = (high, low) if down else (low, high)
                    else:
                        down = (sub & (size // many)) == 0
                        parts[v] = jnp.where(down, high, low)
                        parts[v | reach] = jnp.where(down, low, high)
            else:
                step = reach // many
                is_first = (sub & step) == 0
                if size >= number:
                    keep_high = is_first
                else:
                    keep_high = is_first == ((sub & (size // many)) == 0)
                for v in range(many):
                    x = parts[v]
                    partner = jnp.where(is_first, pltpu.roll(x, 8 - step, 0), pltpu.roll(x, step, 0))
                    parts[v] = jnp.where(keep_high, jnp.maximum(x, partner), jnp.minimum(x, partner))
            reach //= 2
        size *= 2
    return parts


def finish_kernel(arrays, per_device, query_tok, topk, slot_of, *refs):
    returned = refs[:arrays]
    scores, best_scores, spread, ranked, rows, turned = refs[arrays:]
    number = slot_of.shape[0]
    step = returned[0].shape[0]
    for at, ref in enumerate(returned):
        spread[at * step : (at + 1) * step, :] = ref[...]
    total = spread.shape[0]
    lane = lax.broadcasted_iota(jnp.int32, (number, total), 1)
    choose = (slot_of[:, 0:1] == lane).astype(jnp.float32).astype(jnp.bfloat16)
    by_candidate = jnp.zeros((number, LANES), jnp.float32)
    for part in split_exact(spread[...]):
        by_candidate += jnp.dot(choose, part, preferred_element_type=jnp.float32)

    each = LANES // query_tok
    step = lane_step(-(-per_device // each), query_tok)
    many_rows = query_tok // step

    def in_order(x):
        turned[...] = x.T
        for m in range(each):
            rows[pl.ds(m, many_rows, stride=each), :] = turned[
                pl.ds(m * query_tok, many_rows, stride=step), :
            ]
        return rows[...]

    scores[...] = in_order(by_candidate)[:per_device, :]
    many = number // 8
    parts = sort_descending([by_candidate[8 * v : 8 * v + 8, :] for v in range(many)], LANES)
    for v in range(many):
        ranked[pl.ds(v, 8, stride=many), :] = parts[v]
    best_scores[...] = in_order(ranked[...])[:per_device, :topk]


def finish(per_device, query_tok, slot_of, returned):
    number = slot_of.shape[0]
    total = sum(r.shape[0] for r in returned)
    return pl.pallas_call(
        functools.partial(finish_kernel, len(returned), per_device, query_tok, TOPK),
        out_shape=(
            jax.ShapeDtypeStruct((per_device, number), jnp.float32),
            jax.ShapeDtypeStruct((per_device, TOPK), jnp.float32),
        ),
        in_specs=[pl.BlockSpec(memory_space=pltpu.VMEM)] * (1 + len(returned)),
        out_specs=(pl.BlockSpec(memory_space=pltpu.VMEM),) * 2,
        scratch_shapes=[
            pltpu.VMEM((total, LANES), jnp.float32),
            pltpu.VMEM((number, LANES), jnp.float32),
            pltpu.VMEM((LANES, number), jnp.float32),
            pltpu.VMEM((LANES, number), jnp.float32),
        ],
        compiler_params=pltpu.CompilerParams(vmem_limit_bytes=VMEM_LIMIT),
        name="finish",
    )(slot_of, *returned)


def local(queries, passages, lengths, candidates):
    peers = lax.axis_size("corpus")
    chips = peers // CORES
    per_owner, tile_rows, feature = passages.shape
    per_device, query_tok = queries.shape[0], queries.shape[1]
    number = candidates.shape[1]
    capacity = max(2, 3 * number // (2 * peers))
    slots = -(-CORES * capacity // 8) * 8
    order = ring_order(chips)

    def moved(x, distance):
        pairs = [
            (order[i] * CORES + core, order[(i + distance) % chips] * CORES + core)
            for i in range(chips)
            for core in range(CORES)
        ]
        return lax.ppermute(x, "corpus", pairs)

    swap = [(i, i ^ 1) for i in range(peers)]
    other = lax.ppermute(passages, "corpus", swap)
    other_lengths = lax.ppermute(lengths, "corpus", swap)
    slot_of, own = ready(lengths, candidates, passages, chips, slots)
    tiles = join(other_lengths, other, own)

    block = pack(
        queries.reshape(per_device * query_tok, feature), candidates, per_owner, chips, slots
    )
    half = per_device * query_tok // LANES // 2 * LANES
    middle = chips // 2
    arrived = {0: [block]}

    def send_on(step):
        if step < middle:
            arrived[step] = [moved(x, 1) for x in arrived[step - 1]]
            arrived[-step] = [moved(x, -1) for x in arrived[1 - step]]
        else:
            arrived[step] = [
                moved(arrived[step - 1][0][:half], 1), moved(arrived[1 - step][0][half:], -1)
            ]

    send_on(1)
    back = {}
    for step in range(middle + 1):
        if 0 < step < middle:
            send_on(step + 1)
        offsets = (step,) if step in (0, middle) else (step, -step)
        fresh = score([arrived[offset] for offset in offsets], slots, query_tok, chips, tiles)
        for offset, result in zip(offsets, fresh):
            back[offset % chips] = moved(result, -offset) if offset else result
        names = [] if step == middle else [step + 1, -step - 1] if step + 1 < middle else [middle]
        earlier = [1, -1] if step == 1 else [step - 1, 1 - step] if 2 < step < middle else []
        earlier = [offset % chips for offset in earlier]
        held, came, _ = lax.optimization_barrier(
            ([arrived[name] for name in names], [back[j] for j in earlier], fresh)
        )
        arrived.update(zip(names, held))
        back.update(zip(earlier, came))
    return finish(per_device, query_tok, slot_of, [back[j] for j in range(chips)])


def solution(mesh):
    return jax.shard_map(
        local,
        mesh=mesh,
        in_specs=(
            P(("groups", "corpus"), None, None),
            P(("groups", "corpus"), None, None),
            P(("groups", "corpus")),
            P(("groups", "corpus"), None),
        ),
        out_specs=(P(("groups", "corpus"), None), P(("groups", "corpus"), None)),
        check_vma=False,
    )
```

```python
import functools

import jax
import jax.numpy as jnp
from jax import lax
from jax.experimental import pallas as pl
from jax.experimental.pallas import tpu as pltpu
from jax.sharding import PartitionSpec as P

TOPK = 100
CORES = 2
LANES = 128
GROUP = 8
VMEM_LIMIT = 32 * 1024 * 1024
READY_LIMIT = 48 * 1024 * 1024


def ring_order(chips):
    return list(range(0, chips, 2)) + list(range(1, chips, 2))[::-1]


def ring_place(chip, chips):
    return jnp.where(chip % 2 == 0, chip // 2, chips - (chip + 1) // 2)


def split_exact(x):
    high = x.astype(jnp.bfloat16)
    rest = x - high.astype(jnp.float32)
    middle = rest.astype(jnp.bfloat16)
    low = (rest - middle.astype(jnp.float32)).astype(jnp.bfloat16)
    return high, middle, low


def pack_kernel(per_owner, chips, slots, queries_in, candidates_in, out, queries, candidates, block, in_sems, out_sems):
    query_rows = queries.shape[0]
    half = query_rows // LANES // 2 * LANES
    spans = [(0, half), (half, query_rows - half)]
    listed = pltpu.make_async_copy(candidates_in, candidates, in_sems.at[2])
    listed.start()
    loads = [
        pltpu.make_async_copy(
            queries_in.at[pl.ds(at, rows)], queries.at[pl.ds(at, rows)], in_sems.at[i]
        )
        for i, (at, rows) in enumerate(spans)
    ]
    for load in loads:
        load.start()
    listed.wait()
    fact_rows = block.shape[0] - query_rows
    number = candidates.shape[1]
    per_chip = CORES * per_owner
    ids = jnp.broadcast_to(candidates[...], (fact_rows, number))
    row = lax.broadcasted_iota(jnp.int32, ids.shape, 0)
    lane = lax.broadcasted_iota(jnp.int32, ids.shape, 1)
    chosen = ring_place(ids // per_chip, chips) == row
    ones = jnp.where(chosen, 1.0, 0.0)
    before = jnp.where(
        lax.broadcasted_iota(jnp.int32, (number, number), 0)
        < lax.broadcasted_iota(jnp.int32, (number, number), 1), 1.0, 0.0,
    )
    rank = jnp.dot(
        ones.astype(jnp.bfloat16), before.astype(jnp.bfloat16), preferred_element_type=jnp.float32
    )
    rank = jnp.where(chosen, rank, -1.0)
    tile = (ids % per_chip).astype(jnp.float32)
    wanted = jnp.where(lane == slots, jnp.sum(ones, axis=1, keepdims=True), 0.0)
    for s in range(slots):
        found = jnp.sum(jnp.where(rank == float(s), tile, 0.0), axis=1, keepdims=True)
        wanted = jnp.where(lane == s, found, wanted)
    block[query_rows:, :] = wanted.astype(jnp.bfloat16)
    stores = []
    for i, (at, rows) in enumerate(spans):
        loads[i].wait()
        for row_at in range(at, at + rows, LANES):
            block[row_at : row_at + LANES, :] = queries[row_at : row_at + LANES, :].T
        if i:
            rows += fact_rows
        stores.append(
            pltpu.make_async_copy(block.at[pl.ds(at, rows)], out.at[pl.ds(at, rows)], out_sems.at[i])
        )
        stores[-1].start()
    for store in stores:
        store.wait()


def fact_rows_of(chips):
    return -(-chips // 16) * 16


def pack(queries, candidates, per_owner, chips, slots):
    rows, feature = queries.shape
    return pl.pallas_call(
        functools.partial(pack_kernel, per_owner, chips, slots),
        out_shape=jax.ShapeDtypeStruct((rows + fact_rows_of(chips), feature), queries.dtype),
        in_specs=[pl.BlockSpec(memory_space=pl.ANY)] * 2,
        out_specs=pl.BlockSpec(memory_space=pl.ANY),
        scratch_shapes=[
            pltpu.VMEM(queries.shape, queries.dtype),
            pltpu.VMEM(candidates.shape, candidates.dtype),
            pltpu.VMEM((rows + fact_rows_of(chips), feature), queries.dtype),
            pltpu.SemaphoreType.DMA((3,)),
            pltpu.SemaphoreType.DMA((2,)),
        ],
        compiler_params=pltpu.CompilerParams(vmem_limit_bytes=56 * 1024 * 1024),
        name="pack",
    )(queries, candidates)


def fill_tiles(source, lens, filled, filled_at, first, number):
    row = lax.broadcasted_iota(jnp.int32, source.shape[1:], 0)

    def some(i, carry):
        for k in range(4):
            at = first + 4 * i + k
            tile = source[at].astype(jnp.float32)
            tile = jnp.where(row < lens[at], tile, tile[0:1, :])
            filled[filled_at + at] = tile.astype(jnp.bfloat16)
        return carry

    lax.fori_loop(0, number // 4, some, 0)


def ready_kernel(chips, slots, parts, lens, candidates, passages, slot_of, filled, sems):
    per_owner = passages.shape[0]
    size = per_owner // parts
    loads = [
        pltpu.make_async_copy(
            passages.at[pl.ds(i * size, size)], filled.at[pl.ds(i * size, size)], sems.at[i]
        )
        for i in range(parts)
    ]
    for load in loads:
        load.start()
    number = candidates.shape[1]
    my_place = ring_place(lax.axis_index("corpus") // CORES, chips)
    wide = jnp.broadcast_to(candidates[...], (number, number)) // (CORES * per_owner)
    tall = wide.astype(jnp.float32).T.astype(jnp.int32)
    row = lax.broadcasted_iota(jnp.int32, (number, number), 0)
    lane = lax.broadcasted_iota(jnp.int32, (number, number), 1)
    earlier = jnp.where((wide == tall) & (lane < row), 1.0, 0.0)
    rank = jnp.sum(earlier, axis=1, keepdims=True).astype(jnp.int32)
    ahead = ring_place(tall, chips) - my_place
    ahead = jnp.where(ahead < 0, ahead + chips, ahead)
    slot_of[...] = ahead * slots + rank
    for i, load in enumerate(loads):
        load.wait()
        fill_tiles(filled, lens, filled, 0, i * size, size)


def ready(lengths, candidates, passages, chips, slots):
    number = candidates.shape[1]
    per_owner = passages.shape[0]
    parts = 4 if per_owner % 16 == 0 else 1
    return pl.pallas_call(
        functools.partial(ready_kernel, chips, slots, parts),
        out_shape=(
            jax.ShapeDtypeStruct((number, number), jnp.int32),
            jax.ShapeDtypeStruct(passages.shape, passages.dtype),
        ),
        in_specs=[
            pl.BlockSpec(memory_space=pltpu.SMEM),
            pl.BlockSpec(memory_space=pltpu.VMEM),
            pl.BlockSpec(memory_space=pl.ANY),
        ],
        out_specs=(pl.BlockSpec(memory_space=pltpu.VMEM),) * 2,
        scratch_shapes=[pltpu.SemaphoreType.DMA((parts,))],
        compiler_params=pltpu.CompilerParams(vmem_limit_bytes=READY_LIMIT),
        name="ready",
    )(lengths, candidates, passages)


def join_kernel(lens, other, own, filled, sem):
    per_owner = other.shape[0]
    core = lax.axis_index("corpus") % CORES
    keep = pltpu.make_async_copy(own, filled.at[pl.ds(core * per_owner, per_owner)], sem)
    keep.start()
    fill_tiles(other, lens, filled, (1 - core) * per_owner, 0, per_owner)
    keep.wait()


def join(lengths, other, own):
    return pl.pallas_call(
        join_kernel,
        out_shape=jax.ShapeDtypeStruct((CORES * own.shape[0],) + own.shape[1:], own.dtype),
        in_specs=[
            pl.BlockSpec(memory_space=pltpu.SMEM),
            pl.BlockSpec(memory_space=pltpu.VMEM),
            pl.BlockSpec(memory_space=pltpu.VMEM),
        ],
        out_specs=pl.BlockSpec(memory_space=pltpu.VMEM),
        scratch_shapes=[pltpu.SemaphoreType.DMA],
        compiler_params=pltpu.CompilerParams(vmem_limit_bytes=VMEM_LIMIT),
        name="join",
    )(lengths, other, own)


def lane_step(chunks, query_tok):
    return query_tok // pl.next_power_of_2(chunks)


def token_sums(parts, query_tok):
    lane = lax.broadcasted_iota(jnp.int32, parts[0].shape, 1)
    parts = list(parts)
    parts += [None] * (pl.next_power_of_2(len(parts)) - len(parts))
    shift = query_tok // 2
    while shift >= 1:
        low = (lane & shift) == 0
        half = max(1, len(parts) // 2)
        merged = []
        for k in range(half):
            a = parts[k]
            b = parts[k + half] if len(parts) > 1 else None
            if a is None:
                merged.append(None)
                continue
            x = a + pltpu.roll(a, LANES - shift, 1)
            if b is not None:
                x = jnp.where(low, x, b + pltpu.roll(b, shift, 1))
            merged.append(x)
        parts = merged
        shift //= 2
    return parts[0]


def score_kernel(pieces, slots, query_tok, chips, *refs):
    blocks = len(pieces)
    arrays = sum(pieces)
    tiles = refs[0]
    held = refs[1 : 1 + arrays]
    outs = refs[1 + arrays : 1 + arrays + blocks]
    weights, nearest, plan_v, plan, sem, weight_sems = refs[1 + arrays + blocks :]
    tile_rows = tiles.shape[1]
    my_place = ring_place(lax.axis_index("corpus") // CORES, chips)
    fact_rows = fact_rows_of(chips)

    loads = []
    fact_row = lax.broadcasted_iota(jnp.int32, (fact_rows, LANES), 0)
    at = 0
    for b, count in enumerate(pieces):
        row = 0
        for ref in held[at : at + count]:
            rows = min(ref.shape[0], weights.shape[1] - row)
            loads.append(
                pltpu.make_async_copy(
                    ref.at[pl.ds(0, rows)], weights.at[b, pl.ds(row, rows)], weight_sems.at[len(loads)]
                )
            )
            row += rows
        fact = ref[rows : rows + fact_rows, :].astype(jnp.float32)
        fact = jnp.sum(jnp.where(fact_row == my_place, fact, 0.0), axis=0, keepdims=True)
        plan_v[b : b + 1, :] = fact.astype(jnp.int32)
        at += count
    to_scalar = pltpu.make_async_copy(plan_v, plan, sem)
    to_scalar.start()
    for load in loads:
        load.start()
    to_scalar.wait()

    slot_row = lax.broadcasted_iota(jnp.int32, (slots, LANES), 0)

    def score_block(b, carry):
        count = plan[b, slots]
        for k in range(blocks):

            @pl.when(b == k)
            def _(k=k):
                for load in loads[sum(pieces[:k]) : sum(pieces[: k + 1])]:
                    load.wait()

        def score_tiles(first, number):
            left = jnp.concatenate([tiles[plan[b, first + t]] for t in range(number)], axis=0)
            start = pl.multiple_of(first * 8, 8 * number)
            for c in range(0, nearest.shape[0], 2):
                pair = [weights[b, k * LANES : (k + 1) * LANES, :] for k in (c, c + 1)]
                similar = jnp.dot(
                    left, jnp.concatenate(pair, axis=1), preferred_element_type=jnp.float32
                )
                best = jnp.max(similar.reshape(number, tile_rows // 8, 8, 2 * LANES), axis=1)
                best = best.reshape(number * 8, 2 * LANES)
                for k in range(2):
                    nearest[c + k, pl.ds(start, number * 8), :] = best[:, k * LANES : (k + 1) * LANES]

        whole = count // GROUP
        rest = count - whole * GROUP
        small = (rest > 0) & (rest <= GROUP // 2)
        turns = pl.cdiv(count, GROUP) - small.astype(jnp.int32)

        def turn(g, carry):
            score_tiles(pl.multiple_of(g * GROUP, GROUP), GROUP)
            return carry

        lax.fori_loop(0, turns, turn, 0)
        pl.when(small)(lambda: score_tiles(pl.multiple_of(whole * GROUP, GROUP), GROUP // 2))

        parts = []
        for k in range(nearest.shape[0]):
            x = nearest[k, pl.ds(0, slots, stride=8), :]
            for sublane in range(1, 8):
                x = jnp.maximum(x, nearest[k, pl.ds(sublane, slots, stride=8), :])
            parts.append(x)
        total = token_sums(parts, query_tok)
        total = jnp.where(slot_row < count, total / float(query_tok), 0.0)
        for k in range(blocks):

            @pl.when(b == k)
            def _(k=k):
                outs[k][...] = total

        return carry

    lax.fori_loop(0, blocks, score_block, 0)


def score(held, slots, query_tok, chips, tiles):
    pieces = tuple(len(arrays) for arrays in held)
    flat = [x for arrays in held for x in arrays]
    blocks = len(pieces)
    _, tile_rows, feature = tiles.shape
    query_rows = sum(x.shape[0] for x in held[0]) - fact_rows_of(chips)
    flops = 2 * blocks * slots * tile_rows * feature * query_rows
    return pl.pallas_call(
        functools.partial(score_kernel, pieces, slots, query_tok, chips),
        out_shape=(jax.ShapeDtypeStruct((slots, LANES), jnp.float32),) * blocks,
        in_specs=[pl.BlockSpec(memory_space=pltpu.VMEM)] * (1 + len(flat)),
        out_specs=(pl.BlockSpec(memory_space=pltpu.VMEM),) * blocks,
        scratch_shapes=[
            pltpu.VMEM((blocks, query_rows, feature), tiles.dtype),
            pltpu.VMEM((query_rows // LANES, 8 * slots, LANES), jnp.float32),
            pltpu.VMEM((8, LANES), jnp.int32),
            pltpu.SMEM((8, LANES), jnp.int32),
            pltpu.SemaphoreType.DMA,
            pltpu.SemaphoreType.DMA((len(flat),)),
        ],
        compiler_params=pltpu.CompilerParams(vmem_limit_bytes=VMEM_LIMIT),
        cost_estimate=pl.CostEstimate(
            flops=3 * flops,
            bytes_accessed=blocks * (slots * tile_rows + query_rows) * feature * 2,
            transcendentals=0,
        ),
        name="score",
    )(tiles, *flat)


def sort_descending(parts, lanes):
    parts = list(parts)
    many = len(parts)
    number = many * 8
    sub = lax.broadcasted_iota(jnp.int32, (8, lanes), 0)
    size = 2
    while size <= number:
        reach = size // 2
        while reach >= 1:
            if reach < many:
                for v in range(many):
                    if v & reach:
                        continue
                    a, b = parts[v], parts[v | reach]
                    high, low = jnp.maximum(a, b), jnp.minimum(a, b)
                    if size >= number:
                        parts[v], parts[v | reach] = high, low
                    elif size < many:
                        down = (v & size) == 0
                        parts[v], parts[v | reach] = (high, low) if down else (low, high)
                    else:
                        down = (sub & (size // many)) == 0
                        parts[v] = jnp.where(down, high, low)
                        parts[v | reach] = jnp.where(down, low, high)
            else:
                step = reach // many
                is_first = (sub & step) == 0
                if size >= number:
                    keep_high = is_first
                else:
                    keep_high = is_first == ((sub & (size // many)) == 0)
                for v in range(many):
                    x = parts[v]
                    partner = jnp.where(is_first, pltpu.roll(x, 8 - step, 0), pltpu.roll(x, step, 0))
                    parts[v] = jnp.where(keep_high, jnp.maximum(x, partner), jnp.minimum(x, partner))
            reach //= 2
        size *= 2
    return parts


def finish_kernel(arrays, per_device, query_tok, topk, slot_of, *refs):
    returned = refs[:arrays]
    scores, best_scores, spread, ranked, rows, turned = refs[arrays:]
    number = slot_of.shape[0]
    step = returned[0].shape[0]
    for at, ref in enumerate(returned):
        spread[at * step : (at + 1) * step, :] = ref[...]
    total = spread.shape[0]
    lane = lax.broadcasted_iota(jnp.int32, (number, total), 1)
    choose = (slot_of[:, 0:1] == lane).astype(jnp.float32).astype(jnp.bfloat16)
    by_candidate = jnp.zeros((number, LANES), jnp.float32)
    for part in split_exact(spread[...]):
        by_candidate += jnp.dot(choose, part, preferred_element_type=jnp.float32)

    each = LANES // query_tok
    step = lane_step(-(-per_device // each), query_tok)
    many_rows = query_tok // step

    def in_order(x):
        turned[...] = x.T
        for m in range(each):
            rows[pl.ds(m, many_rows, stride=each), :] = turned[
                pl.ds(m * query_tok, many_rows, stride=step), :
            ]
        return rows[...]

    scores[...] = in_order(by_candidate)[:per_device, :]
    many = number // 8
    parts = sort_descending([by_candidate[8 * v : 8 * v + 8, :] for v in range(many)], LANES)
    for v in range(many):
        ranked[pl.ds(v, 8, stride=many), :] = parts[v]
    best_scores[...] = in_order(ranked[...])[:per_device, :topk]


def finish(per_device, query_tok, slot_of, returned):
    number = slot_of.shape[0]
    total = sum(r.shape[0] for r in returned)
    return pl.pallas_call(
        functools.partial(finish_kernel, len(returned), per_device, query_tok, TOPK),
        out_shape=(
            jax.ShapeDtypeStruct((per_device, number), jnp.float32),
            jax.ShapeDtypeStruct((per_device, TOPK), jnp.float32),
        ),
        in_specs=[pl.BlockSpec(memory_space=pltpu.VMEM)] * (1 + len(returned)),
        out_specs=(pl.BlockSpec(memory_space=pltpu.VMEM),) * 2,
        scratch_shapes=[
            pltpu.VMEM((total, LANES), jnp.float32),
            pltpu.VMEM((number, LANES), jnp.float32),
            pltpu.VMEM((LANES, number), jnp.float32),
            pltpu.VMEM((LANES, number), jnp.float32),
        ],
        compiler_params=pltpu.CompilerParams(vmem_limit_bytes=VMEM_LIMIT),
        name="finish",
    )(slot_of, *returned)


def local(queries, passages, lengths, candidates):
    peers = lax.axis_size("corpus")
    chips = peers // CORES
    per_owner, tile_rows, feature = passages.shape
    per_device, query_tok = queries.shape[0], queries.shape[1]
    number = candidates.shape[1]
    capacity = max(2, 3 * number // (2 * peers))
    slots = -(-CORES * capacity // 8) * 8
    order = ring_order(chips)

    def moved(x, distance):
        pairs = [
            (order[i] * CORES + core, order[(i + distance) % chips] * CORES + core)
            for i in range(chips)
            for core in range(CORES)
        ]
        return lax.ppermute(x, "corpus", pairs)

    swap = [(i, i ^ 1) for i in range(peers)]
    other = lax.ppermute(passages, "corpus", swap)
    other_lengths = lax.ppermute(lengths, "corpus", swap)
    slot_of, own = ready(lengths, candidates, passages, chips, slots)
    tiles = join(other_lengths, other, own)

    block = pack(
        queries.reshape(per_device * query_tok, feature), candidates, per_owner, chips, slots
    )
    half = per_device * query_tok // LANES // 2 * LANES
    middle = chips // 2
    arrived = {0: [block]}

    def send_on(step):
        if step < middle:
            arrived[step] = [moved(x, 1) for x in arrived[step - 1]]
            arrived[-step] = [moved(x, -1) for x in arrived[1 - step]]
        else:
            arrived[step] = [
                moved(arrived[step - 1][0][:half], 1), moved(arrived[1 - step][0][half:], -1)
            ]

    send_on(1)
    scored, back = {}, {}

    def send_back(offsets):
        return {offset % chips: moved(scored[offset], -offset) for offset in offsets}

    for step in range(middle + 1):
        if 0 < step < middle:
            send_on(step + 1)
        offsets = (step,) if step in (0, middle) else (step, -step)
        fresh = score([arrived[offset] for offset in offsets], slots, query_tok, chips, tiles)
        scored.update(zip(offsets, fresh))
        names = [] if step == middle else [step + 1, -step - 1] if step + 1 < middle else [middle]
        sent = send_back(offsets) if 0 < step < middle - 1 else {}
        held, scored, sent = lax.optimization_barrier(
            ([arrived[name] for name in names], scored, sent)
        )
        back.update(sent)
        arrived.update(zip(names, held))
    back.update(send_back([offset for offset in scored if abs(offset) >= middle - 1]))
    back[0] = scored[0]
    return finish(per_device, query_tok, slot_of, [back[j] for j in range(chips)])


def solution(mesh):
    return jax.shard_map(
        local,
        mesh=mesh,
        in_specs=(
            P(("groups", "corpus"), None, None),
            P(("groups", "corpus"), None, None),
            P(("groups", "corpus")),
            P(("groups", "corpus"), None),
        ),
        out_specs=(P(("groups", "corpus"), None), P(("groups", "corpus"), None)),
        check_vma=False,
    )
```
